32 devices in a mesh: dp: 8 (over z, y), tensor: 4 (over x, core).
Axes of the slice: x: 2, y: 2, z: 4, core: 2. Of those that a mesh axis runs over, the one named last changes fastest.
Arguments:
- layer_input: bfloat16 [16384, 2048], P(('dp', 'tensor')), may hold values from -6 to 6
- seq_lens: int32 [8, 4], P('dp'), may hold values from 1 to 2045, as said below
- ln_gain: float32 [2048], replicated, may hold values from 0.5 to 1.5
- ln_bias: float32 [2048], replicated, may hold values from -1.25 to 1.25
- w_qkv: bfloat16 [2048, 3, 2048], P('dp', None, 'tensor'), may hold values from -0.125 to 0.125
- b_qkv: float32 [3, 2048], P(None, 'tensor'), may hold values from -3 to 3
- w_dense: bfloat16 [2048, 2048], P('tensor', 'dp'), may hold values from -0.375 to 0.375
- b_dense: float32 [2048], replicated, may hold values from -1.75 to 1.75
- w_fc1: bfloat16 [2048, 8192], P('dp', 'tensor'), may hold values from -0.125 to 0.125
- b_fc1: float32 [8192], P('tensor'), may hold values from -3 to 3
- w_fc2: bfloat16 [8192, 2048], P('tensor', 'dp'), may hold values from -0.0625 to 0.0625
- b_fc2: float32 [2048], replicated, may hold values from -1.75 to 1.75
- cotangent: bfloat16 [16384, 2048], P(('dp', 'tensor')), may hold values from -6 to 6
Outputs:
- layer_output: bfloat16 [16384, 2048], P(('dp', 'tensor'))
- grad_x: float32 [16384, 2048], P(('dp', 'tensor'))
- grad_ln_gain: float32 [2048], replicated
- grad_ln_bias: float32 [2048], replicated
- grad_w_qkv: float32 [2048, 3, 2048], P('dp', None, 'tensor')
- grad_b_qkv: float32 [3, 2048], P(None, 'tensor')
- grad_w_dense: float32 [2048, 2048], P('tensor', 'dp')
- grad_b_dense: float32 [2048], replicated
- grad_w_fc1: float32 [2048, 8192], P('dp', 'tensor')
- grad_b_fc1: float32 [8192], P('tensor')
- grad_w_fc2: float32 [8192, 2048], P('tensor', 'dp')
- grad_b_fc2: float32 [2048], replicated
The draws below stay inside these ranges and needn't reach their ends.
Inputs may be any that keep to these rules, and one draw needn't show every extreme that they name: `seq_lens`: in each group, one sequence, which one drawn from the seed, starts within the first 512 rows and ends within the last 512 rows of the group; the lengths of a group sum to at most 2048, leaving fewer than 129 padding rows. The first group has no padding and all its sequences but the long one have length 1.
All inputs are finite; a program needn't handle non-finite values.
Results may differ from the reference program's by a relative error of at most 0.01.
Values may be sent and summed in bfloat16 or wider, within the bound.
A program may use at most 256 MiB of HBM per device.

```python
import math
import jax
import jax.numpy as jnp
from jax import lax

D = 2048
HEADS = 32
FF = 8192
HEAD = 64
ROT = 32
SEQS = 4
TOK_DEV = 512
TOK_GRP = 2048
TOKENS = 16384
N_DP = 8


def draw_seq_lens(key, part):
    key = jax.random.fold_in(key, 11)
    key_short, key_pad, key_pick = jax.random.split(key, 3)
    short_most = max(1, TOK_DEV // (2 * SEQS))
    short = jax.random.randint(key_short, (N_DP, SEQS), 1, short_most + 1)
    padding = jax.random.randint(key_pad, (N_DP, 1), 0, max(1, TOK_DEV // 4))
    pick = jax.random.randint(key_pick, (N_DP, 1), 0, SEQS)
    slot = lax.broadcasted_iota(jnp.int32, (N_DP, SEQS), 1)
    group_id = lax.broadcasted_iota(jnp.int32, (N_DP, SEQS), 0)
    short = jnp.where(group_id == 0, 1, short)
    padding = jnp.where(group_id[:, :1] == 0, 0, padding)
    chosen = slot == pick
    others = jnp.sum(jnp.where(chosen, 0, short), axis=1, keepdims=True)
    longest = TOK_GRP - padding - others
    return jnp.where(chosen, longest, short).astype(jnp.int32)


def levels(rng, extent, shards, low, largest):
    loudness, own = 1.0, jax.random.fold_in(rng, 6)
    for axis_at, shards_of in shards:
        heights = jnp.exp(jax.random.uniform(jax.random.fold_in(own, axis_at), (shards_of,), jnp.float32, low / len(shards), largest / len(shards)))
        loudness = loudness * jnp.repeat(heights, extent[axis_at] // shards_of).reshape([-1 if axis == axis_at else 1 for axis in range(len(extent))])
    return loudness


def noise(stream_key, extent, deviation, most, cuts=(), held_as=jnp.bfloat16):
    factor_of = levels(stream_key, extent, cuts, -0.22, 0.18) if cuts else 1.0
    values = jax.random.normal(stream_key, extent, jnp.float32) * deviation * factor_of
    return jnp.minimum(jnp.maximum(values, -most), most).astype(held_as)


def setup_inputs(seed: int = 0) -> dict:
    arg_keys = jax.random.split(jax.random.key(seed), 14)
    layer_input = noise(arg_keys[0], (TOKENS, D), 1.0, 6.0, ((0, 32),))
    seq_lens = draw_seq_lens(jax.random.fold_in(arg_keys[13], 71), 0)
    ln_gain = jnp.clip(1.0 + 0.1 * jax.random.normal(arg_keys[2], (D,), jnp.float32), 0.5, 1.5)
    ln_bias = noise(arg_keys[3], (D,), 0.2, 1.25, (), jnp.float32)
    w_qkv = noise(arg_keys[4], (D, 3, D), D ** -0.5, 0.125, ((0, 8), (2, 4)))
    b_qkv = noise(arg_keys[5], (3, D), 0.5, 3.0, ((1, 4),), jnp.float32)
    w_dense = noise(arg_keys[6], (D, D), (D // 8) ** -0.5, 0.375, ((0, 4), (1, 8)))
    b_dense = noise(arg_keys[7], (D,), 0.3, 1.75, (), jnp.float32)
    w_fc1 = noise(arg_keys[8], (D, FF), D ** -0.5, 0.125, ((0, 8), (1, 4)))
    b_fc1 = noise(arg_keys[9], (FF,), 0.5, 3.0, ((0, 4),), jnp.float32)
    w_fc2 = noise(arg_keys[10], (FF, D), FF ** -0.5, 0.0625, ((0, 4), (1, 8)))
    b_fc2 = noise(arg_keys[11], (D,), 0.3, 1.75, (), jnp.float32)
    cotangent = noise(arg_keys[12], (TOKENS, D), 1.0, 6.0, ((0, 32),))
    return dict(layer_input=layer_input, seq_lens=seq_lens, ln_gain=ln_gain, ln_bias=ln_bias, w_qkv=w_qkv, b_qkv=b_qkv, w_dense=w_dense, b_dense=b_dense, w_fc1=w_fc1, b_fc1=b_fc1, w_fc2=w_fc2, b_fc2=b_fc2, cotangent=cotangent)


@jax.custom_vjp
def low(v):
    return lax.optimization_barrier(v.astype(jnp.bfloat16)).astype(jnp.float32)

@jax.custom_vjp
def low_back(v):
    return v

def low_keep(v):
    return (low(v), None)

def low_pass(kept, grad):
    return (grad,)

def back_keep(v):
    return (v, None)

def back_low(kept, grad):
    return (low(grad),)
low.defvjp(low_keep, low_pass)
low_back.defvjp(back_keep, back_low)
EPS = 1e-05
HIGH = lax.Precision.HIGHEST

def layout(seq_row):
    ends = jnp.cumsum(seq_row).astype(jnp.int32)
    starts = (ends - seq_row).astype(jnp.int32)
    rows = jnp.arange(TOK_GRP, dtype=jnp.int32)
    segment = lax.optimization_barrier(jnp.sum((rows[:, None] >= ends[None, :]).astype(jnp.int32), axis=1))
    start_all = jnp.concatenate([starts, ends[-1:]]).astype(jnp.int32)
    labels = jnp.arange(SEQS + 1, dtype=jnp.int32)
    first = lax.optimization_barrier(jnp.sum(jnp.where(segment[:, None] == labels[None, :], start_all[None, :], 0), axis=1))
    return (segment, (rows - first).astype(jnp.int32))

def rotary_tables(position):
    steps = jnp.arange(ROT // 2, dtype=jnp.float32)
    inverse = jnp.exp(-math.log(10000.0) * 2.0 * steps / ROT)
    angle = position.astype(jnp.float32)[:, None] * inverse[None, :]
    return (jnp.cos(angle)[:, None, :], jnp.sin(angle)[:, None, :])

def apply_rotary(heads, cosine, sine):
    half = ROT // 2
    first = heads[..., :half]
    second = heads[..., half:ROT]
    turned = jnp.concatenate([first * cosine - second * sine, second * cosine + first * sine], axis=-1)
    return jnp.concatenate([turned, heads[..., ROT:]], axis=-1)

def attend_block(start, query, key, value, segment):
    block = min(512, TOK_GRP)
    q_blk = lax.dynamic_slice_in_dim(query, start, block, 0)
    seg_blk = lax.dynamic_slice_in_dim(segment, start, block, 0)
    raw = jnp.einsum('qhd,khd->hqk', q_blk, key, precision=HIGH) * (1.0 / math.sqrt(HEAD))
    raw = low_back(raw)
    rows = start + jnp.arange(block, dtype=jnp.int32)
    cols = jnp.arange(TOK_GRP, dtype=jnp.int32)
    allowed = (seg_blk[:, None] == segment[None, :]) & (cols[None, :] <= rows[:, None])
    masked = jnp.where(allowed[None], raw, -1e+30)
    top = lax.optimization_barrier(jnp.max(masked, axis=2, keepdims=True))
    weights = jnp.exp(masked - top)
    prob = low(weights / lax.optimization_barrier(jnp.sum(weights, axis=2, keepdims=True)))
    return jnp.einsum('hqk,khd->qhd', prob, value, precision=HIGH)

def group_forward(x_rows, seq_row, params):
    ln_gain, ln_bias, w_qkv, b_qkv, w_dense, b_dense, w_fc1, b_fc1, w_fc2, b_fc2 = params
    mean = lax.optimization_barrier(jnp.mean(x_rows, axis=1, keepdims=True))
    centred = x_rows - mean
    var = lax.optimization_barrier(jnp.mean(centred * centred, axis=1, keepdims=True))
    normed = low(centred * lax.rsqrt(var + EPS) * ln_gain + ln_bias)
    mixed = jnp.einsum('rd,dce->rce', normed, w_qkv, precision=HIGH) + b_qkv[None]
    mixed = low_back(mixed)
    segment, position = layout(seq_row)
    cosine, sine = rotary_tables(position)
    query = low(apply_rotary(mixed[:, 0].reshape(TOK_GRP, HEADS, HEAD), cosine, sine))
    key = low(apply_rotary(mixed[:, 1].reshape(TOK_GRP, HEADS, HEAD), cosine, sine))
    value = low(mixed[:, 2].reshape(TOK_GRP, HEADS, HEAD))
    block = min(512, TOK_GRP)
    starts = jnp.arange(TOK_GRP // block, dtype=jnp.int32) * block
    pieces = lax.map(jax.checkpoint(lambda s: attend_block(s, query, key, value, segment)), starts)
    attended = low(low_back(pieces.reshape(TOK_GRP, D)))
    pre = low_back(jnp.dot(normed, w_fc1, precision=HIGH) + b_fc1)
    act = low(jax.nn.gelu(pre, approximate=True))
    branch = low_back(jnp.dot(attended, w_dense, precision=HIGH) + jnp.dot(act, w_fc2, precision=HIGH))
    return x_rows + branch + b_dense + b_fc2

def reference(layer_input, seq_lens, ln_gain, ln_bias, w_qkv, b_qkv, w_dense, b_dense, w_fc1, b_fc1, w_fc2, b_fc2, cotangent):
    x_float = layer_input.astype(jnp.float32)
    params = (ln_gain.astype(jnp.float32), ln_bias.astype(jnp.float32), w_qkv.astype(jnp.float32), b_qkv.astype(jnp.float32), w_dense.astype(jnp.float32), b_dense.astype(jnp.float32), w_fc1.astype(jnp.float32), b_fc1.astype(jnp.float32), w_fc2.astype(jnp.float32), b_fc2.astype(jnp.float32))

    def forward(x_all, weights):
        groups = x_all.reshape(N_DP, TOK_GRP, D)
        result = lax.map(jax.checkpoint(lambda item: group_forward(item[0], item[1], weights)), (groups, seq_lens))
        return result.reshape(TOKENS, D)
    output, pull = jax.vjp(forward, x_float, params)
    used = lax.optimization_barrier(jnp.sum(seq_lens, axis=1))
    rows = jnp.arange(TOK_GRP, dtype=jnp.int32)
    valid = (rows[None, :] < used[:, None]).astype(jnp.float32).reshape(TOKENS, 1)
    grad_x, grads = pull(cotangent.astype(jnp.float32) * valid)
    g_gain, g_shift, g_qkv, g_bqkv, g_dense, g_bdense, g_fc1, g_bfc1, g_fc2, g_bfc2 = grads
    return (output.astype(jnp.bfloat16), grad_x, g_gain, g_shift, g_qkv, g_bqkv, g_dense, g_bdense, g_fc1, g_bfc1, g_fc2, g_bfc2)
```

```python
import functools
import math

import jax
import jax.numpy as jnp
from jax import lax
from jax.experimental import pallas as pl
from jax.experimental.pallas import tpu as pltpu
from jax.sharding import PartitionSpec as P

HEAD = 64
ROT = 32
EPS = 1e-05
NEG = -1e30
LANES = 128
BF = jnp.bfloat16
F32 = jnp.float32
NT = (((1,), (1,)), ((), ()))
TN = (((0,), (0,)), ((), ()))
VMEM = 56 * 2**20


def swap(x, axis, bit):
    size = lax.axis_size(axis)
    return lax.ppermute(x, axis, [(i, i ^ bit) for i in range(size)])


def up(x, step):
    size = lax.axis_size("dp")
    return lax.ppermute(x, "dp", [(i, i + 2) for i in range(2 * (step - 1), size - 2)])


def down(x, step):
    size = lax.axis_size("dp")
    return lax.ppermute(x, "dp", [(i, i - 2) for i in range(2, size - 2 * (step - 1))])


def pick(x, index):
    return lax.dynamic_index_in_dim(x, index, 0, keepdims=False)


def place(buffer, block, *index):
    return lax.dynamic_update_slice(
        buffer, block.reshape((1,) * len(index) + block.shape), tuple(index) + (0,) * block.ndim
    )


def gather_line(pair, at, places):
    ups, downs = [pair], [pair]
    for step in range(1, places):
        ups.append(up(ups[-1], step))
        downs.append(down(downs[-1], step))
    out = jnp.zeros((places,) + pair.shape, pair.dtype)
    out = place(out, pair, at)
    for j in range(1, places):
        block = jnp.where(at + j < places, downs[j], ups[places - j])
        out = place(out, block, lax.rem(at + j, places))
    return out


def reduce_line(parts, places):
    add = lambda a, b: (a.astype(F32) + b.astype(F32)).astype(BF)
    going_up, going_down = parts[places - 1], parts[1]
    for distance in range(places - 1, 0, -1):
        size = lax.axis_size("dp")
        got_up = lax.ppermute(
            going_up, "dp", [(i, i + 2) for i in range(0, size - 2 * distance)]
        )
        got_down = lax.ppermute(
            going_down, "dp", [(i, i - 2) for i in range(2 * distance, size)]
        )
        if distance > 1:
            going_up = add(parts[distance - 1], got_up)
            going_down = add(parts[places - distance + 1], got_down)
    return parts[0].astype(F32) + got_up.astype(F32) + got_down.astype(F32)


def lanes_of(shape):
    return lax.broadcasted_iota(jnp.int32, shape, 1)


def turn(x, cosine, sine):
    lane = lanes_of(x.shape) % HEAD
    other = jnp.where(lane < ROT // 2, pltpu.roll(x, LANES - ROT // 2, 1), pltpu.roll(x, ROT // 2, 1))
    return x * cosine + other * sine


def qkv_kernel(pairs, h_ref, w_ref, b_ref, cos_ref, sin_ref, out_ref):
    acc = jnp.dot(h_ref[...], w_ref[...], preferred_element_type=F32) + b_ref[...]
    cosine, sine = cos_ref[...], sin_ref[...]
    for j in range(pairs):
        at = 3 * LANES * j
        q = turn(acc[:, at : at + LANES], cosine, sine).astype(BF)
        out_ref[:, at : at + LANES] = (q.astype(F32) * HEAD**-0.5).astype(BF)
        out_ref[:, at + LANES : at + 2 * LANES] = turn(
            acc[:, at + LANES : at + 2 * LANES], cosine, sine
        ).astype(BF)
        out_ref[:, at + 2 * LANES : at + 3 * LANES] = acc[:, at + 2 * LANES : at + 3 * LANES].astype(BF)


def qkv_call(h, w, bias, cosine, sine, block=512):
    rows, depth = h.shape
    columns = w.shape[1]
    return pl.pallas_call(
        functools.partial(qkv_kernel, columns // (3 * LANES)),
        grid=(rows // block,),
        in_specs=[
            pl.BlockSpec((block, depth), lambda i: (i, 0)),
            pl.BlockSpec((depth, columns), lambda i: (0, 0)),
            pl.BlockSpec((1, columns), lambda i: (0, 0)),
            pl.BlockSpec((block, LANES), lambda i: (i, 0)),
            pl.BlockSpec((block, LANES), lambda i: (i, 0)),
        ],
        out_specs=pl.BlockSpec((block, columns), lambda i: (i, 0)),
        out_shape=jax.ShapeDtypeStruct((rows, columns), BF),
        compiler_params=pltpu.CompilerParams(vmem_limit_bytes=VMEM),
        cost_estimate=pl.CostEstimate(
            flops=2 * rows * depth * columns, bytes_accessed=2 * rows * depth, transcendentals=0
        ),
    )(h, w, bias, cosine, sine)


def attend_kernel(rows, block, qkv_ref, aq_ref, ak_ref, o_ref, lse_ref):
    lane = lanes_of((rows, LANES))
    lane_q = lanes_of((block, LANES))
    one = jnp.where(lane % HEAD < 3, 1.0, 0.0).astype(BF)
    first = lane < HEAD
    keys = [jnp.where(half, qkv_ref[:, LANES : 2 * LANES], ak_ref[...]) for half in (first, ~first)]
    values = [jnp.where(half, qkv_ref[:, 2 * LANES :], one) for half in (first, ~first)]
    causal = lanes_of((block, block)) <= lax.broadcasted_iota(jnp.int32, (block, block), 0)
    for b in range(rows // block):
        here = pl.ds(b * block, block)
        lo, hi = b * block, (b + 1) * block
        outs, sums = [], []
        for side in (0, 1):
            half = (lane_q < HEAD) if side == 0 else (lane_q >= HEAD)
            q = jnp.where(half, qkv_ref[here, :LANES], aq_ref[here])
            s_near = lax.dot_general(q, keys[side][lo:hi], NT, preferred_element_type=F32)
            s_near = jnp.where(causal, s_near, NEG)
            top = jnp.max(s_near, axis=1, keepdims=True)
            if b:
                s_far = lax.dot_general(q, keys[side][:lo], NT, preferred_element_type=F32)
                top = jnp.maximum(top, jnp.max(s_far, axis=1, keepdims=True))
            o = jnp.dot(jnp.exp(s_near - top).astype(BF), values[side][lo:hi], preferred_element_type=F32)
            if b:
                o = o + jnp.dot(
                    jnp.exp(s_far - top).astype(BF), values[side][:lo], preferred_element_type=F32
                )
            at = HEAD if side == 0 else 0
            total = o[:, at : at + 1]
            outs.append(o / total)
            sums.append(top + jnp.log(total))
        o_ref[here] = jnp.where(lane_q < HEAD, outs[0], outs[1])
        lse_ref[here] = jnp.where(lane_q < HEAD, sums[0], sums[1])


def attend_cost(groups, pairs, rows, products):
    pairs_of = groups * pairs * 2 * rows * rows
    return pl.CostEstimate(
        flops=products * pairs_of * 256, bytes_accessed=groups * pairs * rows * 4096, transcendentals=pairs_of // 2
    )


def attend_call(qkv, aq, ak, rows, block=512):
    groups, pairs = qkv.shape[0] // rows, qkv.shape[1] // (3 * LANES)
    wide = pl.BlockSpec((rows, 3 * LANES), lambda g, j: (g, j))
    one = pl.BlockSpec((rows, LANES), lambda g, j: (g, j))
    aug = pl.BlockSpec((rows, LANES), lambda g, j: (g, 0))
    shape = jax.ShapeDtypeStruct((groups * rows, pairs * LANES), F32)
    return pl.pallas_call(
        functools.partial(attend_kernel, rows, block),
        grid=(groups, pairs),
        in_specs=[wide, aug, aug],
        out_specs=[one, one],
        out_shape=[shape, shape],
        compiler_params=pltpu.CompilerParams(vmem_limit_bytes=VMEM),
        cost_estimate=attend_cost(groups, pairs, rows, 2),
    )(qkv, aq, ak)


def split3(x):
    a = x.astype(BF).astype(F32)
    b = (x - a).astype(BF).astype(F32)
    return a, b, x - a - b


def attend_back_kernel(
    rows, block, qkv_ref, aq_ref, ak_ref, o_ref, lse_ref, go_ref, cos_ref, sin_ref, out_ref, dk_s, dv_s, dqt_s
):
    lane = lanes_of((rows, LANES))
    lane_k = lanes_of((block, LANES))
    one = jnp.where(lane % HEAD < 3, 1.0, 0.0).astype(BF)
    causal = lax.broadcasted_iota(jnp.int32, (block, block), 0) <= lanes_of((block, block))
    prod = o_ref[...] * go_ref[...].astype(F32)
    dq_first = None
    for side in (0, 1):
        half = (lane < HEAD) if side == 0 else (lane >= HEAD)
        delta = -jnp.sum(jnp.where(half, prod, 0.0), axis=1, keepdims=True)
        at = 0 if side == 0 else HEAD
        lse = -lse_ref[:, at : at + 1]
        q = jnp.where(half, qkv_ref[:, :LANES], aq_ref[...]).astype(F32)
        g = jnp.where(half, go_ref[...].astype(F32), 0.0)
        base = HEAD - at
        for i, (a, d) in enumerate(zip(split3(lse), split3(delta))):
            q = jnp.where(lane == base + 8 + i, a, q)
            g = jnp.where(lane == base + i, d, g)
        q, g = q.astype(BF), g.astype(BF)
        k = jnp.where(half, qkv_ref[:, LANES : 2 * LANES], ak_ref[...])
        v = jnp.where(half, qkv_ref[:, 2 * LANES :], one)
        kt = k.T
        for b in range(rows // block):
            lo, hi = b * block, (b + 1) * block
            here = pl.ds(lo, block)
            st = lax.dot_general(k[lo:hi], q[lo:], NT, preferred_element_type=F32)
            dpt = lax.dot_general(v[lo:hi], g[lo:], NT, preferred_element_type=F32)
            p = jnp.exp(st)
            near = jnp.where(causal, p[:, :block], 0.0)
            p = jnp.concatenate([near, p[:, block:]], axis=1) if hi < rows else near
            ds = (p * dpt).astype(BF)
            dv = jnp.dot(p.astype(BF), g[lo:], preferred_element_type=F32)
            dk = jnp.dot(ds, q[lo:], preferred_element_type=F32)
            dq = jnp.dot(kt[:, lo:hi], ds, preferred_element_type=F32)
            if side == 0:
                dk_s[here] = dk
                dv_s[here] = dv
            else:
                dk = jnp.where(lane_k < HEAD, dk_s[here], dk)
                dv = jnp.where(lane_k < HEAD, dv_s[here], dv)
                out_ref[here, LANES : 2 * LANES] = turn(dk, cos_ref[here], -sin_ref[here]).astype(BF)
                out_ref[here, 2 * LANES :] = dv.astype(BF)
            if b == 0:
                dqt_s[...] = dq
            else:
                dqt_s[:, lo:] += dq
        d = dqt_s[...].T * HEAD**-0.5
        if side == 0:
            dq_first = d
        else:
            d = jnp.where(lane < HEAD, dq_first, d)
            out_ref[:, :LANES] = turn(d, cos_ref[...], -sin_ref[...]).astype(BF)


def attend_back_call(qkv, aq, ak, o, lse, go, cosine, sine, rows, block=256):
    groups, pairs = qkv.shape[0] // rows, qkv.shape[1] // (3 * LANES)
    wide = pl.BlockSpec((rows, 3 * LANES), lambda g, j: (g, j))
    one = pl.BlockSpec((rows, LANES), lambda g, j: (g, j))
    aug = pl.BlockSpec((rows, LANES), lambda g, j: (g, 0))
    return pl.pallas_call(
        functools.partial(attend_back_kernel, rows, block),
        grid=(groups, pairs),
        in_specs=[wide, aug, aug, one, one, one, aug, aug],
        out_specs=wide,
        out_shape=jax.ShapeDtypeStruct(qkv.shape, BF),
        scratch_shapes=[
            pltpu.VMEM((rows, LANES), F32),
            pltpu.VMEM((rows, LANES), F32),
            pltpu.VMEM((LANES, rows), F32),
        ],
        compiler_params=pltpu.CompilerParams(vmem_limit_bytes=VMEM),
        cost_estimate=attend_cost(groups, pairs, rows, 5),
    )(qkv, aq, ak, o, lse, go, cosine, sine)


def rows_kernel(terms, added, dtype, index_ref, *refs):
    ins, out_ref = refs[:-1], refs[-1]
    acc = lax.dot_general(ins[0][...], ins[1][...], NT, preferred_element_type=F32)
    for i in range(1, terms):
        acc = acc + lax.dot_general(ins[2 * i][...], ins[2 * i + 1][...], NT, preferred_element_type=F32)
    for i in range(added):
        acc = acc + ins[2 * terms + i][...].astype(F32)
    out_ref[...] = acc.astype(dtype)


def rows_call(index, count, factors, part, parts, added, block, dtype):
    columns = factors[0][1].shape[0] // parts
    in_specs, args = [], []
    flops = 0
    for a, b in factors:
        depth = a.shape[1]
        in_specs.append(pl.BlockSpec((block, depth), lambda i, index: (index[i], 0)))
        in_specs.append(pl.BlockSpec((columns, depth), lambda i, index: (part, 0)))
        args += [a, b]
        flops += 2 * count * block * columns * depth
    for a in added:
        in_specs.append(pl.BlockSpec((block, columns), lambda i, index: (i, 0)))
        args.append(a)
    return pl.pallas_call(
        functools.partial(rows_kernel, len(factors), len(added), dtype),
        grid_spec=pltpu.PrefetchScalarGridSpec(
            num_scalar_prefetch=1,
            grid=(count,),
            in_specs=in_specs,
            out_specs=pl.BlockSpec((block, columns), lambda i, index: (i, 0)),
        ),
        out_shape=jax.ShapeDtypeStruct((count * block, columns), dtype),
        compiler_params=pltpu.CompilerParams(vmem_limit_bytes=VMEM),
        cost_estimate=pl.CostEstimate(flops=flops, bytes_accessed=4 * count * block * columns, transcendentals=0),
    )(index, *args)


def gelu_slope(z):
    c = math.sqrt(2.0 / math.pi)
    t = jnp.tanh(c * (z + 0.044715 * z * z * z))
    return 0.5 * (1.0 + t) + 0.5 * z * (1.0 - t * t) * c * (1.0 + 3.0 * 0.044715 * z * z)


def local(
    layer_input,
    seq_lens,
    ln_gain,
    ln_bias,
    w_qkv,
    b_qkv,
    w_dense,
    b_dense,
    w_fc1,
    b_fc1,
    w_fc2,
    b_fc2,
    cotangent,
):
    own, width = layer_input.shape
    ndp, nt = lax.axis_size("dp"), lax.axis_size("tensor")
    dp, t = lax.axis_index("dp"), lax.axis_index("tensor")
    half, at, places = dp % 2, dp // 2, ndp // 2
    chip, core = t // 2, t % 2
    group = own * nt
    shard = w_qkv.shape[0]
    q_width = w_qkv.shape[2] // 2
    f_width = w_fc1.shape[1] // 2
    pairs = q_width // LANES
    other = 1 - half

    wq = w_qkv.reshape(shard, 3, 2, pairs, LANES).transpose(2, 0, 3, 1, 4).reshape(2, shard, 3 * q_width)
    wd = w_dense.T.reshape(shard, 2, q_width).transpose(1, 0, 2)
    w1 = w_fc1.reshape(shard, 2, f_width).transpose(1, 0, 2)
    w2 = w_fc2.T.reshape(shard, 2, f_width).transpose(1, 0, 2)

    def gather_weight(w):
        theirs = swap(pick(w, other), "dp", 1)
        pair = jnp.zeros((2, shard, w.shape[2]), BF)
        pair = place(place(pair, pick(w, half), half), theirs, other)
        full = gather_line(pair.reshape(2 * shard, w.shape[2]), at, places)
        return full.reshape(width, w.shape[2])

    def gather_rows(a):
        mid = own // 2
        a_x = swap(a, "tensor", 2)
        a_y = swap(a, "dp", 1)
        a_c = swap(a, "tensor", 1)
        a_yx = jnp.concatenate([swap(a_x[:mid], "dp", 1), swap(a_y[mid:], "tensor", 2)], axis=0)
        out = jnp.zeros((2, nt, own, width), a.dtype)
        for block, g, x in ((a, half, chip), (a_x, half, 1 - chip), (a_y, other, chip), (a_yx, other, 1 - chip)):
            out = place(out, block, g, 2 * x + core)
            out = place(out, a_c if block is a else swap(block, "tensor", 1), g, 2 * x + 1 - core)
        return out.reshape(2 * group, width)

    xf = layer_input.astype(F32)
    mean = jnp.mean(xf, axis=1, keepdims=True)
    centred = xf - mean
    rstd = lax.rsqrt(jnp.mean(centred * centred, axis=1, keepdims=True) + EPS)
    x_hat = centred * rstd
    h_own = (x_hat * ln_gain + ln_bias).astype(BF)
    used = jnp.sum(seq_lens[0])
    valid = (t * own + jnp.arange(own, dtype=jnp.int32) < used).astype(F32)[:, None]
    gy = cotangent.astype(F32) * valid
    gb_own = gy.astype(BF)

    wq_all = gather_weight(wq)
    h = gather_rows(h_own)
    wd_all = gather_weight(wd)
    gb = gather_rows(gb_own)
    w1_all = gather_weight(w1)
    w2_all = gather_weight(w2)

    lens = jnp.zeros((2, seq_lens.shape[1]), jnp.int32)
    lens = place(place(lens, seq_lens[0], half), swap(seq_lens, "dp", 1)[0], other)
    ends = jnp.cumsum(lens, axis=1)
    rows = jnp.arange(group, dtype=jnp.int32)
    segment = jnp.sum((rows[None, :, None] >= ends[:, None, :]).astype(jnp.int32), axis=2)
    begins = jnp.concatenate([ends - lens, ends[:, -1:]], axis=1)
    labels = jnp.arange(begins.shape[1], dtype=jnp.int32)
    mine = segment[:, :, None] == labels
    position = rows[None] - jnp.sum(jnp.where(mine, begins[:, None, :], 0), axis=2)
    steps = jnp.arange(ROT // 2, dtype=F32)
    inverse = jnp.exp(-math.log(10000.0) * 2.0 * steps / ROT)
    angle = inverse[:, None] * position.reshape(1, 2 * group).astype(F32)
    cos16, sin16 = jnp.cos(angle).T, jnp.sin(angle).T
    still = jnp.zeros((2 * group, HEAD - ROT), F32)
    cosine = jnp.concatenate([cos16, cos16, still + 1.0] * 2, axis=1)
    sine = jnp.concatenate([-sin16, sin16, still] * 2, axis=1)
    lane = jnp.arange(LANES, dtype=jnp.int32) % HEAD
    same = segment.reshape(2 * group, 1) == lane[None, :]
    count = begins.shape[1]
    aq = jnp.where(same & (lane < count), NEG, 0.0).astype(BF)
    ak = jnp.where(~same & (lane < count) | (lane >= 8) & (lane < 11), 1.0, 0.0).astype(BF)

    bias_q = pick(b_qkv.reshape(3, 2, pairs, LANES).transpose(1, 2, 0, 3), half).reshape(1, 3 * q_width)
    bias_1 = pick(b_fc1.reshape(2, f_width), half)[None]

    qkv = qkv_call(h, wq_all, bias_q, cosine, sine)
    o_float, lse = attend_call(qkv, aq, ak, group)
    o = o_float.astype(BF)
    go = jnp.dot(gb, wd_all, preferred_element_type=F32).astype(BF)
    z = jnp.dot(h, w1_all, preferred_element_type=F32) + bias_1
    act = jax.nn.gelu(z, approximate=True).astype(BF)

    block = 2 * shard

    def reduce_weight(left, right):
        parts = []
        for j in range(places):
            columns = lax.dynamic_slice_in_dim(left, lax.rem(at + j, places) * block, block, 1)
            parts.append(lax.dot_general(columns, right, TN, preferred_element_type=F32))
        parts = parts[:1] + [x.astype(BF) for x in parts[1:]]
        total = reduce_line(parts, places).reshape(2, shard, right.shape[1])
        theirs = swap(pick(total, other).astype(BF), "dp", 1).astype(F32)
        out = jnp.zeros(total.shape, F32)
        return place(place(out, pick(total, half), half), theirs, other)

    g_wd = reduce_weight(gb, o)
    g_w2 = reduce_weight(gb, act)
    slope = gelu_slope(z)
    gz_float = jnp.dot(gb, w2_all, preferred_element_type=F32) * slope
    gz = gz_float.astype(BF)
    g_w1 = reduce_weight(h, gz)

    def scatter_rows(factors):
        size = own
        name = lambda g, x, c: g * nt + 2 * x + c

        def blocks(*names):
            return jnp.stack([jnp.asarray(n, jnp.int32) for n in names])

        outs = []
        for part in (0, 1):
            call = lambda index, n, added, dtype=BF: rows_call(index, n, factors, part, 2, added, size, dtype)
            p0, p1 = half, other
            x0, x1 = chip, 1 - chip
            order = [(p1, x1), (p1, x0), (p0, x1), (p0, x0)]
            if part == 1:
                order = [(p1, x1), (p0, x1), (p1, x0), (p0, x0)]
            given = call(blocks(*[name(g, x, 1 - core) for g, x in order]), 4, [])
            got = swap(given, "tensor", 1)
            mine = [name(g, x, core) for g, x in order]
            axes = (("dp", 1), ("tensor", 2)) if part == 0 else (("tensor", 2), ("dp", 1))
            given = call(blocks(*mine[:2]), 2, [got[: 2 * size]])
            got_1 = swap(given, *axes[0])
            given = call(blocks(mine[2]), 1, [got[2 * size : 3 * size], got_1[:size]])
            got_2 = swap(given, *axes[1])
            outs.append(call(blocks(mine[3]), 1, [got[3 * size :], got_1[size:], got_2], F32))
        return jnp.concatenate(outs, axis=1)

    branch = scatter_rows([(act, w2_all), (o, wd_all)])
    output = (xf + branch + b_dense + b_fc2).astype(BF)

    da = attend_back_call(qkv, aq, ak, o_float, lse, go, cosine, sine, group)
    dn = scatter_rows([(gz, w1_all), (da, wq_all)])
    g_wq = reduce_weight(h, da)

    scaled = dn * ln_gain
    m1 = jnp.mean(scaled, axis=1, keepdims=True)
    m2 = jnp.mean(scaled * x_hat, axis=1, keepdims=True)
    grad_x = rstd * (scaled - m1 - x_hat * m2) + gy

    def everywhere(x, axes):
        for axis in axes:
            bit = 1
            while bit < lax.axis_size(axis):
                x = x + swap(x, axis, bit)
                bit *= 2
        return x

    def both_halves(x):
        bit = 2
        while bit < ndp:
            x = x + swap(x, "dp", bit)
            bit *= 2
        out = jnp.zeros((2,) + x.shape, F32)
        return place(place(out, x, half), swap(x, "dp", 1), other)

    early = everywhere(jnp.sum(gy, axis=0, keepdims=True), ("tensor", "dp"))[0]
    late = jnp.stack([jnp.sum(dn * x_hat, axis=0), jnp.sum(dn, axis=0)])
    late = everywhere(late, ("tensor", "dp"))
    g_b1 = both_halves(jnp.sum(gz, axis=0, dtype=F32, keepdims=True)).reshape(2 * f_width)
    g_bq = both_halves(jnp.sum(da, axis=0, dtype=F32, keepdims=True))
    g_bq = g_bq.reshape(2, pairs, 3, LANES).transpose(2, 0, 1, 3).reshape(3, 2 * q_width)

    out_wq = g_wq.reshape(2, shard, pairs, 3, LANES).transpose(1, 3, 0, 2, 4).reshape(shard, 3, 2 * q_width)
    out_wd = g_wd.transpose(0, 2, 1).reshape(2 * q_width, shard)
    out_w1 = g_w1.transpose(1, 0, 2).reshape(shard, 2 * f_width)
    out_w2 = g_w2.transpose(0, 2, 1).reshape(2 * f_width, shard)
    return (
        output,
        grad_x,
        late[0],
        late[1],
        out_wq,
        g_bq,
        out_wd,
        early,
        out_w1,
        g_b1,
        out_w2,
        early,
    )


def solution(mesh):
    rows = P(("dp", "tensor"), None)
    in_specs = (
        rows,
        P("dp", None),
        P(),
        P(),
        P("dp", None, "tensor"),
        P(None, "tensor"),
        P("tensor", "dp"),
        P(),
        P("dp", "tensor"),
        P("tensor"),
        P("tensor", "dp"),
        P(),
        rows,
    )
    out_specs = (
        rows,
        rows,
        P(),
        P(),
        P("dp", None, "tensor"),
        P(None, "tensor"),
        P("tensor", "dp"),
        P(),
        P("dp", "tensor"),
        P("tensor"),
        P("tensor", "dp"),
        P(),
    )
    return jax.shard_map(local, mesh=mesh, in_specs=in_specs, out_specs=out_specs, check_vma=False)
```

```python
import functools
import math

import jax
import jax.numpy as jnp
from jax import lax
from jax.experimental import pallas as pl
from jax.experimental.pallas import tpu as pltpu
from jax.sharding import PartitionSpec as P

HEAD = 64
ROT = 32
EPS = 1e-05
NEG = -1e30
LANES = 128
BF = jnp.bfloat16
F32 = jnp.float32
NT = (((1,), (1,)), ((), ()))
TN = (((0,), (0,)), ((), ()))
VMEM = 56 * 2**20
COST = pl.CostEstimate(flops=0, bytes_accessed=0, transcendentals=0)


def swap(x, axis, bit):
    size = lax.axis_size(axis)
    return lax.ppermute(x, axis, [(i, i ^ bit) for i in range(size)])


def line(x, pairs):
    return lax.ppermute(x, "dp", [(2 * i + s, 2 * j + s) for i, j in pairs for s in (0, 1)])


def after(x, *earlier):
    return lax.optimization_barrier((x,) + earlier)[0]


def pick(x, index):
    return lax.dynamic_index_in_dim(x, index, 0, keepdims=False)


def place(buffer, block, *index):
    return lax.dynamic_update_slice(
        buffer, block.reshape((1,) * len(index) + block.shape), tuple(index) + (0,) * block.ndim
    )


def add(*terms):
    return functools.reduce(lambda a, b: a + b, [x.astype(F32) for x in terms])


def first_terms(parts, places):
    if places != 4:
        return ()
    return (
        line(parts[3], [(0, 1)]),
        line(parts[1], [(3, 2)]),
        line(parts[1], [(0, 1), (1, 2), (2, 3)]),
        line(parts[3], [(1, 0), (2, 1), (3, 2)]),
    )


def join_terms(parts, begun, places, *earlier):
    if places != 4:
        return ()
    joined = add(parts[2], after(begun[0], *earlier), begun[1]).astype(BF)
    return joined, line(joined, [(i, (i + 2) % 4) for i in range(4)])


def last_terms(parts, begun, joined, places, *earlier):
    own = after(parts[0], *earlier) if earlier else parts[0]
    if places == 4:
        return add(own, begun[2], begun[3], joined[1])
    going_up, going_down = parts[places - 1], parts[1]
    for distance in range(places - 1, 0, -1):
        got_up = line(going_up, [(i, i + 1) for i in range(places - distance)])
        got_down = line(going_down, [(i, i - 1) for i in range(distance, places)])
        if distance > 1:
            going_up = add(parts[distance - 1], got_up).astype(BF)
            going_down = add(parts[places - distance + 1], got_down).astype(BF)
    return add(own, got_up, got_down)


def everywhere(x, axes):
    for axis in axes:
        bits = lax.axis_size(axis).bit_length() - 1
        done = 0
        while done < bits:
            now = min(3, bits - done)
            terms = [x] + [swap(x, axis, k << done) for k in range(1, 1 << now)]
            while len(terms) > 1:
                terms = [a + b for a, b in zip(terms[::2], terms[1::2])]
            x = terms[0]
            done += now
    return x


def lanes_of(shape):
    return lax.broadcasted_iota(jnp.int32, shape, 1)


def turn(x, cosine, sine):
    lane = lanes_of(x.shape) % HEAD
    other = jnp.where(lane < ROT // 2, pltpu.roll(x, LANES - ROT // 2, 1), pltpu.roll(x, ROT // 2, 1))
    return x * cosine + other * sine


def qkv_rows(acc, extras, outs):
    bias, cosine, sine = (ref[...] for ref in extras)
    acc = acc + bias
    out_ref = outs[0]
    for at in range(0, acc.shape[1], 3 * LANES):
        q = turn(acc[:, at : at + LANES], cosine, sine).astype(BF)
        out_ref[:, at : at + LANES] = (q.astype(F32) * HEAD**-0.5).astype(BF)
        k = turn(acc[:, at + LANES : at + 2 * LANES], cosine, sine)
        out_ref[:, at + LANES : at + 2 * LANES] = k.astype(BF)
        out_ref[:, at + 2 * LANES : at + 3 * LANES] = acc[:, at + 2 * LANES : at + 3 * LANES].astype(BF)


def plain_rows(acc, extras, outs):
    outs[0][...] = acc.astype(BF)


def gelu_rows(acc, extras, outs):
    z = acc + extras[0][...]
    c = math.sqrt(2.0 / math.pi)
    square = z * z
    gate = 0.5 + 0.5 * jnp.tanh(z * (c + (c * 0.044715) * square))
    value = z * gate
    outs[0][...] = value.astype(BF)
    outs[1][...] = (gate + (value - value * gate) * (2.0 * c + (6.0 * 0.044715 * c) * square)).astype(BF)


def slope_rows(acc, extras, outs):
    outs[0][...] = (acc * extras[0][...].astype(F32)).astype(BF)


class Links:
    def __init__(self, send, recv):
        self.send, self.recv, self.count, self.pending = send, recv, 0, []

    def copy(self, src, dst, device, sends=None, gets=None):
        n = self.count
        self.count += 1
        made = pltpu.make_async_remote_copy(
            src_ref=src,
            dst_ref=dst,
            send_sem=self.send.at[n],
            recv_sem=self.recv.at[n],
            device_id=device,
            device_id_type=pl.DeviceIdType.MESH,
        )
        return Sent(self, made, sends, gets)

    def finish(self):
        for sent in self.pending:
            sent.when(sent.sends, sent.made.wait_send)


class Sent:
    def __init__(self, links, made, sends, gets):
        self.links, self.made, self.sends, self.gets = links, made, sends, gets

    def when(self, condition, action):
        if condition is None:
            action()
        else:
            pl.when(condition)(action)

    def start(self):
        self.when(self.sends, self.made.start)
        self.links.pending.append(self)
        return self

    def get(self):
        self.when(self.gets, self.made.wait_recv)


def greet(devices):
    barrier = pltpu.get_barrier_semaphore()
    for device in devices:
        pl.semaphore_signal(barrier, inc=1, device_id=device, device_id_type=pl.DeviceIdType.MESH)
    pl.semaphore_wait(barrier, len(devices))


class Spot:
    def __init__(self, ndp, nt):
        self.dp, self.t = lax.axis_index("dp"), lax.axis_index("tensor")
        self.half, self.at = self.dp % 2, self.dp // 2
        self.chip, self.core = self.t // 2, self.t % 2
        self.places, self.nt = ndp // 2, nt
        self.mate = (self.dp + 1 - 2 * self.half, self.t)
        self.across = (self.dp, self.t + 2 - 4 * self.chip)
        self.twin = (self.dp, self.t + 1 - 2 * self.core)

    def along(self, place):
        return (2 * place + self.half, self.t)

    def partners(self):
        line = [self.along((self.at + j) % self.places) for j in range(1, self.places)]
        return [self.mate, self.across, self.twin] + line

    def block(self, mates, acrosses, twins):
        g = self.half if not mates else 1 - self.half
        x = self.chip if not acrosses else 1 - self.chip
        c = self.core if not twins else 1 - self.core
        return g * self.nt + 2 * x + c


class GatherRows:
    def __init__(self, links, spot, own, whole, sem):
        self.links, self.spot, self.whole, self.own = links, spot, whole, own
        self.size = own.shape[0]
        self.mid = self.size // 4
        self.local = pltpu.make_async_copy(own, self.rows(spot.block(0, 0, 0)), sem)

    def rows(self, block, first=0, count=None):
        at = pl.multiple_of(block * self.size, self.size) + first
        return self.whole.at[pl.ds(at, count or self.size)]

    def forward(self, block, device, first=0, count=None):
        place = self.rows(block, first, count)
        return self.links.copy(place, place, device).start()

    def first(self):
        spot = self.spot
        self.local.start()
        place = self.rows(spot.block(0, 0, 0))
        self.x = self.links.copy(self.own, place, spot.across).start()
        self.y = self.links.copy(self.own, place, spot.mate).start()
        self.parts = [self.links.copy(self.own, place, spot.twin).start()]

    def second(self):
        spot, rest = self.spot, self.size - self.mid
        self.x.get()
        self.low = self.forward(spot.block(0, 1, 0), spot.mate, 0, self.mid)
        self.parts.append(self.forward(spot.block(0, 1, 0), spot.twin))
        self.y.get()
        self.high = self.forward(spot.block(1, 0, 0), spot.across, self.mid, rest)
        self.parts.append(self.forward(spot.block(1, 0, 0), spot.twin))

    def third(self):
        spot, rest = self.spot, self.size - self.mid
        self.low.get()
        self.parts.append(self.forward(spot.block(1, 1, 0), spot.twin, 0, self.mid))
        self.high.get()
        self.parts.append(self.forward(spot.block(1, 1, 0), spot.twin, self.mid, rest))

    def finish(self):
        self.local.wait()
        for part in self.parts:
            part.get()


class GatherWeight:
    def __init__(self, links, spot, halves, whole, sem):
        self.links, self.spot, self.halves, self.whole = links, spot, halves, whole
        self.shard = halves.shape[1]
        at = pl.multiple_of((2 * spot.at + spot.half) * self.shard, self.shard)
        self.place = whole.at[pl.ds(at, self.shard)]
        self.local = pltpu.make_async_copy(halves.at[spot.half], self.place, sem)

    def pair(self, place):
        return self.whole.at[pl.ds(pl.multiple_of(place * 2 * self.shard, 2 * self.shard), 2 * self.shard)]

    def forward(self, place, to, sends=None, gets=None):
        return self.links.copy(self.pair(place), self.pair(place), self.spot.along(to), sends, gets).start()

    def first(self):
        self.local.start()
        self.y = self.links.copy(self.halves.at[1 - self.spot.half], self.place, self.spot.mate).start()

    def second(self):
        at, places = self.spot.at, self.spot.places
        self.local.wait()
        self.y.get()
        if places == 4:
            self.two = self.forward(at, (at + 2) % 4)
            self.parts = [
                self.forward(at, (at + 1) % 4, at < 3, at > 0),
                self.forward(at, (at + 3) % 4, at > 0, at < 3),
            ]
        else:
            self.parts = [self.forward(at, (at + j) % places) for j in range(1, places)]

    def third(self):
        at = self.spot.at
        if self.spot.places == 4:
            self.two.get()
            inner = (at == 1) | (at == 2)
            self.parts.append(self.forward((at + 2) % 4, 3 * (at // 2), inner, ~inner))

    def finish(self):
        for part in self.parts:
            part.get()


def qkv_body(h_ref, w_ref, b_ref, cos_ref, sin_ref, out_ref):
    acc = jnp.dot(h_ref[...], w_ref[...], preferred_element_type=F32) + b_ref[...]
    cosine, sine = cos_ref[...], sin_ref[...]
    for at in range(0, acc.shape[1], 3 * LANES):
        q = turn(acc[:, at : at + LANES], cosine, sine).astype(BF)
        out_ref[:, at : at + LANES] = (q.astype(F32) * HEAD**-0.5).astype(BF)
        k = turn(acc[:, at + LANES : at + 2 * LANES], cosine, sine)
        out_ref[:, at + LANES : at + 2 * LANES] = k.astype(BF)
        out_ref[:, at + 2 * LANES : at + 3 * LANES] = acc[:, at + 2 * LANES : at + 3 * LANES].astype(BF)


def gelu_body(h_ref, w_ref, b_ref, act_ref, slope_ref):
    z = jnp.dot(h_ref[...], w_ref[...], preferred_element_type=F32) + b_ref[...]
    c = math.sqrt(2.0 / math.pi)
    square = z * z
    gate = 0.5 + 0.5 * jnp.tanh(z * (c + (c * 0.044715) * square))
    value = z * gate
    act_ref[...] = value.astype(BF)
    slope_ref[...] = (gate + (value - value * gate) * (2.0 * c + (6.0 * 0.044715 * c) * square)).astype(BF)


def plain_body(h_ref, w_ref, out_ref):
    out_ref[...] = jnp.dot(h_ref[...], w_ref[...], preferred_element_type=F32).astype(BF)


def slope_body(h_ref, w_ref, slope_ref, out_ref):
    acc = jnp.dot(h_ref[...], w_ref[...], preferred_element_type=F32)
    out_ref[...] = (acc * slope_ref[...].astype(F32)).astype(BF)


def by_rows(body, ins, outs, block, first=0, count=None):
    total = outs[0].shape[0]
    count = count or total // block

    def spec(ref):
        width = ref.shape[1]
        if ref.shape[0] == total:
            return pl.BlockSpec((block, width), lambda i: (first + i, 0))
        return pl.BlockSpec(ref.shape, lambda i: (0, 0))

    pltpu.emit_pipeline(
        body, grid=(count,), in_specs=[spec(r) for r in ins], out_specs=[spec(r) for r in outs]
    )(*ins, *outs)


def by_heads(body, wide_ins, ins, aug_ins, outs, rows, g):
    pairs = wide_ins[0].shape[1] // (3 * LANES)

    def spec(ref, kind):
        if kind == 2:
            return pl.BlockSpec((rows, LANES), lambda j: (g, 0))
        width = 3 * LANES if ref.shape[1] == pairs * 3 * LANES else LANES
        return pl.BlockSpec((rows, width), lambda j: (g, j))

    specs = [spec(r, 0) for r in wide_ins] + [spec(r, 2) for r in aug_ins] + [spec(r, 0) for r in ins]
    pltpu.emit_pipeline(
        body, grid=(pairs,), in_specs=specs, out_specs=[spec(r, 0) for r in outs]
    )(*wide_ins, *aug_ins, *ins, *outs)


def front_kernel(ndp, nt, *refs):
    refs = list(refs)
    take = lambda n: [refs.pop(0) for _ in range(n)]
    h_own, gb_own, wq2, w12, wd2, w22, bias_q, bias_1, cosine, sine, aq, ak = take(12)
    h, gb, wq, w1, wd, w2, qkv, o_float, o, lse, act, slope, go, da = take(14)
    dk_s, dv_s, dqt_s, local_sem, send, recv = take(6)
    spot = Spot(ndp, nt)
    links = Links(send, recv)
    group = h.shape[0] // 2
    own = h_own.shape[0]
    greet(spot.partners())

    rows_h = GatherRows(links, spot, h_own, h, local_sem.at[0])
    rows_gb = GatherRows(links, spot, gb_own, gb, local_sem.at[1])
    gather_q = GatherWeight(links, spot, wq2, wq, local_sem.at[2])
    gather_1 = GatherWeight(links, spot, w12, w1, local_sem.at[3])
    gather_d = GatherWeight(links, spot, wd2, wd, local_sem.at[4])
    gather_2 = GatherWeight(links, spot, w22, w2, local_sem.at[5])

    gather_q.first()
    rows_h.first()
    gather_1.first()
    gather_q.second()
    rows_h.second()
    gather_q.third()
    gather_1.second()
    rows_h.third()
    gather_q.finish()
    rows_gb.first()
    gather_d.first()
    gather_2.first()
    rows_h.finish()
    by_rows(qkv_body, [h, wq, bias_q, cosine, sine], [qkv], own)
    attend = functools.partial(attend_kernel, group, 512)
    by_heads(attend, [qkv], [], [aq, ak], [o_float, o, lse], group, 0)
    gather_1.third()
    gather_d.second()
    by_heads(attend, [qkv], [], [aq, ak], [o_float, o, lse], group, 1)
    rows_gb.second()
    gather_2.second()
    gather_1.finish()
    steps = 2 * group // own
    by_rows(gelu_body, [h, w1, bias_1], [act, slope], own, 0, steps // 2)
    rows_gb.third()
    gather_d.third()
    by_rows(gelu_body, [h, w1, bias_1], [act, slope], own, steps // 2, steps // 2)
    rows_gb.finish()
    gather_d.finish()
    by_rows(plain_body, [gb, wd], [go], own)
    back = functools.partial(attend_back_kernel, group, 256)

    def attend_back(qkv_ref, aq_ref, ak_ref, cos_ref, sin_ref, o_ref, lse_ref, go_ref, out_ref):
        back(qkv_ref, aq_ref, ak_ref, o_ref, lse_ref, go_ref, cos_ref, sin_ref, out_ref, dk_s, dv_s, dqt_s)

    by_heads(attend_back, [qkv], [o_float, lse, go], [aq, ak, cosine, sine], [da], group, 0)
    gather_2.third()
    by_heads(attend_back, [qkv], [o_float, lse, go], [aq, ak, cosine, sine], [da], group, 1)
    gather_2.finish()
    links.finish()


def front_call(ndp, nt, h_own, gb_own, weights, biases, tables):
    own, width = h_own.shape
    rows = 2 * nt * own
    q3, f, q = weights[0].shape[2], weights[1].shape[2], weights[2].shape[2]
    shape = lambda a, b, dtype=BF: jax.ShapeDtypeStruct((a, b), dtype)
    out_shape = [shape(rows, width), shape(rows, width)]
    out_shape += [shape(width, n) for n in (q3, f, q, f)]
    out_shape += [shape(rows, q3), shape(rows, q, F32), shape(rows, q), shape(rows, q, F32)]
    out_shape += [shape(rows, f), shape(rows, f), shape(rows, q), shape(rows, q3)]
    anywhere = pl.BlockSpec(memory_space=pl.ANY)
    group = nt * own
    transfers = 2 * 10 + 4 * (1 + max(4, ndp // 2))
    return pl.pallas_call(
        functools.partial(front_kernel, ndp, nt),
        in_specs=[anywhere] * 12,
        out_specs=[anywhere] * 14,
        out_shape=out_shape,
        scratch_shapes=[
            pltpu.VMEM((group, LANES), F32),
            pltpu.VMEM((group, LANES), F32),
            pltpu.VMEM((LANES, group), F32),
            pltpu.SemaphoreType.DMA((6,)),
            pltpu.SemaphoreType.DMA((transfers,)),
            pltpu.SemaphoreType.DMA((transfers,)),
        ],
        compiler_params=pltpu.CompilerParams(collective_id=0, has_side_effects=True, vmem_limit_bytes=VMEM),
    )(h_own, gb_own, *weights, *biases, *tables)


def outer_kernel(places, steps, n_right, order_ref, left_ref, *refs):
    rights, outs, acc = refs[:n_right], refs[n_right : n_right + places], refs[n_right + places]
    j, r = pl.program_id(0), pl.program_id(1)
    block = left_ref.shape[0]
    here = pl.ds(pl.multiple_of(r * block, block), block)
    first = 0
    for right_ref in rights:
        columns = slice(first, first + right_ref.shape[1])
        first += right_ref.shape[1]
        term = lax.dot_general(left_ref[...], right_ref[here], TN, preferred_element_type=F32)
        for n in range(places):
            @pl.when((j == n) & (r == steps - 1))
            def _():
                outs[n][:, columns] = (term if steps == 1 else acc[:, columns] + term).astype(outs[n].dtype)

        if steps > 1:
            @pl.when(r == 0)
            def _():
                acc[:, columns] = term

            @pl.when((r > 0) & (r < steps - 1))
            def _():
                acc[:, columns] += term


def outer_call(left, rights, at, places, block=2048):
    rows, width = left.shape
    columns = sum(right.shape[1] for right in rights)
    size = width // places
    order = (at + jnp.arange(places, dtype=jnp.int32)) % places
    steps = rows // block
    return pl.pallas_call(
        functools.partial(outer_kernel, places, steps, len(rights)),
        grid_spec=pltpu.PrefetchScalarGridSpec(
            num_scalar_prefetch=1,
            grid=(places, steps),
            in_specs=[pl.BlockSpec((block, size), lambda j, r, order: (r, order[j]))]
            + [pl.BlockSpec((rows, right.shape[1]), lambda j, r, order: (0, 0)) for right in rights],
            out_specs=[pl.BlockSpec((size, columns), lambda j, r, order: (0, 0))] * places,
            scratch_shapes=[pltpu.VMEM((size, columns), F32)],
        ),
        out_shape=[jax.ShapeDtypeStruct((size, columns), BF if j else F32) for j in range(places)],
        compiler_params=pltpu.CompilerParams(vmem_limit_bytes=VMEM),
        cost_estimate=COST,
    )(order, left, *rights)


def attend_kernel(rows, block, qkv_ref, aq_ref, ak_ref, *refs):
    o_ref, bf_ref, lse_ref = refs[-3:]
    lane = lanes_of((rows, LANES))
    lane_q = lanes_of((block, LANES))
    one = jnp.where(lane % HEAD < 3, 1.0, 0.0).astype(BF)
    first = lane < HEAD
    keys = [jnp.where(half, qkv_ref[:, LANES : 2 * LANES], ak_ref[...]) for half in (first, ~first)]
    values = [jnp.where(half, qkv_ref[:, 2 * LANES :], one) for half in (first, ~first)]
    causal = lanes_of((block, block)) <= lax.broadcasted_iota(jnp.int32, (block, block), 0)
    for b in range(rows // block):
        here = pl.ds(b * block, block)
        lo, hi = b * block, (b + 1) * block
        outs, sums = [], []
        for side in (0, 1):
            half = (lane_q < HEAD) if side == 0 else (lane_q >= HEAD)
            q = jnp.where(half, qkv_ref[here, :LANES], aq_ref[here])
            s_near = lax.dot_general(q, keys[side][lo:hi], NT, preferred_element_type=F32)
            s_near = jnp.where(causal, s_near, NEG)
            top = jnp.max(s_near, axis=1, keepdims=True)
            if b:
                s_far = lax.dot_general(q, keys[side][:lo], NT, preferred_element_type=F32)
                top = jnp.maximum(top, jnp.max(s_far, axis=1, keepdims=True))
            o = jnp.dot(jnp.exp(s_near - top).astype(BF), values[side][lo:hi], preferred_element_type=F32)
            if b:
                o = o + jnp.dot(
                    jnp.exp(s_far - top).astype(BF), values[side][:lo], preferred_element_type=F32
                )
            at = HEAD if side == 0 else 0
            total = o[:, at : at + 1]
            outs.append(o / total)
            sums.append(top + jnp.log(total))
        out = jnp.where(lane_q < HEAD, outs[0], outs[1])
        o_ref[here] = out
        bf_ref[here] = out.astype(BF)
        lse_ref[here] = jnp.where(lane_q < HEAD, sums[0], sums[1])


def split3(x):
    a = x.astype(BF).astype(F32)
    b = (x - a).astype(BF).astype(F32)
    return a, b, x - a - b


def attend_back_kernel(
    rows, block, qkv_ref, aq_ref, ak_ref, o_ref, lse_ref, go_ref, cos_ref, sin_ref, *refs
):
    out_ref, dk_s, dv_s, dqt_s = refs
    lane = lanes_of((rows, LANES))
    lane_k = lanes_of((block, LANES))
    one = jnp.where(lane % HEAD < 3, 1.0, 0.0).astype(BF)
    causal = lax.broadcasted_iota(jnp.int32, (block, block), 0) <= lanes_of((block, block))
    prod = o_ref[...] * go_ref[...].astype(F32)
    dq_first = None
    for side in (0, 1):
        half = (lane < HEAD) if side == 0 else (lane >= HEAD)
        delta = -jnp.sum(jnp.where(half, prod, 0.0), axis=1, keepdims=True)
        at = 0 if side == 0 else HEAD
        lse = -lse_ref[:, at : at + 1]
        q = jnp.where(half, qkv_ref[:, :LANES], aq_ref[...]).astype(F32)
        g = jnp.where(half, go_ref[...].astype(F32), 0.0)
        base = HEAD - at
        for i, (a, d) in enumerate(zip(split3(lse), split3(delta))):
            q = jnp.where(lane == base + 8 + i, a, q)
            g = jnp.where(lane == base + i, d, g)
        q, g = q.astype(BF), g.astype(BF)
        k = jnp.where(half, qkv_ref[:, LANES : 2 * LANES], ak_ref[...])
        v = jnp.where(half, qkv_ref[:, 2 * LANES :], one)
        kt = k.T
        for b in range(rows // block):
            lo, hi = b * block, (b + 1) * block
            here = pl.ds(lo, block)
            st = lax.dot_general(k[lo:hi], q[lo:], NT, preferred_element_type=F32)
            dpt = lax.dot_general(v[lo:hi], g[lo:], NT, preferred_element_type=F32)
            p = jnp.exp(st)
            near = jnp.where(causal, p[:, :block], 0.0)
            p = jnp.concatenate([near, p[:, block:]], axis=1) if hi < rows else near
            ds = (p * dpt).astype(BF)
            dv = jnp.dot(p.astype(BF), g[lo:], preferred_element_type=F32)
            dk = jnp.dot(ds, q[lo:], preferred_element_type=F32)
            dq = jnp.dot(kt[:, lo:hi], ds, preferred_element_type=F32)
            if side == 0:
                dk_s[here] = dk
                dv_s[here] = dv
            else:
                dk = jnp.where(lane_k < HEAD, dk_s[here], dk)
                dv = jnp.where(lane_k < HEAD, dv_s[here], dv)
                out_ref[here, LANES : 2 * LANES] = turn(dk, cos_ref[here], -sin_ref[here]).astype(BF)
                out_ref[here, 2 * LANES :] = dv.astype(BF)
            if b == 0:
                dqt_s[...] = dq
            else:
                dqt_s[:, lo:] += dq
        d = dqt_s[...].T * HEAD**-0.5
        if side == 0:
            dq_first = d
        else:
            d = jnp.where(lane < HEAD, dq_first, d)
            out_ref[:, :LANES] = turn(d, cos_ref[...], -sin_ref[...]).astype(BF)


def slope_call(rows, w, slope, block):
    total, depth = rows.shape
    columns = w.shape[1]
    return pl.pallas_call(
        slope_body,
        grid=(total // block,),
        in_specs=[
            pl.BlockSpec((block, depth), lambda i: (i, 0)),
            pl.BlockSpec((depth, columns), lambda i: (0, 0)),
            pl.BlockSpec((block, columns), lambda i: (i, 0)),
        ],
        out_specs=pl.BlockSpec((block, columns), lambda i: (i, 0)),
        out_shape=jax.ShapeDtypeStruct((total, columns), BF),
        compiler_params=pltpu.CompilerParams(vmem_limit_bytes=VMEM),
        cost_estimate=COST,
    )(rows, w, slope)


def rows_kernel(count, terms, added, dtype, index_ref, *refs):
    ins, outs = refs[:-2], refs[-2:]
    i = pl.program_id(0)
    acc = lax.dot_general(ins[0][...], ins[1][...], NT, preferred_element_type=F32)
    for n in range(1, terms):
        acc = acc + lax.dot_general(ins[2 * n][...], ins[2 * n + 1][...], NT, preferred_element_type=F32)
    for part in (0, 1):
        @pl.when(i // count == part)
        def _():
            total = acc
            first = 2 * terms + part * added
            for ref in ins[first : first + added]:
                total = total + ref[...].astype(F32)
            outs[part][...] = total.astype(dtype)


def rows_call(index, factors, added, block, dtype):
    count = len(index[0])
    columns = factors[0][1].shape[0] // 2
    in_specs, args = [], []
    for a, b in factors:
        depth = a.shape[1]
        in_specs.append(pl.BlockSpec((block, depth), lambda i, index: (index[i], 0)))
        in_specs.append(pl.BlockSpec((columns, depth), lambda i, index: (i // count, 0)))
        args += [a, b]
    places = (lambda i: jnp.minimum(i, count - 1), lambda i: jnp.maximum(i - count, 0))
    for part in (0, 1):
        for a, first in added[part]:
            spec = pl.BlockSpec(
                (block, columns), lambda i, index, first=first, part=part: (first + places[part](i), 0)
            )
            in_specs.append(spec)
            args.append(a)
    return pl.pallas_call(
        functools.partial(rows_kernel, count, len(factors), len(added[0]), dtype),
        grid_spec=pltpu.PrefetchScalarGridSpec(
            num_scalar_prefetch=1,
            grid=(2 * count,),
            in_specs=in_specs,
            out_specs=[
                pl.BlockSpec((block, columns), lambda i, index: (places[0](i), 0)),
                pl.BlockSpec((block, columns), lambda i, index: (places[1](i), 0)),
            ],
        ),
        out_shape=[jax.ShapeDtypeStruct((count * block, columns), dtype)] * 2,
        compiler_params=pltpu.CompilerParams(vmem_limit_bytes=VMEM),
        cost_estimate=COST,
    )(jnp.stack(index[0] + index[1]).astype(jnp.int32), *args)


def local(
    layer_input,
    seq_lens,
    ln_gain,
    ln_bias,
    w_qkv,
    b_qkv,
    w_dense,
    b_dense,
    w_fc1,
    b_fc1,
    w_fc2,
    b_fc2,
    cotangent,
):
    own, width = layer_input.shape
    ndp, nt = lax.axis_size("dp"), lax.axis_size("tensor")
    dp, t = lax.axis_index("dp"), lax.axis_index("tensor")
    half, at, places = dp % 2, dp // 2, ndp // 2
    chip, core = t // 2, t % 2
    group = own * nt
    shard = w_qkv.shape[0]
    q_width = w_qkv.shape[2] // 2
    f_width = w_fc1.shape[1] // 2
    pairs = q_width // LANES
    other = 1 - half

    wq = w_qkv.reshape(shard, 3, 2, pairs, LANES).transpose(2, 0, 3, 1, 4).reshape(2, shard, 3 * q_width)
    wd = w_dense.T.reshape(shard, 2, q_width).transpose(1, 0, 2)
    w1 = w_fc1.reshape(shard, 2, f_width).transpose(1, 0, 2)
    w2 = w_fc2.T.reshape(shard, 2, f_width).transpose(1, 0, 2)

    xf = layer_input.astype(F32)
    mean = jnp.mean(xf, axis=1, keepdims=True)
    centred = xf - mean
    rstd = lax.rsqrt(jnp.mean(centred * centred, axis=1, keepdims=True) + EPS)
    x_hat = centred * rstd
    h_own = (x_hat * ln_gain + ln_bias).astype(BF)
    used = jnp.sum(seq_lens[0])
    valid = (t * own + jnp.arange(own, dtype=jnp.int32) < used).astype(F32)[:, None]
    gy = cotangent.astype(F32) * valid
    gb_own = gy.astype(BF)

    lens_of_mate = swap(seq_lens, "dp", 1)

    lens = jnp.zeros((2, seq_lens.shape[1]), jnp.int32)
    lens = place(place(lens, seq_lens[0], half), lens_of_mate[0], other)
    ends = jnp.cumsum(lens, axis=1)
    rows = jnp.arange(group, dtype=jnp.int32)
    segment = jnp.sum((rows[None, :, None] >= ends[:, None, :]).astype(jnp.int32), axis=2)
    begins = jnp.concatenate([ends - lens, ends[:, -1:]], axis=1)
    labels = jnp.arange(begins.shape[1], dtype=jnp.int32)
    mine = segment[:, :, None] == labels
    position = rows[None] - jnp.sum(jnp.where(mine, begins[:, None, :], 0), axis=2)
    steps = jnp.arange(ROT // 2, dtype=F32)
    inverse = jnp.exp(-math.log(10000.0) * 2.0 * steps / ROT)
    angle = inverse[:, None] * position.reshape(1, 2 * group).astype(F32)
    cos16, sin16 = jnp.cos(angle).T, jnp.sin(angle).T
    still = jnp.zeros((2 * group, HEAD - ROT), F32)
    cosine = jnp.concatenate([cos16, cos16, still + 1.0] * 2, axis=1)
    sine = jnp.concatenate([-sin16, sin16, still] * 2, axis=1)
    lane = jnp.arange(LANES, dtype=jnp.int32) % HEAD
    same = segment.reshape(2 * group, 1) == lane[None, :]
    count = begins.shape[1]
    aq = jnp.where(same & (lane < count), NEG, 0.0).astype(BF)
    ak = jnp.where(~same & (lane < count) | (lane >= 8) & (lane < 11), 1.0, 0.0).astype(BF)

    bias_q = pick(b_qkv.reshape(3, 2, pairs, LANES).transpose(1, 2, 0, 3), half).reshape(1, 3 * q_width)
    bias_1 = pick(b_fc1.reshape(2, f_width), half)[None]

    def weight_out(total, *earlier):
        total = total.reshape(2, shard, total.shape[1])
        theirs = swap(pick(total, other).astype(BF), "dp", 1)
        return pick(total, half), theirs

    def both(mine, theirs):
        theirs = theirs.astype(F32)
        return jnp.stack([jnp.where(half == 0, mine, theirs), jnp.where(half == 0, theirs, mine)])

    name = lambda g, x, c: g * nt + 2 * x + c
    p0, p1, x0, x1 = half, other, chip, 1 - chip
    targets = ([(p1, x1), (p1, x0), (p0, x1), (p0, x0)], [(p1, x1), (p0, x1), (p1, x0), (p0, x0)])
    axes = ((("dp", 1), ("tensor", 2)), (("tensor", 2), ("dp", 1)))

    def scatter(stage, factors, got, *earlier):
        if earlier:
            factors = [(after(factors[0][0], *earlier), factors[0][1])] + factors[1:]
        first, last = ((0, 4), (0, 2), (2, 3), (3, 4))[stage]
        c = 1 - core if stage == 0 else core
        index = [[name(g, x, c) for g, x in target[first:last]] for target in targets]
        offsets = ((), (0,), (2, 0), (3, 1, 0))[stage]
        added = [[(got[n][part], offsets[n]) for n in range(stage)] for part in (0, 1)]
        outs = rows_call(index, factors, added, own, F32 if stage == 3 else BF)
        if stage == 3:
            return outs
        if stage == 0:
            return [swap(x, "tensor", 1) for x in outs]
        return [swap(x, *axes[part][stage - 1]) for part, x in enumerate(outs)]

    h, gb, wq_all, w1_all, wd_all, w2_all, qkv, o_float, o, lse, act, slope, go, da = front_call(
        ndp, nt, h_own, gb_own, [wq, w1, wd, w2], [bias_q, bias_1], [cosine, sine, aq, ak]
    )
    g2 = outer_call(gb, [act, o], at, places)
    g2_begun = first_terms(g2, places)
    gz = slope_call(after(gb, g2[0]), w2_all, slope, own)
    g2_joined = join_terms(g2, g2_begun, places, gz)
    branch_by, grad_by = [(act, w2_all), (o, wd_all)], [(gz, w1_all)]
    branch = [scatter(0, branch_by, [], gz)]
    g1 = outer_call(after(h, gz, branch_by[0][0]), [gz], at, places)
    g1_begun = first_terms(g1, places)
    g2_out = weight_out(last_terms(g2, g2_begun, g2_joined, places, g1[0]))
    branch.append(scatter(1, branch_by, branch, g1[0], g2_out[0]))
    grad_by.append((da, wq_all))
    grad = [scatter(0, grad_by, [], g2_out[0])]
    g1_joined = join_terms(g1, g1_begun, places, grad[0][0])
    branch.append(scatter(2, branch_by, branch, grad[0][0]))
    gq = outer_call(after(h, branch[2][0]), [da], at, places)
    gq_begun = first_terms(gq, places)
    grad.append(scatter(1, grad_by, grad, gq[0]))
    g1_out = weight_out(last_terms(g1, g1_begun, g1_joined, places, gq[0]))
    gq_joined = join_terms(gq, gq_begun, places, g1_out[0])
    branch = jnp.concatenate(scatter(3, branch_by, branch, gq[0]), axis=1)
    output = (xf + branch + b_dense + b_fc2).astype(BF)
    grad.append(scatter(2, grad_by, grad, output))
    gq_out = weight_out(last_terms(gq, gq_begun, gq_joined, places))
    dn = jnp.concatenate(scatter(3, grad_by, grad), axis=1)

    scaled = dn * ln_gain
    m1 = jnp.mean(scaled, axis=1, keepdims=True)
    m2 = jnp.mean(scaled * x_hat, axis=1, keepdims=True)
    grad_x = rstd * (scaled - m1 - x_hat * m2) + gy

    def spread(x):
        return place(jnp.zeros((2,) + x.shape, F32), x, half).reshape(-1)

    late = everywhere(jnp.stack([jnp.sum(dn * x_hat, axis=0), jnp.sum(dn, axis=0)]), ("tensor", "dp"))
    early = everywhere(jnp.sum(gy, axis=0, keepdims=True), ("tensor", "dp"))[0]
    g_b1 = spread(jnp.sum(gz, axis=0, dtype=F32))
    g_bq = spread(jnp.sum(da, axis=0, dtype=F32))
    g_biases = everywhere(jnp.concatenate([g_b1, g_bq])[None], ("dp",))[0]
    g_b1 = g_biases[: 2 * f_width]
    g_bq = g_biases[2 * f_width :].reshape(2, pairs, 3, LANES).transpose(2, 0, 1, 3).reshape(3, 2 * q_width)

    g_2 = both(*g2_out)
    g_w2, g_wd = g_2[:, :, :f_width], g_2[:, :, f_width:]
    g_w1, g_wq = both(*g1_out), both(*gq_out)
    out_wq = g_wq.reshape(2, shard, pairs, 3, LANES).transpose(1, 3, 0, 2, 4).reshape(shard, 3, 2 * q_width)
    out_wd = g_wd.transpose(0, 2, 1).reshape(2 * q_width, shard)
    out_w1 = g_w1.transpose(1, 0, 2).reshape(shard, 2 * f_width)
    out_w2 = g_w2.transpose(0, 2, 1).reshape(2 * f_width, shard)
    return (
        output,
        grad_x,
        late[0],
        late[1],
        out_wq,
        g_bq,
        out_wd,
        early,
        out_w1,
        g_b1,
        out_w2,
        early,
    )


def solution(mesh):
    rows = P(("dp", "tensor"), None)
    in_specs = (
        rows,
        P("dp", None),
        P(),
        P(),
        P("dp", None, "tensor"),
        P(None, "tensor"),
        P("tensor", "dp"),
        P(),
        P("dp", "tensor"),
        P("tensor"),
        P("tensor", "dp"),
        P(),
        rows,
    )
    out_specs = (
        rows,
        rows,
        P(),
        P(),
        P("dp", None, "tensor"),
        P(None, "tensor"),
        P("tensor", "dp"),
        P(),
        P("dp", "tensor"),
        P("tensor"),
        P("tensor", "dp"),
        P(),
    )
    return jax.shard_map(local, mesh=mesh, in_specs=in_specs, out_specs=out_specs, check_vma=False)
```

```python
import functools
import math

import jax
import jax.numpy as jnp
from jax import lax
from jax.experimental import pallas as pl
from jax.experimental.pallas import tpu as pltpu
from jax.sharding import PartitionSpec as P

HEAD = 64
ROT = 32
EPS = 1e-05
NEG = -1e30
LANES = 128
BF = jnp.bfloat16
F32 = jnp.float32
NT = (((1,), (1,)), ((), ()))
TN = (((0,), (0,)), ((), ()))
VMEM = 56 * 2**20
COST = pl.CostEstimate(flops=0, bytes_accessed=0, transcendentals=0)


def swap(x, axis, bit):
    size = lax.axis_size(axis)
    return lax.ppermute(x, axis, [(i, i ^ bit) for i in range(size)])


def pick(x, index):
    return lax.dynamic_index_in_dim(x, index, 0, keepdims=False)


def place(buffer, block, *index):
    return lax.dynamic_update_slice(
        buffer, block.reshape((1,) * len(index) + block.shape), tuple(index) + (0,) * block.ndim
    )


def lanes_of(shape):
    return lax.broadcasted_iota(jnp.int32, shape, 1)


def turn(x, cosine, sine):
    lane = lanes_of(x.shape) % HEAD
    other = jnp.where(lane < ROT // 2, pltpu.roll(x, LANES - ROT // 2, 1), pltpu.roll(x, ROT // 2, 1))
    return x * cosine + other * sine


def qkv_rows(acc, extras, outs):
    bias, cosine, sine = (ref[...] for ref in extras)
    acc = acc + bias
    out_ref = outs[0]
    for at in range(0, acc.shape[1], 3 * LANES):
        q = turn(acc[:, at : at + LANES], cosine, sine).astype(BF)
        out_ref[:, at : at + LANES] = (q.astype(F32) * HEAD**-0.5).astype(BF)
        k = turn(acc[:, at + LANES : at + 2 * LANES], cosine, sine)
        out_ref[:, at + LANES : at + 2 * LANES] = k.astype(BF)
        out_ref[:, at + 2 * LANES : at + 3 * LANES] = acc[:, at + 2 * LANES : at + 3 * LANES].astype(BF)


def plain_rows(acc, extras, outs):
    outs[0][...] = acc.astype(BF)


def gelu_rows(acc, extras, outs):
    z = acc + extras[0][...]
    c = math.sqrt(2.0 / math.pi)
    square = z * z
    gate = 0.5 + 0.5 * jnp.tanh(z * (c + (c * 0.044715) * square))
    value = z * gate
    outs[0][...] = value.astype(BF)
    outs[1][...] = (gate + (value - value * gate) * (2.0 * c + (6.0 * 0.044715 * c) * square)).astype(BF)


def slope_rows(acc, extras, outs):
    outs[0][...] = (acc * extras[0][...].astype(F32)).astype(BF)


class Links:
    def __init__(self, send, recv):
        self.send, self.recv, self.count, self.pending = send, recv, 0, []

    def copy(self, src, dst, device, sends=None, gets=None):
        n = self.count
        self.count += 1
        made = pltpu.make_async_remote_copy(
            src_ref=src,
            dst_ref=dst,
            send_sem=self.send.at[n],
            recv_sem=self.recv.at[n],
            device_id=device,
            device_id_type=pl.DeviceIdType.MESH,
        )
        return Sent(self, made, sends, gets)

    def finish(self):
        for sent in self.pending:
            sent.when(sent.sends, sent.made.wait_send)


class Sent:
    def __init__(self, links, made, sends, gets):
        self.links, self.made, self.sends, self.gets = links, made, sends, gets

    def when(self, condition, action):
        if condition is None:
            action()
        else:
            pl.when(condition)(action)

    def start(self):
        self.when(self.sends, self.made.start)
        self.links.pending.append(self)
        return self

    def get(self):
        self.when(self.gets, self.made.wait_recv)

    def drain(self):
        self.links.pending.remove(self)
        self.when(self.sends, self.made.wait_send)


def greet(devices):
    barrier = pltpu.get_barrier_semaphore()
    for device in devices:
        pl.semaphore_signal(barrier, inc=1, device_id=device, device_id_type=pl.DeviceIdType.MESH)
    pl.semaphore_wait(barrier, len(devices))


class Spot:
    def __init__(self, ndp, nt):
        self.dp, self.t = lax.axis_index("dp"), lax.axis_index("tensor")
        self.half, self.at = self.dp % 2, self.dp // 2
        self.chip, self.core = self.t // 2, self.t % 2
        self.places, self.nt = ndp // 2, nt
        self.mate = (self.dp + 1 - 2 * self.half, self.t)
        self.across = (self.dp, self.t + 2 - 4 * self.chip)
        self.twin = (self.dp, self.t + 1 - 2 * self.core)

    def along(self, place):
        return (2 * place + self.half, self.t)

    def partners(self):
        line = [self.along((self.at + j) % self.places) for j in range(1, self.places)]
        return [self.mate, self.across, self.twin] + line

    def block(self, mates, acrosses, twins):
        g = self.half if not mates else 1 - self.half
        x = self.chip if not acrosses else 1 - self.chip
        c = self.core if not twins else 1 - self.core
        return g * self.nt + 2 * x + c


class GatherRows:
    def __init__(self, links, spot, own, whole, sem):
        self.links, self.spot, self.whole, self.own = links, spot, whole, own
        self.size = own.shape[0]
        self.mid = self.size // 4
        self.local = pltpu.make_async_copy(own, self.rows(spot.block(0, 0, 0)), sem)

    def rows(self, block, first=0, count=None):
        at = pl.multiple_of(block * self.size, self.size) + first
        return self.whole.at[pl.ds(at, count or self.size)]

    def forward(self, block, device, first=0, count=None):
        place = self.rows(block, first, count)
        return self.links.copy(place, place, device).start()

    def first(self):
        spot = self.spot
        self.local.start()
        place = self.rows(spot.block(0, 0, 0))
        self.x = self.links.copy(self.own, place, spot.across).start()
        self.y = self.links.copy(self.own, place, spot.mate).start()
        self.parts = [self.links.copy(self.own, place, spot.twin).start()]

    def second(self):
        spot, rest = self.spot, self.size - self.mid
        self.x.get()
        self.low = self.forward(spot.block(0, 1, 0), spot.mate, 0, self.mid)
        self.parts.append(self.forward(spot.block(0, 1, 0), spot.twin))
        self.y.get()
        self.high = self.forward(spot.block(1, 0, 0), spot.across, self.mid, rest)
        self.parts.append(self.forward(spot.block(1, 0, 0), spot.twin))

    def third(self):
        spot, rest = self.spot, self.size - self.mid
        self.low.get()
        self.parts.append(self.forward(spot.block(1, 1, 0), spot.twin, 0, self.mid))
        self.high.get()
        self.parts.append(self.forward(spot.block(1, 1, 0), spot.twin, self.mid, rest))

    def finish(self):
        self.local.wait()
        for part in self.parts:
            part.get()


class GatherWeight:
    def __init__(self, links, spot, halves, whole, sem):
        self.links, self.spot, self.halves, self.whole = links, spot, halves, whole
        self.shard = halves.shape[1]
        at = pl.multiple_of((2 * spot.at + spot.half) * self.shard, self.shard)
        self.place = whole.at[pl.ds(at, self.shard)]
        self.local = pltpu.make_async_copy(halves.at[spot.half], self.place, sem)

    def pair(self, place):
        return self.whole.at[pl.ds(pl.multiple_of(place * 2 * self.shard, 2 * self.shard), 2 * self.shard)]

    def forward(self, place, to, sends=None, gets=None):
        return self.links.copy(self.pair(place), self.pair(place), self.spot.along(to), sends, gets).start()

    def first(self):
        self.local.start()
        self.y = self.links.copy(self.halves.at[1 - self.spot.half], self.place, self.spot.mate).start()

    def second(self):
        at, places = self.spot.at, self.spot.places
        self.local.wait()
        self.y.get()
        if places == 4:
            self.two = self.forward(at, (at + 2) % 4)
            self.parts = [
                self.forward(at, (at + 1) % 4, at < 3, at > 0),
                self.forward(at, (at + 3) % 4, at > 0, at < 3),
            ]
        else:
            self.parts = [self.forward(at, (at + j) % places) for j in range(1, places)]

    def third(self):
        at = self.spot.at
        if self.spot.places == 4:
            self.two.get()
            inner = (at == 1) | (at == 2)
            self.parts.append(self.forward((at + 2) % 4, 3 * (at // 2), inner, ~inner))

    def finish(self):
        for part in self.parts:
            part.get()


def qkv_body(h_ref, w_ref, b_ref, cos_ref, sin_ref, out_ref):
    acc = jnp.dot(h_ref[...], w_ref[...], preferred_element_type=F32) + b_ref[...]
    cosine, sine = cos_ref[...], sin_ref[...]
    for at in range(0, acc.shape[1], 3 * LANES):
        q = turn(acc[:, at : at + LANES], cosine, sine).astype(BF)
        out_ref[:, at : at + LANES] = (q.astype(F32) * HEAD**-0.5).astype(BF)
        k = turn(acc[:, at + LANES : at + 2 * LANES], cosine, sine)
        out_ref[:, at + LANES : at + 2 * LANES] = k.astype(BF)
        out_ref[:, at + 2 * LANES : at + 3 * LANES] = acc[:, at + 2 * LANES : at + 3 * LANES].astype(BF)


def gelu_body(h_ref, w_ref, b_ref, act_ref, slope_ref):
    z = jnp.dot(h_ref[...], w_ref[...], preferred_element_type=F32) + b_ref[...]
    c = math.sqrt(2.0 / math.pi)
    square = z * z
    gate = 0.5 + 0.5 * jnp.tanh(z * (c + (c * 0.044715) * square))
    value = z * gate
    act_ref[...] = value.astype(BF)
    slope_ref[...] = (gate + (value - value * gate) * (2.0 * c + (6.0 * 0.044715 * c) * square)).astype(BF)


def plain_body(h_ref, w_ref, out_ref):
    out_ref[...] = jnp.dot(h_ref[...], w_ref[...], preferred_element_type=F32).astype(BF)


def slope_body(h_ref, w_ref, slope_ref, out_ref):
    acc = jnp.dot(h_ref[...], w_ref[...], preferred_element_type=F32)
    out_ref[...] = (acc * slope_ref[...].astype(F32)).astype(BF)


def by_rows(body, ins, outs, block, first=0, count=None):
    total = outs[0].shape[0]
    count = count or total // block

    def spec(ref):
        width = ref.shape[1]
        if ref.shape[0] == total:
            return pl.BlockSpec((block, width), lambda i: (first + i, 0))
        return pl.BlockSpec(ref.shape, lambda i: (0, 0))

    pltpu.emit_pipeline(
        body, grid=(count,), in_specs=[spec(r) for r in ins], out_specs=[spec(r) for r in outs]
    )(*ins, *outs)


def by_heads(body, wide_ins, ins, aug_ins, outs, rows, g):
    pairs = wide_ins[0].shape[1] // (3 * LANES)

    def spec(ref, kind):
        if kind == 2:
            return pl.BlockSpec((rows, LANES), lambda j: (g, 0))
        width = 3 * LANES if ref.shape[1] == pairs * 3 * LANES else LANES
        return pl.BlockSpec((rows, width), lambda j: (g, j))

    specs = [spec(r, 0) for r in wide_ins] + [spec(r, 2) for r in aug_ins] + [spec(r, 0) for r in ins]
    pltpu.emit_pipeline(
        body, grid=(pairs,), in_specs=specs, out_specs=[spec(r, 0) for r in outs]
    )(*wide_ins, *aug_ins, *ins, *outs)


def front_kernel(ndp, nt, *refs):
    refs = list(refs)
    take = lambda n: [refs.pop(0) for _ in range(n)]
    h_own, gb_own, wq2, w12, wd2, w22, bias_q, bias_1, cosine, sine, aq, ak = take(12)
    h, gb, wq, w1, wd, w2, qkv, o_float, o, lse, act, slope, go, da = take(14)
    dk_s, dv_s, dqt_s, local_sem, send, recv = take(6)
    spot = Spot(ndp, nt)
    links = Links(send, recv)
    group = h.shape[0] // 2
    own = h_own.shape[0]
    greet(spot.partners())

    rows_h = GatherRows(links, spot, h_own, h, local_sem.at[0])
    rows_gb = GatherRows(links, spot, gb_own, gb, local_sem.at[1])
    gather_q = GatherWeight(links, spot, wq2, wq, local_sem.at[2])
    gather_1 = GatherWeight(links, spot, w12, w1, local_sem.at[3])
    gather_d = GatherWeight(links, spot, wd2, wd, local_sem.at[4])
    gather_2 = GatherWeight(links, spot, w22, w2, local_sem.at[5])

    gather_q.first()
    rows_h.first()
    gather_1.first()
    gather_q.second()
    rows_h.second()
    gather_q.third()
    gather_1.second()
    rows_h.third()
    gather_q.finish()
    rows_gb.first()
    gather_d.first()
    gather_2.first()
    rows_h.finish()
    by_rows(qkv_body, [h, wq, bias_q, cosine, sine], [qkv], own)
    attend = functools.partial(attend_kernel, group, 512)
    by_heads(attend, [qkv], [], [aq, ak], [o_float, o, lse], group, 0)
    gather_1.third()
    gather_d.second()
    by_heads(attend, [qkv], [], [aq, ak], [o_float, o, lse], group, 1)
    rows_gb.second()
    gather_2.second()
    gather_1.finish()
    steps = 2 * group // own
    by_rows(gelu_body, [h, w1, bias_1], [act, slope], own, 0, steps // 2)
    rows_gb.third()
    gather_d.third()
    by_rows(gelu_body, [h, w1, bias_1], [act, slope], own, steps // 2, steps // 2)
    rows_gb.finish()
    gather_d.finish()
    by_rows(plain_body, [gb, wd], [go], own)
    back = functools.partial(attend_back_kernel, group, 256)

    def attend_back(qkv_ref, aq_ref, ak_ref, cos_ref, sin_ref, o_ref, lse_ref, go_ref, out_ref):
        back(qkv_ref, aq_ref, ak_ref, o_ref, lse_ref, go_ref, cos_ref, sin_ref, out_ref, dk_s, dv_s, dqt_s)

    by_heads(attend_back, [qkv], [o_float, lse, go], [aq, ak, cosine, sine], [da], group, 0)
    gather_2.third()
    by_heads(attend_back, [qkv], [o_float, lse, go], [aq, ak, cosine, sine], [da], group, 1)
    gather_2.finish()
    links.finish()


def front_call(ndp, nt, h_own, gb_own, weights, biases, tables):
    own, width = h_own.shape
    rows = 2 * nt * own
    q3, f, q = weights[0].shape[2], weights[1].shape[2], weights[2].shape[2]
    shape = lambda a, b, dtype=BF: jax.ShapeDtypeStruct((a, b), dtype)
    out_shape = [shape(rows, width), shape(rows, width)]
    out_shape += [shape(width, n) for n in (q3, f, q, f)]
    out_shape += [shape(rows, q3), shape(rows, q, F32), shape(rows, q), shape(rows, q, F32)]
    out_shape += [shape(rows, f), shape(rows, f), shape(rows, q), shape(rows, q3)]
    anywhere = pl.BlockSpec(memory_space=pl.ANY)
    group = nt * own
    transfers = 2 * 10 + 4 * (1 + max(4, ndp // 2))
    return pl.pallas_call(
        functools.partial(front_kernel, ndp, nt),
        in_specs=[anywhere] * 12,
        out_specs=[anywhere] * 14,
        out_shape=out_shape,
        scratch_shapes=[
            pltpu.VMEM((group, LANES), F32),
            pltpu.VMEM((group, LANES), F32),
            pltpu.VMEM((LANES, group), F32),
            pltpu.SemaphoreType.DMA((6,)),
            pltpu.SemaphoreType.DMA((transfers,)),
            pltpu.SemaphoreType.DMA((transfers,)),
        ],
        compiler_params=pltpu.CompilerParams(collective_id=0, has_side_effects=True, vmem_limit_bytes=VMEM),
    )(h_own, gb_own, *weights, *biases, *tables)


def attend_kernel(rows, block, qkv_ref, aq_ref, ak_ref, *refs):
    o_ref, bf_ref, lse_ref = refs[-3:]
    lane = lanes_of((rows, LANES))
    lane_q = lanes_of((block, LANES))
    one = jnp.where(lane % HEAD < 3, 1.0, 0.0).astype(BF)
    first = lane < HEAD
    keys = [jnp.where(half, qkv_ref[:, LANES : 2 * LANES], ak_ref[...]) for half in (first, ~first)]
    values = [jnp.where(half, qkv_ref[:, 2 * LANES :], one) for half in (first, ~first)]
    causal = lanes_of((block, block)) <= lax.broadcasted_iota(jnp.int32, (block, block), 0)
    for b in range(rows // block):
        here = pl.ds(b * block, block)
        lo, hi = b * block, (b + 1) * block
        outs, sums = [], []
        for side in (0, 1):
            half = (lane_q < HEAD) if side == 0 else (lane_q >= HEAD)
            q = jnp.where(half, qkv_ref[here, :LANES], aq_ref[here])
            s_near = lax.dot_general(q, keys[side][lo:hi], NT, preferred_element_type=F32)
            s_near = jnp.where(causal, s_near, NEG)
            top = jnp.max(s_near, axis=1, keepdims=True)
            if b:
                s_far = lax.dot_general(q, keys[side][:lo], NT, preferred_element_type=F32)
                top = jnp.maximum(top, jnp.max(s_far, axis=1, keepdims=True))
            o = jnp.dot(jnp.exp(s_near - top).astype(BF), values[side][lo:hi], preferred_element_type=F32)
            if b:
                o = o + jnp.dot(
                    jnp.exp(s_far - top).astype(BF), values[side][:lo], preferred_element_type=F32
                )
            at = HEAD if side == 0 else 0
            total = o[:, at : at + 1]
            outs.append(o / total)
            sums.append(top + jnp.log(total))
        out = jnp.where(lane_q < HEAD, outs[0], outs[1])
        o_ref[here] = out
        bf_ref[here] = out.astype(BF)
        lse_ref[here] = jnp.where(lane_q < HEAD, sums[0], sums[1])


def split3(x):
    a = x.astype(BF).astype(F32)
    b = (x - a).astype(BF).astype(F32)
    return a, b, x - a - b


def attend_back_kernel(
    rows, block, qkv_ref, aq_ref, ak_ref, o_ref, lse_ref, go_ref, cos_ref, sin_ref, *refs
):
    out_ref, dk_s, dv_s, dqt_s = refs
    lane = lanes_of((rows, LANES))
    lane_k = lanes_of((block, LANES))
    one = jnp.where(lane % HEAD < 3, 1.0, 0.0).astype(BF)
    causal = lax.broadcasted_iota(jnp.int32, (block, block), 0) <= lanes_of((block, block))
    prod = o_ref[...] * go_ref[...].astype(F32)
    dq_first = None
    for side in (0, 1):
        half = (lane < HEAD) if side == 0 else (lane >= HEAD)
        delta = -jnp.sum(jnp.where(half, prod, 0.0), axis=1, keepdims=True)
        at = 0 if side == 0 else HEAD
        lse = -lse_ref[:, at : at + 1]
        q = jnp.where(half, qkv_ref[:, :LANES], aq_ref[...]).astype(F32)
        g = jnp.where(half, go_ref[...].astype(F32), 0.0)
        base = HEAD - at
        for i, (a, d) in enumerate(zip(split3(lse), split3(delta))):
            q = jnp.where(lane == base + 8 + i, a, q)
            g = jnp.where(lane == base + i, d, g)
        q, g = q.astype(BF), g.astype(BF)
        k = jnp.where(half, qkv_ref[:, LANES : 2 * LANES], ak_ref[...])
        v = jnp.where(half, qkv_ref[:, 2 * LANES :], one)
        kt = k.T
        for b in range(rows // block):
            lo, hi = b * block, (b + 1) * block
            here = pl.ds(lo, block)
            st = lax.dot_general(k[lo:hi], q[lo:], NT, preferred_element_type=F32)
            dpt = lax.dot_general(v[lo:hi], g[lo:], NT, preferred_element_type=F32)
            p = jnp.exp(st)
            near = jnp.where(causal, p[:, :block], 0.0)
            p = jnp.concatenate([near, p[:, block:]], axis=1) if hi < rows else near
            ds = (p * dpt).astype(BF)
            dv = jnp.dot(p.astype(BF), g[lo:], preferred_element_type=F32)
            dk = jnp.dot(ds, q[lo:], preferred_element_type=F32)
            dq = jnp.dot(kt[:, lo:hi], ds, preferred_element_type=F32)
            if side == 0:
                dk_s[here] = dk
                dv_s[here] = dv
            else:
                dk = jnp.where(lane_k < HEAD, dk_s[here], dk)
                dv = jnp.where(lane_k < HEAD, dv_s[here], dv)
                out_ref[here, LANES : 2 * LANES] = turn(dk, cos_ref[here], -sin_ref[here]).astype(BF)
                out_ref[here, 2 * LANES :] = dv.astype(BF)
            if b == 0:
                dqt_s[...] = dq
            else:
                dqt_s[:, lo:] += dq
        d = dqt_s[...].T * HEAD**-0.5
        if side == 0:
            dq_first = d
        else:
            d = jnp.where(lane < HEAD, dq_first, d)
            out_ref[:, :LANES] = turn(d, cos_ref[...], -sin_ref[...]).astype(BF)


def outer_products(left, rights, parts, acc, spot, block, sums=None):
    places = spot.places
    rows, size = left.shape[0], left.shape[1] // places
    steps = rows // block
    columns = parts.shape[2]

    def body(step, left_ref, *refs):
        right_refs, out = refs[:-1], refs[-1]
        r, j = step.index
        first = 0
        for right_ref in right_refs:
            there = slice(first, first + right_ref.shape[1])
            first += right_ref.shape[1]
            term = lax.dot_general(left_ref[...], right_ref[...], TN, preferred_element_type=F32)

            @pl.when(r == 0)
            def _():
                acc[j, :, there] = term

            @pl.when((r > 0) & (r < steps - 1))
            def _():
                acc[j, :, there] += term

            @pl.when(r == steps - 1)
            def _():
                out[:, there] = (acc[j, :, there] + term).astype(BF)

            if sums is not None:
                @pl.when(j == 0)
                def _():
                    sums[...] += jnp.sum(right_ref[...].astype(F32), axis=0, keepdims=True)

    pltpu.emit_pipeline(
        body,
        grid=(steps, places),
        in_specs=[pl.BlockSpec((block, size), lambda r, j: (r, lax.rem(spot.at + j, places)))]
        + [pl.BlockSpec((block, x.shape[1]), lambda r, j: (r, 0)) for x in rights],
        out_specs=[pl.BlockSpec((None, size, columns), lambda r, j: (jnp.where(r == steps - 1, j, 0), 0, 0))],
        _explicit_indices=True,
    )(left, *rights, parts)


class ReduceWeight:
    def __init__(self, links, spot, parts, slots, end, joined, mine, given, theirs):
        self.links, self.spot = links, spot
        self.parts, self.slots, self.end, self.joined = parts, slots, end, joined
        self.mine, self.given, self.theirs = mine, given, theirs
        self.shard = mine.shape[0]

    def send(self, src, dst, to, sends=None, gets=None):
        return self.links.copy(src, dst, self.spot.along(to), sends, gets).start()

    def first(self):
        at = self.spot.at
        if self.spot.places == 4:
            self.edges = [
                self.send(self.parts.at[3], self.end, 1, at == 0, at == 1),
                self.send(self.parts.at[1], self.end, 2, at == 3, at == 2),
            ]

    def second(self):
        at, places, parts, slots = self.spot.at, self.spot.places, self.parts, self.slots
        if places == 4:
            inner = (at == 1) | (at == 2)
            self.got = [
                self.send(parts.at[1], slots.at[0], (at + 1) % 4, at < 3, at > 0),
                self.send(parts.at[3], slots.at[1], (at + 3) % 4, at > 0, at < 3),
                self.send(parts.at[2], slots.at[2], (at + 2) % 4, ~inner, inner),
            ]
        else:
            self.got = [self.send(parts.at[j], slots.at[j - 1], (at + j) % places) for j in range(1, places)]

    def third(self):
        if self.spot.places != 4:
            return
        at = self.spot.at
        inner = (at == 1) | (at == 2)
        for edge in self.edges:
            edge.get()
        size, columns = self.parts.shape[1:]

        def body(a, b, out):
            out[...] = (a[...].astype(F32) + b[...].astype(F32)).astype(BF)

        @pl.when(inner)
        def _():
            spec = pl.BlockSpec((self.shard, columns), lambda i: (i, 0))
            pltpu.emit_pipeline(
                body,
                grid=(size // self.shard,),
                in_specs=[pl.BlockSpec((None, self.shard, columns), lambda i: (2, i, 0)), spec],
                out_specs=[spec],
            )(self.parts, self.end, self.joined)

        self.got.append(self.send(self.joined, self.slots.at[2], (at + 2) % 4, inner, ~inner))

    def fourth(self):
        spot = self.spot
        at, places = spot.at, spot.places
        for sent in self.got:
            sent.get()
        columns = self.parts.shape[2]

        def body(own, *refs):
            out = refs[-1]
            total = own[...].astype(F32)
            for k, ref in enumerate(refs[:-1]):
                term = ref[...].astype(F32)
                if places == 4 and k < 2:
                    term = term * jnp.where(at > 0 if k == 0 else at < 3, 1.0, 0.0)
                total = total + term
            out[...] = total.astype(out.dtype)

        def slot(k, part):
            if places == 4 and k < 2:
                k = jnp.where(at > 0, 0, 2) if k == 0 else jnp.where(at < 3, 1, 2)
            return pl.BlockSpec((None, self.shard, columns), lambda i: (k, part, 0))

        for part, out in ((1 - spot.half, self.given), (spot.half, self.mine)):
            own = pl.BlockSpec((None, self.shard, columns), lambda i, part=part: (0, part, 0))
            pltpu.emit_pipeline(
                body,
                grid=(1,),
                in_specs=[own] + [slot(k, part) for k in range(places - 1)],
                out_specs=[pl.BlockSpec((self.shard, columns), lambda i: (0, 0))],
            )(self.parts, *[self.slots] * (places - 1), out)
            if out is self.given:
                self.mate = self.links.copy(self.given, self.theirs, spot.mate).start()

    def finish(self):
        self.mate.get()


class ReduceRows:
    def __init__(self, links, spot, factors, buffers, own):
        self.links, self.spot, self.factors, self.own = links, spot, factors, own
        self.given, self.got = buffers[:3], buffers[3:]
        self.columns = factors[0][1].shape[0] // 2
        self.sent = [[None, None] for _ in range(3)]

    def block(self, part, n, twins):
        spot = self.spot
        g_own, x_own = (n // 2, n % 2) if part == 0 else (n % 2, n // 2)
        other, x1 = 1 - spot.half, 1 - spot.chip
        g = other + g_own * (spot.half - other)
        x = x1 + x_own * (spot.chip - x1)
        c = 1 - spot.core if twins else spot.core
        return g * spot.nt + 2 * x + c

    def added(self, stage):
        return [((), (0,), (2, 0), (3, 1, 0))[stage][k] for k in range(stage)]

    def run(self, stage, part, cut):
        first, last = ((0, 4), (0, 2), (2, 3))[stage]
        own, columns = self.own, self.columns
        rows = own // cut
        n_factors = len(self.factors)
        for earlier in range(stage):
            self.wait(earlier, part, stage)

        def body(*refs):
            ins, out = refs[:-1], refs[-1]
            total = None
            for k in range(n_factors):
                term = lax.dot_general(ins[2 * k][...], ins[2 * k + 1][...], NT, preferred_element_type=F32)
                total = term if total is None else total + term
            for ref in ins[2 * n_factors :]:
                total = total + ref[...].astype(F32)
            out[...] = total.astype(BF)

        in_specs, args = [], []
        for a, b in self.factors:
            depth = a.shape[1]
            in_specs.append(
                pl.BlockSpec(
                    (rows, depth), lambda i: (self.block(part, first + i // cut, stage == 0) * cut + i % cut, 0)
                )
            )
            in_specs.append(pl.BlockSpec((columns, depth), lambda i: (part, 0)))
            args += [a, b]
        for k, offset in enumerate(self.added(stage)):
            in_specs.append(
                pl.BlockSpec((None, rows, columns), lambda i, offset=offset: (part, offset * cut + i, 0))
            )
            args.append(self.got[k])
        pltpu.emit_pipeline(
            body,
            grid=((last - first) * cut,),
            in_specs=in_specs,
            out_specs=[pl.BlockSpec((None, rows, columns), lambda i: (part, i, 0))],
        )(*args, self.given[stage])
        axes = (self.spot.mate, self.spot.across) if part == 0 else (self.spot.across, self.spot.mate)
        device = self.spot.twin if stage == 0 else axes[stage - 1]
        pieces = ((0, 2), (2, 1), (3, 1)) if stage == 0 else ((0, 1), (1, 1)) if stage == 1 else ((0, 1),)
        sent = []
        for at, count in pieces:
            there = pl.ds(at * own, count * own)
            sent.append(
                self.links.copy(self.given[stage].at[part, there], self.got[stage].at[part, there], device).start()
            )
        self.sent[stage][part] = sent

    def wait(self, earlier, part, stage):
        self.sent[earlier][part][stage - earlier - 1].get()

    def last(self, epilogue, ins, outs, cut):
        own, columns = self.own, self.columns
        rows = own // cut
        n_factors = len(self.factors)
        for part in (0, 1):
            for earlier in range(3):
                self.wait(earlier, part, 3)

        def body(*refs):
            mine, rest = refs[: 2 * n_factors], refs[2 * n_factors :]
            total = None
            for k in range(n_factors):
                term = lax.dot_general(mine[2 * k][...], mine[2 * k + 1][...], NT, preferred_element_type=F32)
                total = term if total is None else total + term
            extra = []
            for part in (0, 1):
                terms = [ref[...].astype(F32) for ref in rest[3 * part : 3 * part + 3]]
                extra.append(terms[0] + terms[1] + terms[2])
            total = total + jnp.concatenate(extra, axis=1)
            epilogue(total, rest[6 : 6 + len(ins)], rest[6 + len(ins) :])

        in_specs, args = [], []
        for a, b in self.factors:
            depth = a.shape[1]
            in_specs.append(pl.BlockSpec((rows, depth), lambda i: (self.block(0, 3, False) * cut + i, 0)))
            in_specs.append(pl.BlockSpec((2 * columns, depth), lambda i: (0, 0)))
            args += [a, b]
        for part in (0, 1):
            for k, offset in enumerate(self.added(3)):
                in_specs.append(
                    pl.BlockSpec(
                        (None, rows, columns), lambda i, part=part, offset=offset: (part, offset * cut + i, 0)
                    )
                )
                args.append(self.got[k])

        def spec(ref):
            if ref.shape[0] == 1:
                return pl.BlockSpec(ref.shape, lambda i: (0, 0))
            return pl.BlockSpec((rows, ref.shape[1]), lambda i: (i, 0))

        pltpu.emit_pipeline(
            body, grid=(cut,), in_specs=in_specs + [spec(r) for r in ins], out_specs=[spec(r) for r in outs]
        )(*args, *ins, *outs)


def output_rows(total, ins, outs):
    x_ref, bias_ref = ins
    outs[0][...] = (x_ref[...].astype(F32) + total + bias_ref[...]).astype(BF)


def norm_rows(sums, total, ins, outs):
    x_ref, g_ref, gain_ref = ins
    x = x_ref[...].astype(F32)
    gy = g_ref[...].astype(F32)
    centred = x - jnp.mean(x, axis=1, keepdims=True)
    rstd = lax.rsqrt(jnp.mean(centred * centred, axis=1, keepdims=True) + EPS)
    x_hat = centred * rstd
    scaled = total * gain_ref[...]
    m1 = jnp.mean(scaled, axis=1, keepdims=True)
    m2 = jnp.mean(scaled * x_hat, axis=1, keepdims=True)
    outs[0][...] = rstd * (scaled - m1 - x_hat * m2) + gy
    sums[0:1, :] += jnp.sum(total * x_hat, axis=0, keepdims=True)
    sums[1:2, :] += jnp.sum(total, axis=0, keepdims=True)
    sums[2:3, :] += jnp.sum(gy, axis=0, keepdims=True)


SUMMED = 8


def back_kernel(ndp, nt, *refs):
    refs = list(refs)
    take = lambda n: [refs.pop(0) for _ in range(n)]
    h, gb, act, slope, o, da, wq, wd, w1, w2, x_own, g_own, gain, bias = take(14)
    output, grad_x, small, gz = take(4)
    weights = [take(7) for _ in range(3)]
    row_buffers = [take(6) for _ in range(2)]
    acc, sums, biases, line_got, pair_got, send, recv = take(7)
    spot = Spot(ndp, nt)
    links = Links(send, recv)
    own = x_own.shape[0]
    greet(spot.partners())
    sums[...] = jnp.zeros(sums.shape, F32)
    biases[...] = jnp.zeros(biases.shape, F32)

    q_columns, f_columns = da.shape[1], act.shape[1]
    reduce_2, reduce_q, reduce_1 = [
        ReduceWeight(links, spot, parts, slots, end, joined, mine, given, theirs)
        for mine, theirs, given, parts, slots, end, joined in weights
    ]
    branch = ReduceRows(links, spot, [(act, w2), (o, wd)], row_buffers[0], own)
    grad = ReduceRows(links, spot, [(gz, w1), (da, wq)], row_buffers[1], own)

    def outer(left, rights, target, columns, total=None):
        outer_products(left, rights, target.parts, acc.at[:, :, pl.ds(0, columns)], spot, left.shape[0] // 2, total)

    outer(h, [da], reduce_q, q_columns, biases.at[1:2, pl.ds(0, q_columns)])
    reduce_q.first()
    branch.run(0, 0, 1)
    branch.run(0, 1, 1)
    reduce_q.second()
    branch.run(1, 0, 1)
    branch.run(1, 1, 1)
    reduce_q.third()
    outer(gb, [act, o], reduce_2, f_columns + o.shape[1])
    reduce_2.first()
    by_rows(slope_body, [gb, w2, slope], [gz], own)
    reduce_2.second()
    grad.run(0, 0, 1)
    grad.run(0, 1, 1)
    branch.run(2, 0, 2)
    branch.run(2, 1, 2)
    reduce_2.third()
    grad.run(1, 0, 1)
    grad.run(1, 1, 1)
    outer(h, [gz], reduce_1, f_columns, biases.at[0:1, pl.ds(0, f_columns)])
    reduce_1.first()
    reduce_q.fourth()
    reduce_1.second()
    branch.last(output_rows, [x_own, bias], [output], 2)
    grad.run(2, 0, 2)
    grad.run(2, 1, 2)
    reduce_1.third()
    reduce_2.fourth()
    reduce_q.finish()
    grad.last(functools.partial(norm_rows, sums), [x_own, g_own, gain], [grad_x], 2)
    reduce_1.fourth()

    sums[SUMMED // 2 : SUMMED // 2 + 2, :] = biases[...]
    places = spot.places
    line_got[0] = sums[...]
    got = [links.copy(sums, line_got.at[j], spot.along((spot.at + j) % places)).start() for j in range(1, places)]
    for sent in got:
        sent.get()
    for sent in got:
        sent.drain()
    total = line_got[spot.at]
    for place in range(1, places):
        total = total + line_got[(spot.at + places - place) % places]
    sums[...] = total
    row = lax.broadcasted_iota(jnp.int32, sums.shape, 0)
    for k, device in enumerate((spot.mate, spot.across, spot.twin)):
        sent = links.copy(sums, pair_got.at[k], device).start()
        sent.get()
        sent.drain()
        theirs = pair_got[k]
        if k == 0:
            small[1] = theirs
        sums[...] = sums[...] + jnp.where(row < SUMMED // 2, theirs, 0.0)
    small[0] = sums[...]
    reduce_2.finish()
    reduce_1.finish()
    links.finish()


def back_call(ndp, nt, h, gb, act, slope, o, da, wq, wd, w1, w2, x_own, g_own, gain, bias):
    own, width = x_own.shape
    rows = h.shape[0]
    places = ndp // 2
    size, shard = width // places, width // ndp
    q3, f, q = wq.shape[1], w1.shape[1], wd.shape[1]
    shape = lambda *s: jax.ShapeDtypeStruct(s, BF)
    full = lambda *s: jax.ShapeDtypeStruct(s, F32)
    out_shape = [shape(own, width), full(own, width), full(2, SUMMED, width), shape(rows, f)]
    for n in (f + q, q3, f):
        out_shape += [full(shard, n), shape(shard, n), shape(shard, n)]
        out_shape += [shape(places, size, n), shape(places - 1, size, n), shape(size, n), shape(size, n)]
    for _ in range(2):
        out_shape += [shape(2, k * own, width // 2) for k in (4, 2, 1)] * 2
    anywhere = pl.BlockSpec(memory_space=pl.ANY)
    out_specs = [anywhere] * len(out_shape)
    out_specs[2] = pl.BlockSpec(memory_space=pltpu.VMEM)
    transfers = 3 * (1 + max(6, places)) + 2 * 2 * 6 + places + 3
    return pl.pallas_call(
        functools.partial(back_kernel, ndp, nt),
        in_specs=[anywhere] * 14,
        out_specs=out_specs,
        out_shape=out_shape,
        scratch_shapes=[
            pltpu.VMEM((places, size, f + q), F32),
            pltpu.VMEM((SUMMED, width), F32),
            pltpu.VMEM((2, width), F32),
            pltpu.VMEM((places, SUMMED, width), F32),
            pltpu.VMEM((3, SUMMED, width), F32),
            pltpu.SemaphoreType.DMA((transfers,)),
            pltpu.SemaphoreType.DMA((transfers,)),
        ],
        compiler_params=pltpu.CompilerParams(collective_id=1, has_side_effects=True, vmem_limit_bytes=VMEM),
    )(h, gb, act, slope, o, da, wq, wd, w1, w2, x_own, g_own, gain, bias)


def local(
    layer_input,
    seq_lens,
    ln_gain,
    ln_bias,
    w_qkv,
    b_qkv,
    w_dense,
    b_dense,
    w_fc1,
    b_fc1,
    w_fc2,
    b_fc2,
    cotangent,
):
    own, width = layer_input.shape
    ndp, nt = lax.axis_size("dp"), lax.axis_size("tensor")
    dp, t = lax.axis_index("dp"), lax.axis_index("tensor")
    half, at, places = dp % 2, dp // 2, ndp // 2
    chip, core = t // 2, t % 2
    group = own * nt
    shard = w_qkv.shape[0]
    q_width = w_qkv.shape[2] // 2
    f_width = w_fc1.shape[1] // 2
    pairs = q_width // LANES
    other = 1 - half

    wq = w_qkv.reshape(shard, 3, 2, pairs, LANES).transpose(2, 0, 3, 1, 4).reshape(2, shard, 3 * q_width)
    wd = w_dense.T.reshape(shard, 2, q_width).transpose(1, 0, 2)
    w1 = w_fc1.reshape(shard, 2, f_width).transpose(1, 0, 2)
    w2 = w_fc2.T.reshape(shard, 2, f_width).transpose(1, 0, 2)

    xf = layer_input.astype(F32)
    mean = jnp.mean(xf, axis=1, keepdims=True)
    centred = xf - mean
    rstd = lax.rsqrt(jnp.mean(centred * centred, axis=1, keepdims=True) + EPS)
    x_hat = centred * rstd
    h_own = (x_hat * ln_gain + ln_bias).astype(BF)
    used = jnp.sum(seq_lens[0])
    valid = (t * own + jnp.arange(own, dtype=jnp.int32) < used).astype(F32)[:, None]
    gy = cotangent.astype(F32) * valid
    gb_own = gy.astype(BF)

    lens_of_mate = swap(seq_lens, "dp", 1)

    lens = jnp.zeros((2, seq_lens.shape[1]), jnp.int32)
    lens = place(place(lens, seq_lens[0], half), lens_of_mate[0], other)
    ends = jnp.cumsum(lens, axis=1)
    rows = jnp.arange(group, dtype=jnp.int32)
    segment = jnp.sum((rows[None, :, None] >= ends[:, None, :]).astype(jnp.int32), axis=2)
    begins = jnp.concatenate([ends - lens, ends[:, -1:]], axis=1)
    labels = jnp.arange(begins.shape[1], dtype=jnp.int32)
    mine = segment[:, :, None] == labels
    position = rows[None] - jnp.sum(jnp.where(mine, begins[:, None, :], 0), axis=2)
    steps = jnp.arange(ROT // 2, dtype=F32)
    inverse = jnp.exp(-math.log(10000.0) * 2.0 * steps / ROT)
    angle = inverse[:, None] * position.reshape(1, 2 * group).astype(F32)
    cos16, sin16 = jnp.cos(angle).T, jnp.sin(angle).T
    still = jnp.zeros((2 * group, HEAD - ROT), F32)
    cosine = jnp.concatenate([cos16, cos16, still + 1.0] * 2, axis=1)
    sine = jnp.concatenate([-sin16, sin16, still] * 2, axis=1)
    lane = jnp.arange(LANES, dtype=jnp.int32) % HEAD
    same = segment.reshape(2 * group, 1) == lane[None, :]
    count = begins.shape[1]
    aq = jnp.where(same & (lane < count), NEG, 0.0).astype(BF)
    ak = jnp.where(~same & (lane < count) | (lane >= 8) & (lane < 11), 1.0, 0.0).astype(BF)

    bias_q = pick(b_qkv.reshape(3, 2, pairs, LANES).transpose(1, 2, 0, 3), half).reshape(1, 3 * q_width)
    bias_1 = pick(b_fc1.reshape(2, f_width), half)[None]

    h, gb, wq_all, w1_all, wd_all, w2_all, qkv, o_float, o, lse, act, slope, go, da = front_call(
        ndp, nt, h_own, gb_own, [wq, w1, wd, w2], [bias_q, bias_1], [cosine, sine, aq, ak]
    )
    made = back_call(
        ndp, nt, h, gb, act, slope, o, da, wq_all, wd_all, w1_all, w2_all, layer_input, gb_own, ln_gain[None],
        (b_dense + b_fc2)[None],
    )
    output, grad_x, small = made[:3]

    def both(mine, theirs):
        theirs = theirs.astype(F32)
        return jnp.stack([jnp.where(half == 0, mine, theirs), jnp.where(half == 0, theirs, mine)])

    g_2, g_wq, g_w1 = [both(made[k], made[k + 1]) for k in (4, 11, 18)]
    g_w2, g_wd = g_2[:, :, :f_width], g_2[:, :, f_width:]
    late, early = small[0, :2], small[0, 2]
    g_biases = both(small[0, SUMMED // 2 : SUMMED // 2 + 2], small[1, SUMMED // 2 : SUMMED // 2 + 2])
    g_b1 = g_biases[:, 0, :f_width].reshape(-1)
    g_bq = g_biases[:, 1, : 3 * q_width].reshape(2, pairs, 3, LANES).transpose(2, 0, 1, 3).reshape(3, 2 * q_width)
    out_wq = g_wq.reshape(2, shard, pairs, 3, LANES).transpose(1, 3, 0, 2, 4).reshape(shard, 3, 2 * q_width)
    out_wd = g_wd.transpose(0, 2, 1).reshape(2 * q_width, shard)
    out_w1 = g_w1.transpose(1, 0, 2).reshape(shard, 2 * f_width)
    out_w2 = g_w2.transpose(0, 2, 1).reshape(2 * f_width, shard)
    return (
        output,
        grad_x,
        late[0],
        late[1],
        out_wq,
        g_bq,
        out_wd,
        early,
        out_w1,
        g_b1,
        out_w2,
        early,
    )


def solution(mesh):
    rows = P(("dp", "tensor"), None)
    in_specs = (
        rows,
        P("dp", None),
        P(),
        P(),
        P("dp", None, "tensor"),
        P(None, "tensor"),
        P("tensor", "dp"),
        P(),
        P("dp", "tensor"),
        P("tensor"),
        P("tensor", "dp"),
        P(),
        rows,
    )
    out_specs = (
        rows,
        rows,
        P(),
        P(),
        P("dp", None, "tensor"),
        P(None, "tensor"),
        P("tensor", "dp"),
        P(),
        P("dp", "tensor"),
        P("tensor"),
        P("tensor", "dp"),
        P(),
    )
    return jax.shard_map(local, mesh=mesh, in_specs=in_specs, out_specs=out_specs, check_vma=False)
```

```python
import functools
import math

import jax
import jax.numpy as jnp
from jax import lax
from jax.experimental import pallas as pl
from jax.experimental.pallas import tpu as pltpu
from jax.sharding import PartitionSpec as P

HEAD = 64
ROT = 32
EPS = 1e-05
NEG = -1e30
LANES = 128
BF = jnp.bfloat16
F32 = jnp.float32
NT = (((1,), (1,)), ((), ()))
TN = (((0,), (0,)), ((), ()))
VMEM = 56 * 2**20
COST = pl.CostEstimate(flops=0, bytes_accessed=0, transcendentals=0)


def pick(x, index):
    return lax.dynamic_index_in_dim(x, index, 0, keepdims=False)


def place(buffer, block, *index):
    return lax.dynamic_update_slice(
        buffer, block.reshape((1,) * len(index) + block.shape), tuple(index) + (0,) * block.ndim
    )


def lanes_of(shape):
    return lax.broadcasted_iota(jnp.int32, shape, 1)


def turn(x, cosine, sine):
    lane = lanes_of(x.shape) % HEAD
    other = jnp.where(lane < ROT // 2, pltpu.roll(x, LANES - ROT // 2, 1), pltpu.roll(x, ROT // 2, 1))
    return x * cosine + other * sine


def qkv_rows(acc, extras, outs):
    bias, cosine, sine = (ref[...] for ref in extras)
    acc = acc + bias
    out_ref = outs[0]
    for at in range(0, acc.shape[1], 3 * LANES):
        q = turn(acc[:, at : at + LANES], cosine, sine).astype(BF)
        out_ref[:, at : at + LANES] = (q.astype(F32) * HEAD**-0.5).astype(BF)
        k = turn(acc[:, at + LANES : at + 2 * LANES], cosine, sine)
        out_ref[:, at + LANES : at + 2 * LANES] = k.astype(BF)
        out_ref[:, at + 2 * LANES : at + 3 * LANES] = acc[:, at + 2 * LANES : at + 3 * LANES].astype(BF)


def plain_rows(acc, extras, outs):
    outs[0][...] = acc.astype(BF)


def gelu_rows(acc, extras, outs):
    z = acc + extras[0][...]
    c = math.sqrt(2.0 / math.pi)
    square = z * z
    gate = 0.5 + 0.5 * jnp.tanh(z * (c + (c * 0.044715) * square))
    value = z * gate
    outs[0][...] = value.astype(BF)
    outs[1][...] = (gate + (value - value * gate) * (2.0 * c + (6.0 * 0.044715 * c) * square)).astype(BF)


def slope_rows(acc, extras, outs):
    outs[0][...] = (acc * extras[0][...].astype(F32)).astype(BF)


class Links:
    def __init__(self, send, recv):
        self.send, self.recv, self.count, self.pending = send, recv, 0, []

    def copy(self, src, dst, device, sends=None, gets=None):
        n = self.count
        self.count += 1
        made = pltpu.make_async_remote_copy(
            src_ref=src,
            dst_ref=dst,
            send_sem=self.send.at[n],
            recv_sem=self.recv.at[n],
            device_id=device,
            device_id_type=pl.DeviceIdType.MESH,
        )
        return Sent(self, made, sends, gets)

    def finish(self):
        for sent in self.pending:
            sent.when(sent.sends, sent.made.wait_send)


class Sent:
    def __init__(self, links, made, sends, gets):
        self.links, self.made, self.sends, self.gets = links, made, sends, gets

    def when(self, condition, action):
        if condition is None:
            action()
        else:
            pl.when(condition)(action)

    def start(self):
        self.when(self.sends, self.made.start)
        self.links.pending.append(self)
        return self

    def get(self):
        self.when(self.gets, self.made.wait_recv)

    def drain(self):
        self.links.pending.remove(self)
        self.when(self.sends, self.made.wait_send)


def greet(devices):
    barrier = pltpu.get_barrier_semaphore()
    for device in devices:
        pl.semaphore_signal(barrier, inc=1, device_id=device, device_id_type=pl.DeviceIdType.MESH)
    pl.semaphore_wait(barrier, len(devices))


class Spot:
    def __init__(self, ndp, nt):
        self.dp, self.t = lax.axis_index("dp"), lax.axis_index("tensor")
        self.half, self.at = self.dp % 2, self.dp // 2
        self.chip, self.core = self.t // 2, self.t % 2
        self.places, self.nt = ndp // 2, nt
        self.mate = (self.dp + 1 - 2 * self.half, self.t)
        self.across = (self.dp, self.t + 2 - 4 * self.chip)
        self.twin = (self.dp, self.t + 1 - 2 * self.core)

    def along(self, place):
        return (2 * place + self.half, self.t)

    def partners(self):
        line = [self.along((self.at + j) % self.places) for j in range(1, self.places)]
        return [self.mate, self.across, self.twin] + line

    def block(self, mates, acrosses, twins):
        g = self.half if not mates else 1 - self.half
        x = self.chip if not acrosses else 1 - self.chip
        c = self.core if not twins else 1 - self.core
        return g * self.nt + 2 * x + c


class GatherRows:
    def __init__(self, links, spot, whole, size):
        self.whole, self.size = whole, size
        low = size // 4
        near, across, mate, far = [spot.block(g, x, 0) for g, x in ((0, 0), (0, 1), (1, 0), (1, 1))]
        made = lambda block, device, first=0, count=size: links.copy(
            self.rows(block, first, count), self.rows(block, first, count), device
        )
        self.x, self.y = made(near, spot.across), made(near, spot.mate)
        self.low = made(across, spot.mate, 0, low)
        self.high = made(mate, spot.across, low, size - low)
        self.near_twin, self.x_twin, self.y_twin = [made(n, spot.twin) for n in (near, across, mate)]
        self.low_twin = made(far, spot.twin, 0, low)
        self.high_twin = made(far, spot.twin, low, size - low)

    def rows(self, block, first, count):
        return self.whole.at[pl.ds(pl.multiple_of(block * self.size, self.size) + first, count)]

    def first(self):
        self.x.start()
        self.y.start()
        self.near_twin.start()

    def second(self):
        self.x.get()
        self.low.start()
        self.x_twin.start()
        self.y.get()
        self.high.start()
        self.y_twin.start()

    def third(self):
        self.low.get()
        self.low_twin.start()
        self.high.get()
        self.high_twin.start()

    def finish_near(self):
        self.near_twin.get()
        self.x_twin.get()

    def finish(self):
        for part in (self.y_twin, self.low_twin, self.high_twin):
            part.get()


class GatherWeight:
    def __init__(self, links, spot, own, whole, sem):
        self.spot, self.whole = spot, whole
        self.shard, columns = own.shape[0], whole.shape[1]
        at, places = spot.at, spot.places
        half = lambda k: own.at[:, pl.ds(pl.multiple_of(k * columns, columns), columns)]
        place = whole.at[pl.ds(pl.multiple_of((2 * at + spot.half) * self.shard, self.shard), self.shard)]
        self.local = pltpu.make_async_copy(half(spot.half), place, sem)
        self.y = links.copy(half(1 - spot.half), place, spot.mate)
        made = lambda n, to, sends=None, gets=None: links.copy(
            self.pair(n), self.pair(n), spot.along(to), sends, gets
        )
        if places == 4:
            inner = (at == 1) | (at == 2)
            self.two = made(at, (at + 2) % 4)
            self.parts = [made(at, (at + 1) % 4, at < 3, at > 0), made(at, (at + 3) % 4, at > 0, at < 3)]
            self.three = made((at + 2) % 4, 3 * (at // 2), inner, ~inner)
        else:
            self.parts = [made(at, (at + j) % places) for j in range(1, places)]

    def pair(self, place):
        rows = 2 * self.shard
        return self.whole.at[pl.ds(pl.multiple_of(place * rows, rows), rows)]

    def first(self):
        self.local.start()
        self.y.start()

    def second(self):
        self.local.wait()
        self.y.get()
        if self.spot.places == 4:
            self.two.start()
        for part in self.parts:
            part.start()

    def third(self):
        if self.spot.places == 4:
            self.two.get()
            self.three.start()

    def finish(self):
        for part in self.parts:
            part.get()
        if self.spot.places == 4:
            self.three.get()


def qkv_body(h_ref, w_ref, b_ref, cos_ref, sin_ref, out_ref):
    acc = jnp.dot(h_ref[...], w_ref[...], preferred_element_type=F32) + b_ref[...]
    cosine, sine = cos_ref[...], sin_ref[...]
    for at in range(0, acc.shape[1], 3 * LANES):
        q = turn(acc[:, at : at + LANES], cosine, sine).astype(BF)
        out_ref[:, at : at + LANES] = (q.astype(F32) * HEAD**-0.5).astype(BF)
        k = turn(acc[:, at + LANES : at + 2 * LANES], cosine, sine)
        out_ref[:, at + LANES : at + 2 * LANES] = k.astype(BF)
        out_ref[:, at + 2 * LANES : at + 3 * LANES] = acc[:, at + 2 * LANES : at + 3 * LANES].astype(BF)


def gelu_body(h_ref, w_ref, b_ref, act_ref, slope_ref):
    z = jnp.dot(h_ref[...], w_ref[...], preferred_element_type=F32) + b_ref[...]
    c = math.sqrt(2.0 / math.pi)
    square = z * z
    gate = 0.5 + 0.5 * jnp.tanh(z * (c + (c * 0.044715) * square))
    value = z * gate
    act_ref[...] = value.astype(BF)
    slope_ref[...] = (gate + (value - value * gate) * (2.0 * c + (6.0 * 0.044715 * c) * square)).astype(BF)


def plain_body(h_ref, w_ref, out_ref):
    out_ref[...] = jnp.dot(h_ref[...], w_ref[...], preferred_element_type=F32).astype(BF)


def slope_body(h_ref, w_ref, slope_ref, out_ref):
    acc = jnp.dot(h_ref[...], w_ref[...], preferred_element_type=F32)
    out_ref[...] = (acc * slope_ref[...].astype(F32)).astype(BF)


def by_rows(body, ins, outs, block, first=0, count=None, events=None):
    total = outs[0].shape[0]
    count = count or total // block

    def spec(ref):
        width = ref.shape[1]
        if ref.shape[0] == total:
            return pl.BlockSpec((block, width), lambda i: (first + i, 0))
        return pl.BlockSpec(ref.shape, lambda i: (0, 0))

    def stepped(step, *refs):
        for k, event in (events or {}).items():
            pl.when(step.index[0] == k)(event)
        body(*refs)

    pltpu.emit_pipeline(
        stepped,
        grid=(count,),
        in_specs=[spec(r) for r in ins],
        out_specs=[spec(r) for r in outs],
        _explicit_indices=True,
    )(*ins, *outs)


def by_heads(body, wide_ins, ins, aug_ins, outs, rows, g):
    pairs = wide_ins[0].shape[1] // (3 * LANES)

    def spec(ref, kind):
        if kind == 2:
            return pl.BlockSpec((rows, LANES), lambda j: (g, 0))
        width = 3 * LANES if ref.shape[1] == pairs * 3 * LANES else LANES
        return pl.BlockSpec((rows, width), lambda j: (g, j))

    specs = [spec(r, 0) for r in wide_ins] + [spec(r, 2) for r in aug_ins] + [spec(r, 0) for r in ins]
    pltpu.emit_pipeline(
        body, grid=(pairs,), in_specs=specs, out_specs=[spec(r, 0) for r in outs]
    )(*wide_ins, *aug_ins, *ins, *outs)


def norm_inputs(spot, x_own, g_own, gain, shift, lens, h, gb, cut):
    own = x_own.shape[0]
    rows = own // cut

    def body(step, x_ref, g_ref, gain_ref, shift_ref, h_ref, gb_ref):
        x = x_ref[...].astype(F32)
        centred = x - jnp.mean(x, axis=1, keepdims=True)
        rstd = lax.rsqrt(jnp.mean(centred * centred, axis=1, keepdims=True) + EPS)
        h_ref[...] = (centred * rstd * gain_ref[...] + shift_ref[...]).astype(BF)
        used = jnp.sum(lens[0:1, :], axis=1, keepdims=True)
        row = lax.broadcasted_iota(jnp.int32, (rows, 1), 0) + (spot.t * own + step.index[0] * rows)
        gb_ref[...] = jnp.where(row.astype(F32) < used, g_ref[...].astype(F32), 0.0).astype(BF)

    wide = pl.BlockSpec((rows, x_own.shape[1]), lambda i: (i, 0))
    one = pl.BlockSpec(gain.shape, lambda i: (0, 0))
    there = pl.BlockSpec((rows, x_own.shape[1]), lambda i: (spot.block(0, 0, 0) * cut + i, 0))
    pltpu.emit_pipeline(
        body, grid=(cut,), in_specs=[wide, wide, one, one], out_specs=[there, there], _explicit_indices=True
    )(x_own, g_own, gain, shift, h, gb)


def make_tables(spot, lens, count, inverse, cosine, sine, aq, ak, block):
    total = cosine.shape[0]
    steps = total // 2 // block

    def body(step, inverse_ref, cos_ref, sin_ref, aq_ref, ak_ref):
        i = step.index[0]
        length = jnp.where(i // steps == spot.half, lens[0][0:1, :], lens[1][0:1, :])
        shape = (block, LANES)
        row = (lax.broadcasted_iota(jnp.int32, shape, 0) + (i % steps) * block).astype(F32)
        lane = lanes_of(shape) % HEAD
        segment, position, end = jnp.zeros(shape, F32), row, 0.0
        for j in range(count):
            end = end + length[:, j : j + 1]
            passed = row >= end
            segment = segment + jnp.where(passed, 1.0, 0.0)
            position = position - jnp.where(passed, length[:, j : j + 1], 0.0)
        angle = position * inverse_ref[...]
        sign = jnp.where(lane < ROT // 2, -1.0, 1.0)
        cos_ref[...] = jnp.cos(angle)
        sin_ref[...] = jnp.sin(angle) * sign
        same = segment == lane.astype(F32)
        aq_ref[...] = jnp.where(same & (lane <= count), NEG, 0.0).astype(BF)
        other = (lane <= count) & ~same
        ak_ref[...] = jnp.where(other | ((lane >= 8) & (lane < 11)), 1.0, 0.0).astype(BF)

    spec = pl.BlockSpec((block, LANES), lambda i: (i, 0))
    pltpu.emit_pipeline(
        body,
        grid=(2 * steps,),
        in_specs=[pl.BlockSpec((1, LANES), lambda i: (0, 0))],
        out_specs=[spec] * 4,
        _explicit_indices=True,
    )(inverse, cosine, sine, aq, ak)


def attend_kernel(rows, block, qkv_ref, aq_ref, ak_ref, *refs):
    o_ref, bf_ref, lse_ref = refs[-3:]
    lane = lanes_of((rows, LANES))
    lane_q = lanes_of((block, LANES))
    one = jnp.where(lane % HEAD < 3, 1.0, 0.0).astype(BF)
    first = lane < HEAD
    keys = [jnp.where(half, qkv_ref[:, LANES : 2 * LANES], ak_ref[...]) for half in (first, ~first)]
    values = [jnp.where(half, qkv_ref[:, 2 * LANES :], one) for half in (first, ~first)]
    causal = lanes_of((block, block)) <= lax.broadcasted_iota(jnp.int32, (block, block), 0)
    for b in range(rows // block):
        here = pl.ds(b * block, block)
        lo, hi = b * block, (b + 1) * block
        outs, sums = [], []
        for side in (0, 1):
            half = (lane_q < HEAD) if side == 0 else (lane_q >= HEAD)
            q = jnp.where(half, qkv_ref[here, :LANES], aq_ref[here])
            s_near = lax.dot_general(q, keys[side][lo:hi], NT, preferred_element_type=F32)
            s_near = jnp.where(causal, s_near, NEG)
            top = jnp.max(s_near, axis=1, keepdims=True)
            if b:
                s_far = lax.dot_general(q, keys[side][:lo], NT, preferred_element_type=F32)
                top = jnp.maximum(top, jnp.max(s_far, axis=1, keepdims=True))
            o = jnp.dot(jnp.exp(s_near - top).astype(BF), values[side][lo:hi], preferred_element_type=F32)
            if b:
                o = o + jnp.dot(
                    jnp.exp(s_far - top).astype(BF), values[side][:lo], preferred_element_type=F32
                )
            at = HEAD if side == 0 else 0
            total = o[:, at : at + 1]
            outs.append(o / total)
            sums.append(top + jnp.log(total))
        out = jnp.where(lane_q < HEAD, outs[0], outs[1])
        o_ref[here] = out
        bf_ref[here] = out.astype(BF)
        lse_ref[here] = jnp.where(lane_q < HEAD, sums[0], sums[1])


def split3(x):
    a = x.astype(BF).astype(F32)
    b = (x - a).astype(BF).astype(F32)
    return a, b, x - a - b


def attend_back_kernel(
    rows, block, qkv_ref, aq_ref, ak_ref, o_ref, lse_ref, go_ref, cos_ref, sin_ref, *refs
):
    out_ref, dk_s, dv_s, dqt_s = refs
    lane = lanes_of((rows, LANES))
    lane_k = lanes_of((block, LANES))
    one = jnp.where(lane % HEAD < 3, 1.0, 0.0).astype(BF)
    causal = lax.broadcasted_iota(jnp.int32, (block, block), 0) <= lanes_of((block, block))
    prod = o_ref[...] * go_ref[...].astype(F32)
    dq_first = None
    for side in (0, 1):
        half = (lane < HEAD) if side == 0 else (lane >= HEAD)
        delta = -jnp.sum(jnp.where(half, prod, 0.0), axis=1, keepdims=True)
        at = 0 if side == 0 else HEAD
        lse = -lse_ref[:, at : at + 1]
        q = jnp.where(half, qkv_ref[:, :LANES], aq_ref[...]).astype(F32)
        g = jnp.where(half, go_ref[...].astype(F32), 0.0)
        base = HEAD - at
        for i, (a, d) in enumerate(zip(split3(lse), split3(delta))):
            q = jnp.where(lane == base + 8 + i, a, q)
            g = jnp.where(lane == base + i, d, g)
        q, g = q.astype(BF), g.astype(BF)
        k = jnp.where(half, qkv_ref[:, LANES : 2 * LANES], ak_ref[...])
        v = jnp.where(half, qkv_ref[:, 2 * LANES :], one)
        kt = k.T
        for b in range(rows // block):
            lo, hi = b * block, (b + 1) * block
            here = pl.ds(lo, block)
            st = lax.dot_general(k[lo:hi], q[lo:], NT, preferred_element_type=F32)
            dpt = lax.dot_general(v[lo:hi], g[lo:], NT, preferred_element_type=F32)
            p = jnp.exp(st)
            near = jnp.where(causal, p[:, :block], 0.0)
            p = jnp.concatenate([near, p[:, block:]], axis=1) if hi < rows else near
            ds = (p * dpt).astype(BF)
            dv = jnp.dot(p.astype(BF), g[lo:], preferred_element_type=F32)
            dk = jnp.dot(ds, q[lo:], preferred_element_type=F32)
            dq = jnp.dot(kt[:, lo:hi], ds, preferred_element_type=F32)
            if side == 0:
                dk_s[here] = dk
                dv_s[here] = dv
            else:
                dk = jnp.where(lane_k < HEAD, dk_s[here], dk)
                dv = jnp.where(lane_k < HEAD, dv_s[here], dv)
                out_ref[here, LANES : 2 * LANES] = turn(dk, cos_ref[here], -sin_ref[here]).astype(BF)
                out_ref[here, 2 * LANES :] = dv.astype(BF)
            if b == 0:
                dqt_s[...] = dq
            else:
                dqt_s[:, lo:] += dq
        d = dqt_s[...].T * HEAD**-0.5
        if side == 0:
            dq_first = d
        else:
            d = jnp.where(lane < HEAD, dq_first, d)
            out_ref[:, :LANES] = turn(d, cos_ref[...], -sin_ref[...]).astype(BF)


def outer_products(left, rights, parts, acc, spot, block, sums=None):
    places = spot.places
    rows, size = left.shape[0], left.shape[1] // places
    steps = rows // block
    columns = parts.shape[2]

    def body(step, left_ref, *refs):
        right_refs, out = refs[:-1], refs[-1]
        r, j = step.index
        first = 0
        for right_ref in right_refs:
            there = slice(first, first + right_ref.shape[1])
            first += right_ref.shape[1]
            term = lax.dot_general(left_ref[...], right_ref[...], TN, preferred_element_type=F32)

            @pl.when(r == 0)
            def _():
                acc[j, :, there] = term

            @pl.when((r > 0) & (r < steps - 1))
            def _():
                acc[j, :, there] += term

            @pl.when(r == steps - 1)
            def _():
                out[:, there] = (acc[j, :, there] + term).astype(BF)

            if sums is not None:
                @pl.when(j == 0)
                def _():
                    sums[...] += jnp.sum(right_ref[...].astype(F32), axis=0, keepdims=True)

    pltpu.emit_pipeline(
        body,
        grid=(steps, places),
        in_specs=[pl.BlockSpec((block, size), lambda r, j: (r, lax.rem(spot.at + j, places)))]
        + [pl.BlockSpec((block, x.shape[1]), lambda r, j: (r, 0)) for x in rights],
        out_specs=[pl.BlockSpec((None, size, columns), lambda r, j: (jnp.where(r == steps - 1, j, 0), 0, 0))],
        _explicit_indices=True,
    )(left, *rights, parts)


class ReduceWeight:
    def __init__(self, links, spot, parts, slots, end, joined, mine, given, theirs):
        self.links, self.spot = links, spot
        self.parts, self.slots, self.end, self.joined = parts, slots, end, joined
        self.mine, self.given, self.theirs = mine, given, theirs
        self.shard = mine.shape[0]

    def send(self, src, dst, to, sends=None, gets=None):
        return self.links.copy(src, dst, self.spot.along(to), sends, gets).start()

    def first(self):
        at = self.spot.at
        if self.spot.places == 4:
            self.edges = [
                self.send(self.parts.at[3], self.end, 1, at == 0, at == 1),
                self.send(self.parts.at[1], self.end, 2, at == 3, at == 2),
            ]

    def second(self):
        at, places, parts, slots = self.spot.at, self.spot.places, self.parts, self.slots
        if places == 4:
            inner = (at == 1) | (at == 2)
            self.got = [
                self.send(parts.at[1], slots.at[0], (at + 1) % 4, at < 3, at > 0),
                self.send(parts.at[3], slots.at[1], (at + 3) % 4, at > 0, at < 3),
                self.send(parts.at[2], slots.at[2], (at + 2) % 4, ~inner, inner),
            ]
        else:
            self.got = [self.send(parts.at[j], slots.at[j - 1], (at + j) % places) for j in range(1, places)]

    def third(self):
        if self.spot.places != 4:
            return
        at = self.spot.at
        inner = (at == 1) | (at == 2)
        for edge in self.edges:
            edge.get()
        size, columns = self.parts.shape[1:]

        def body(a, b, out):
            out[...] = (a[...].astype(F32) + b[...].astype(F32)).astype(BF)

        @pl.when(inner)
        def _():
            spec = pl.BlockSpec((self.shard, columns), lambda i: (i, 0))
            pltpu.emit_pipeline(
                body,
                grid=(size // self.shard,),
                in_specs=[pl.BlockSpec((None, self.shard, columns), lambda i: (2, i, 0)), spec],
                out_specs=[spec],
            )(self.parts, self.end, self.joined)

        self.got.append(self.send(self.joined, self.slots.at[2], (at + 2) % 4, inner, ~inner))

    def fourth(self):
        spot = self.spot
        at, places = spot.at, spot.places
        for sent in self.got:
            sent.get()
        columns = self.parts.shape[2]

        def body(own, *refs):
            out = refs[-1]
            total = own[...].astype(F32)
            for k, ref in enumerate(refs[:-1]):
                term = ref[...].astype(F32)
                if places == 4 and k < 2:
                    term = term * jnp.where(at > 0 if k == 0 else at < 3, 1.0, 0.0)
                total = total + term
            out[...] = total.astype(out.dtype)

        def slot(k, part):
            if places == 4 and k < 2:
                k = jnp.where(at > 0, 0, 2) if k == 0 else jnp.where(at < 3, 1, 2)
            return pl.BlockSpec((None, self.shard, columns), lambda i: (k, part, 0))

        for part, out in ((1 - spot.half, self.given), (spot.half, self.mine)):
            own = pl.BlockSpec((None, self.shard, columns), lambda i, part=part: (0, part, 0))
            pltpu.emit_pipeline(
                body,
                grid=(1,),
                in_specs=[own] + [slot(k, part) for k in range(places - 1)],
                out_specs=[pl.BlockSpec((self.shard, columns), lambda i: (0, 0))],
            )(self.parts, *[self.slots] * (places - 1), out)
            if out is self.given:
                self.mate = self.links.copy(self.given, self.theirs, spot.mate).start()

    def finish(self):
        self.mate.get()


class ReduceRows:
    def __init__(self, links, spot, factors, buffers, own):
        self.links, self.spot, self.factors, self.own = links, spot, factors, own
        self.given, self.got = buffers[:3], buffers[3:]
        self.columns = factors[0][1].shape[0] // 2
        self.sent = [[None, None] for _ in range(3)]

    def block(self, part, n, twins):
        spot = self.spot
        g_own, x_own = (n // 2, n % 2) if part == 0 else (n % 2, n // 2)
        other, x1 = 1 - spot.half, 1 - spot.chip
        g = other + g_own * (spot.half - other)
        x = x1 + x_own * (spot.chip - x1)
        c = 1 - spot.core if twins else spot.core
        return g * spot.nt + 2 * x + c

    def added(self, stage):
        return [((), (0,), (2, 0), (3, 1, 0))[stage][k] for k in range(stage)]

    def run(self, stage, part, cut):
        first, last = ((0, 4), (0, 2), (2, 3))[stage]
        own, columns = self.own, self.columns
        rows = own // cut
        n_factors = len(self.factors)
        for earlier in range(stage):
            self.wait(earlier, part, stage)

        def body(*refs):
            ins, out = refs[:-1], refs[-1]
            total = None
            for k in range(n_factors):
                term = lax.dot_general(ins[2 * k][...], ins[2 * k + 1][...], NT, preferred_element_type=F32)
                total = term if total is None else total + term
            for ref in ins[2 * n_factors :]:
                total = total + ref[...].astype(F32)
            out[...] = total.astype(BF)

        in_specs, args = [], []
        for a, b in self.factors:
            depth = a.shape[1]
            in_specs.append(
                pl.BlockSpec(
                    (rows, depth), lambda i: (self.block(part, first + i // cut, stage == 0) * cut + i % cut, 0)
                )
            )
            in_specs.append(pl.BlockSpec((columns, depth), lambda i: (part, 0)))
            args += [a, b]
        for k, offset in enumerate(self.added(stage)):
            in_specs.append(
                pl.BlockSpec((None, rows, columns), lambda i, offset=offset: (part, offset * cut + i, 0))
            )
            args.append(self.got[k])
        pltpu.emit_pipeline(
            body,
            grid=((last - first) * cut,),
            in_specs=in_specs,
            out_specs=[pl.BlockSpec((None, rows, columns), lambda i: (part, i, 0))],
        )(*args, self.given[stage])
        axes = (self.spot.mate, self.spot.across) if part == 0 else (self.spot.across, self.spot.mate)
        device = self.spot.twin if stage == 0 else axes[stage - 1]
        pieces = ((0, 2), (2, 1), (3, 1)) if stage == 0 else ((0, 1), (1, 1)) if stage == 1 else ((0, 1),)
        sent = []
        for at, count in pieces:
            there = pl.ds(at * own, count * own)
            sent.append(
                self.links.copy(self.given[stage].at[part, there], self.got[stage].at[part, there], device).start()
            )
        self.sent[stage][part] = sent

    def wait(self, earlier, part, stage):
        self.sent[earlier][part][stage - earlier - 1].get()

    def last(self, epilogue, ins, outs, cut):
        own, columns = self.own, self.columns
        rows = own // cut
        n_factors = len(self.factors)
        for part in (0, 1):
            for earlier in range(3):
                self.wait(earlier, part, 3)

        def body(*refs):
            mine, rest = refs[: 2 * n_factors], refs[2 * n_factors :]
            total = None
            for k in range(n_factors):
                term = lax.dot_general(mine[2 * k][...], mine[2 * k + 1][...], NT, preferred_element_type=F32)
                total = term if total is None else total + term
            extra = []
            for part in (0, 1):
                terms = [ref[...].astype(F32) for ref in rest[3 * part : 3 * part + 3]]
                extra.append(terms[0] + terms[1] + terms[2])
            total = total + jnp.concatenate(extra, axis=1)
            epilogue(total, rest[6 : 6 + len(ins)], rest[6 + len(ins) :])

        in_specs, args = [], []
        for a, b in self.factors:
            depth = a.shape[1]
            in_specs.append(pl.BlockSpec((rows, depth), lambda i: (self.block(0, 3, False) * cut + i, 0)))
            in_specs.append(pl.BlockSpec((2 * columns, depth), lambda i: (0, 0)))
            args += [a, b]
        for part in (0, 1):
            for k, offset in enumerate(self.added(3)):
                in_specs.append(
                    pl.BlockSpec(
                        (None, rows, columns), lambda i, part=part, offset=offset: (part, offset * cut + i, 0)
                    )
                )
                args.append(self.got[k])

        def spec(ref):
            if ref.shape[0] == 1:
                return pl.BlockSpec(ref.shape, lambda i: (0, 0))
            return pl.BlockSpec((rows, ref.shape[1]), lambda i: (i, 0))

        pltpu.emit_pipeline(
            body, grid=(cut,), in_specs=in_specs + [spec(r) for r in ins], out_specs=[spec(r) for r in outs]
        )(*args, *ins, *outs)


def output_rows(total, ins, outs):
    x_ref, bias_ref = ins
    outs[0][...] = (x_ref[...].astype(F32) + total + bias_ref[...]).astype(BF)


def norm_rows(sums, total, ins, outs):
    x_ref, g_ref, gain_ref = ins
    x = x_ref[...].astype(F32)
    gy = g_ref[...].astype(F32)
    centred = x - jnp.mean(x, axis=1, keepdims=True)
    rstd = lax.rsqrt(jnp.mean(centred * centred, axis=1, keepdims=True) + EPS)
    x_hat = centred * rstd
    scaled = total * gain_ref[...]
    m1 = jnp.mean(scaled, axis=1, keepdims=True)
    m2 = jnp.mean(scaled * x_hat, axis=1, keepdims=True)
    outs[0][...] = rstd * (scaled - m1 - x_hat * m2) + gy
    sums[0:1, :] += jnp.sum(total * x_hat, axis=0, keepdims=True)
    sums[1:2, :] += jnp.sum(total, axis=0, keepdims=True)
    sums[2:3, :] += jnp.sum(gy, axis=0, keepdims=True)


SUMMED = 8


def layer_kernel(ndp, nt, count, *refs):
    refs = list(refs)
    take = lambda n: [refs.pop(0) for _ in range(n)]
    x_own, g_own, gain, shift, lens_own, inverse, wq_own, w1_own, wd_own, w2_own, bias_q, bias_1, bias_out = take(13)
    output, grad_x, small = take(3)
    weights = [take(7) for _ in range(3)]
    row_buffers = [take(6) for _ in range(2)]
    h, gb, wq, w1, wd, w2, qkv, o_float, o, lse, act, slope, go, da, cosine, sine, aq, ak, gz = take(19)
    dk_s, dv_s, dqt_s, lens, acc, sums, biases, line_got, pair_got, local_sem, send, recv = take(12)
    spot = Spot(ndp, nt)
    links = Links(send, recv)
    group = h.shape[0] // 2
    own = x_own.shape[0]
    half, other = spot.half, 1 - spot.half
    greet(spot.partners())

    lens_given = links.copy(lens_own, lens, spot.mate)
    gather_q = GatherWeight(links, spot, wq_own, wq, local_sem.at[0])
    gather_1 = GatherWeight(links, spot, w1_own, w1, local_sem.at[1])
    gather_d = GatherWeight(links, spot, wd_own, wd, local_sem.at[2])
    gather_2 = GatherWeight(links, spot, w2_own, w2, local_sem.at[3])
    rows_h = GatherRows(links, spot, h, own)
    rows_gb = GatherRows(links, spot, gb, own)
    reduce_2, reduce_q, reduce_1 = [
        ReduceWeight(links, spot, parts, slots, end, joined, mine, given, theirs)
        for mine, theirs, given, parts, slots, end, joined in weights
    ]
    branch = ReduceRows(links, spot, [(act, w2), (o, wd)], row_buffers[0], own)
    grad = ReduceRows(links, spot, [(gz, w1), (da, wq)], row_buffers[1], own)
    tables = [cosine, sine, aq, ak]
    blocks = group // own
    q_columns, f_columns = da.shape[1], act.shape[1]
    attend = functools.partial(attend_kernel, group, min(512, group))
    back = functools.partial(attend_back_kernel, group, min(256, group))

    def attend_back(qkv_ref, aq_ref, ak_ref, cos_ref, sin_ref, o_ref, lse_ref, go_ref, out_ref):
        back(qkv_ref, aq_ref, ak_ref, o_ref, lse_ref, go_ref, cos_ref, sin_ref, out_ref, dk_s, dv_s, dqt_s)

    def project(g):
        by_rows(qkv_body, [h, wq, bias_q, cosine, sine], [qkv], own, g * blocks, blocks)

    def attend_group(g):
        by_heads(attend, [qkv], [], [aq, ak], [o_float, o, lse], group, g)

    def output_grads(g):
        by_rows(plain_body, [gb, wd], [go], own, g * blocks, blocks)

    def attend_back_group(g):
        by_heads(attend_back, [qkv], [o_float, lse, go], [aq, ak, cosine, sine], [da], group, g)

    def outer(left, rights, target, columns, total=None):
        outer_products(left, rights, target.parts, acc.at[:, :, pl.ds(0, columns)], spot, left.shape[0] // 2, total)

    lens_given.start()
    gather_q.first()
    sums[...] = jnp.zeros(sums.shape, F32)
    biases[...] = jnp.zeros(biases.shape, F32)
    norm_inputs(spot, x_own, g_own, gain, shift, lens_own, h, gb, 2)
    rows_h.first()
    gather_q.second()
    gather_d.first()
    gather_1.first()
    lens_given.get()
    make_tables(spot, (lens_own, lens), count, inverse, cosine, sine, aq, ak, own)
    gather_q.third()
    rows_h.second()
    gather_d.second()
    gather_q.finish()
    gather_1.second()
    rows_h.finish_near()
    project(half)
    rows_h.third()
    rows_gb.first()
    gather_2.first()
    attend_group(half)
    gather_d.third()
    rows_h.finish()
    project(other)
    attend_group(other)
    rows_gb.second()
    gather_d.finish()
    rows_gb.finish_near()
    output_grads(half)
    gather_1.third()
    gather_2.second()
    attend_back_group(half)
    rows_gb.third()
    gather_1.finish()
    by_rows(gelu_body, [h, w1, bias_1], [act, slope], own)
    rows_gb.finish()
    output_grads(other)
    gather_2.third()
    outer(gb, [act, o], reduce_2, f_columns + o.shape[1])
    reduce_2.first()
    gather_2.finish()
    branch.run(0, 0, 1)
    reduce_2.second()
    branch.run(0, 1, 1)
    attend_back_group(other)
    reduce_2.third()
    branch.run(1, 0, 1)
    branch.run(1, 1, 1)
    outer(h, [da], reduce_q, q_columns, biases.at[1:2, pl.ds(0, q_columns)])
    reduce_q.first()
    by_rows(slope_body, [gb, w2, slope], [gz], own)
    reduce_q.second()
    grad.run(0, 0, 1)
    grad.run(0, 1, 1)
    reduce_q.third()
    branch.run(2, 0, 2)
    branch.run(2, 1, 2)
    grad.run(1, 0, 1)
    grad.run(1, 1, 1)
    outer(h, [gz], reduce_1, f_columns, biases.at[0:1, pl.ds(0, f_columns)])
    reduce_1.first()
    reduce_2.fourth()
    reduce_1.second()
    branch.last(output_rows, [x_own, bias_out], [output], 2)
    grad.run(2, 0, 2)
    grad.run(2, 1, 2)
    reduce_q.fourth()
    reduce_1.third()
    norm = functools.partial(norm_rows, sums)
    grad.last(norm, [x_own, gb.at[pl.ds(pl.multiple_of(spot.block(0, 0, 0) * own, own), own)], gain], [grad_x], 2)
    reduce_1.fourth()

    sums[SUMMED // 2 : SUMMED // 2 + 2, :] = biases[...]
    places = spot.places
    line_got[0] = sums[...]
    got = [links.copy(sums, line_got.at[j], spot.along((spot.at + j) % places)).start() for j in range(1, places)]
    for sent in got:
        sent.get()
    for sent in got:
        sent.drain()
    total = line_got[spot.at]
    for place in range(1, places):
        total = total + line_got[(spot.at + places - place) % places]
    sums[...] = total
    row = lax.broadcasted_iota(jnp.int32, sums.shape, 0)
    for k, device in enumerate((spot.mate, spot.across, spot.twin)):
        sent = links.copy(sums, pair_got.at[k], device).start()
        sent.get()
        sent.drain()
        theirs = pair_got[k]
        if k == 0:
            small[1] = theirs
        sums[...] = sums[...] + jnp.where(row < SUMMED // 2, theirs, 0.0)
    small[0] = sums[...]
    for reduced in (reduce_2, reduce_q, reduce_1):
        reduced.finish()
    links.finish()


def layer_call(ndp, nt, count, x_own, g_own, gain, shift, lens, inverse, weights, biases):
    own, width = x_own.shape
    group = nt * own
    rows = 2 * group
    places = ndp // 2
    size, shard = width // places, width // ndp
    q3, f, q = [weights[k].shape[1] // 2 for k in (0, 1, 2)]
    shape = lambda *s: jax.ShapeDtypeStruct(s, BF)
    full = lambda *s: jax.ShapeDtypeStruct(s, F32)
    out_shape = [shape(own, width), full(own, width), full(2, SUMMED, width)]
    for n in (f + q, q3, f):
        out_shape += [full(shard, n), shape(shard, n), shape(shard, n)]
        out_shape += [shape(places, size, n), shape(places - 1, size, n), shape(size, n), shape(size, n)]
    for _ in range(2):
        out_shape += [shape(2, k * own, width // 2) for k in (4, 2, 1)] * 2
    out_shape += [shape(rows, width), shape(rows, width)]
    out_shape += [shape(width, n) for n in (q3, f, q, f)]
    out_shape += [shape(rows, q3), full(rows, q), shape(rows, q), full(rows, q)]
    out_shape += [shape(rows, f), shape(rows, f), shape(rows, q), shape(rows, q3)]
    out_shape += [full(rows, LANES), full(rows, LANES), shape(rows, LANES), shape(rows, LANES), shape(rows, f)]
    anywhere = pl.BlockSpec(memory_space=pl.ANY)
    in_specs = [anywhere] * 13
    in_specs[4] = pl.BlockSpec(memory_space=pltpu.VMEM)
    out_specs = [anywhere] * len(out_shape)
    out_specs[2] = pl.BlockSpec(memory_space=pltpu.VMEM)
    transfers = 1 + 2 * 9 + 4 * (1 + max(4, places)) + 3 * (1 + max(6, places)) + 2 * 2 * 6 + places + 3
    return pl.pallas_call(
        functools.partial(layer_kernel, ndp, nt, count),
        in_specs=in_specs,
        out_specs=out_specs,
        out_shape=out_shape,
        scratch_shapes=[
            pltpu.VMEM((group, LANES), F32),
            pltpu.VMEM((group, LANES), F32),
            pltpu.VMEM((LANES, group), F32),
            pltpu.VMEM(lens.shape, F32),
            pltpu.VMEM((places, size, f + q), F32),
            pltpu.VMEM((SUMMED, width), F32),
            pltpu.VMEM((2, width), F32),
            pltpu.VMEM((places, SUMMED, width), F32),
            pltpu.VMEM((3, SUMMED, width), F32),
            pltpu.SemaphoreType.DMA((4,)),
            pltpu.SemaphoreType.DMA((transfers,)),
            pltpu.SemaphoreType.DMA((transfers,)),
        ],
        compiler_params=pltpu.CompilerParams(collective_id=0, has_side_effects=True, vmem_limit_bytes=VMEM),
    )(x_own, g_own, gain, shift, lens, inverse, *weights, *biases)


def local(
    layer_input,
    seq_lens,
    ln_gain,
    ln_bias,
    w_qkv,
    b_qkv,
    w_dense,
    b_dense,
    w_fc1,
    b_fc1,
    w_fc2,
    b_fc2,
    cotangent,
):
    own, width = layer_input.shape
    ndp, nt = lax.axis_size("dp"), lax.axis_size("tensor")
    dp, t = lax.axis_index("dp"), lax.axis_index("tensor")
    half, at, places = dp % 2, dp // 2, ndp // 2
    chip, core = t // 2, t % 2
    group = own * nt
    shard = w_qkv.shape[0]
    q_width = w_qkv.shape[2] // 2
    f_width = w_fc1.shape[1] // 2
    pairs = q_width // LANES
    other = 1 - half

    wq = w_qkv.reshape(shard, 3, 2, pairs, LANES).transpose(0, 2, 3, 1, 4).reshape(shard, 6 * q_width)
    bias_q = pick(b_qkv.reshape(3, 2, pairs, LANES).transpose(1, 2, 0, 3), half).reshape(1, 3 * q_width)
    bias_1 = pick(b_fc1.reshape(2, f_width), half)[None]
    count = seq_lens.shape[1]
    lens = jnp.zeros((8, LANES), F32).at[0, :count].set(seq_lens[0].astype(F32))
    steps = jnp.arange(ROT // 2, dtype=F32)
    inverse = jnp.exp(-math.log(10000.0) * 2.0 * steps / ROT)
    inverse = jnp.concatenate([inverse, inverse, jnp.zeros((HEAD - ROT,), F32)] * 2)[None]

    made = layer_call(
        ndp, nt, count, layer_input, cotangent, ln_gain[None], ln_bias[None], lens, inverse,
        [wq, w_fc1, w_dense.T, w_fc2.T], [bias_q, bias_1, (b_dense + b_fc2)[None]],
    )
    output, grad_x, small = made[:3]

    def both(mine, theirs):
        theirs = theirs.astype(F32)
        return jnp.stack([jnp.where(half == 0, mine, theirs), jnp.where(half == 0, theirs, mine)])

    g_2, g_wq, g_w1 = [both(made[k], made[k + 1]) for k in (3, 10, 17)]
    g_w2, g_wd = g_2[:, :, :f_width], g_2[:, :, f_width:]
    late, early = small[0, :2], small[0, 2]
    g_biases = both(small[0, SUMMED // 2 : SUMMED // 2 + 2], small[1, SUMMED // 2 : SUMMED // 2 + 2])
    g_b1 = g_biases[:, 0, :f_width].reshape(-1)
    g_bq = g_biases[:, 1, : 3 * q_width].reshape(2, pairs, 3, LANES).transpose(2, 0, 1, 3).reshape(3, 2 * q_width)
    out_wq = g_wq.reshape(2, shard, pairs, 3, LANES).transpose(1, 3, 0, 2, 4).reshape(shard, 3, 2 * q_width)
    out_wd = g_wd.transpose(0, 2, 1).reshape(2 * q_width, shard)
    out_w1 = g_w1.transpose(1, 0, 2).reshape(shard, 2 * f_width)
    out_w2 = g_w2.transpose(0, 2, 1).reshape(2 * f_width, shard)
    return (
        output,
        grad_x,
        late[0],
        late[1],
        out_wq,
        g_bq,
        out_wd,
        early,
        out_w1,
        g_b1,
        out_w2,
        early,
    )


def solution(mesh):
    rows = P(("dp", "tensor"), None)
    in_specs = (
        rows,
        P("dp", None),
        P(),
        P(),
        P("dp", None, "tensor"),
        P(None, "tensor"),
        P("tensor", "dp"),
        P(),
        P("dp", "tensor"),
        P("tensor"),
        P("tensor", "dp"),
        P(),
        rows,
    )
    out_specs = (
        rows,
        rows,
        P(),
        P(),
        P("dp", None, "tensor"),
        P(None, "tensor"),
        P("tensor", "dp"),
        P(),
        P("dp", "tensor"),
        P("tensor"),
        P("tensor", "dp"),
        P(),
    )
    return jax.shard_map(local, mesh=mesh, in_specs=in_specs, out_specs=out_specs, check_vma=False)
```

```python
import functools
import math

import jax
import jax.numpy as jnp
from jax import lax
from jax.experimental import pallas as pl
from jax.experimental.pallas import tpu as pltpu
from jax.sharding import PartitionSpec as P

HEAD = 64
ROT = 32
EPS = 1e-05
NEG = -1e30
LANES = 128
BF = jnp.bfloat16
F32 = jnp.float32
NT = (((1,), (1,)), ((), ()))
TN = (((0,), (0,)), ((), ()))
VMEM = 56 * 2**20
COST = pl.CostEstimate(flops=0, bytes_accessed=0, transcendentals=0)


def pick(x, index):
    return lax.dynamic_index_in_dim(x, index, 0, keepdims=False)


def place(buffer, block, *index):
    return lax.dynamic_update_slice(
        buffer, block.reshape((1,) * len(index) + block.shape), tuple(index) + (0,) * block.ndim
    )


def lanes_of(shape):
    return lax.broadcasted_iota(jnp.int32, shape, 1)


def turn(x, cosine, sine):
    lane = lanes_of(x.shape) % HEAD
    other = jnp.where(lane < ROT // 2, pltpu.roll(x, LANES - ROT // 2, 1), pltpu.roll(x, ROT // 2, 1))
    return x * cosine + other * sine


def qkv_rows(acc, extras, outs):
    bias, cosine, sine = (ref[...] for ref in extras)
    acc = acc + bias
    out_ref = outs[0]
    for at in range(0, acc.shape[1], 3 * LANES):
        q = turn(acc[:, at : at + LANES], cosine, sine).astype(BF)
        out_ref[:, at : at + LANES] = (q.astype(F32) * HEAD**-0.5).astype(BF)
        k = turn(acc[:, at + LANES : at + 2 * LANES], cosine, sine)
        out_ref[:, at + LANES : at + 2 * LANES] = k.astype(BF)
        out_ref[:, at + 2 * LANES : at + 3 * LANES] = acc[:, at + 2 * LANES : at + 3 * LANES].astype(BF)


def plain_rows(acc, extras, outs):
    outs[0][...] = acc.astype(BF)


def gelu_rows(acc, extras, outs):
    z = acc + extras[0][...]
    c = math.sqrt(2.0 / math.pi)
    square = z * z
    gate = 0.5 + 0.5 * jnp.tanh(z * (c + (c * 0.044715) * square))
    value = z * gate
    outs[0][...] = value.astype(BF)
    outs[1][...] = (gate + (value - value * gate) * (2.0 * c + (6.0 * 0.044715 * c) * square)).astype(BF)


def slope_rows(acc, extras, outs):
    outs[0][...] = (acc * extras[0][...].astype(F32)).astype(BF)


class Links:
    def __init__(self, send, recv):
        self.send, self.recv, self.count, self.pending = send, recv, 0, []

    def copy(self, src, dst, device, sends=None, gets=None):
        n = self.count
        self.count += 1
        made = pltpu.make_async_remote_copy(
            src_ref=src,
            dst_ref=dst,
            send_sem=self.send.at[n],
            recv_sem=self.recv.at[n],
            device_id=device,
            device_id_type=pl.DeviceIdType.MESH,
        )
        return Sent(self, made, sends, gets)

    def finish(self):
        for sent in self.pending:
            sent.when(sent.sends, sent.made.wait_send)


class Sent:
    def __init__(self, links, made, sends, gets):
        self.links, self.made, self.sends, self.gets = links, made, sends, gets

    def when(self, condition, action):
        if condition is None:
            action()
        else:
            pl.when(condition)(action)

    def start(self):
        self.when(self.sends, self.made.start)
        self.links.pending.append(self)
        return self

    def get(self):
        self.when(self.gets, self.made.wait_recv)

    def drain(self):
        self.links.pending.remove(self)
        self.when(self.sends, self.made.wait_send)


def greet(devices):
    barrier = pltpu.get_barrier_semaphore()
    for device in devices:
        pl.semaphore_signal(barrier, inc=1, device_id=device, device_id_type=pl.DeviceIdType.MESH)
    pl.semaphore_wait(barrier, len(devices))


class Spot:
    def __init__(self, ndp, nt):
        self.dp, self.t = lax.axis_index("dp"), lax.axis_index("tensor")
        self.half, self.at = self.dp % 2, self.dp // 2
        self.chip, self.core = self.t // 2, self.t % 2
        self.places, self.nt = ndp // 2, nt
        self.mate = (self.dp + 1 - 2 * self.half, self.t)
        self.across = (self.dp, self.t + 2 - 4 * self.chip)
        self.twin = (self.dp, self.t + 1 - 2 * self.core)

    def along(self, place):
        return (2 * place + self.half, self.t)

    def partners(self):
        line = [self.along((self.at + j) % self.places) for j in range(1, self.places)]
        return [self.mate, self.across, self.twin] + line

    def block(self, mates, acrosses, twins):
        g = self.half if not mates else 1 - self.half
        x = self.chip if not acrosses else 1 - self.chip
        c = self.core if not twins else 1 - self.core
        return g * self.nt + 2 * x + c


class GatherRows:
    def __init__(self, links, spot, whole, size):
        self.whole, self.size = whole, size
        low = size // 4
        near, across, mate, far = [spot.block(g, x, 0) for g, x in ((0, 0), (0, 1), (1, 0), (1, 1))]
        made = lambda block, device, first=0, count=size: links.copy(
            self.rows(block, first, count), self.rows(block, first, count), device
        )
        self.x, self.y = made(near, spot.across), made(near, spot.mate)
        self.low = made(across, spot.mate, 0, low)
        self.high = made(mate, spot.across, low, size - low)
        self.near_twin, self.x_twin, self.y_twin = [made(n, spot.twin) for n in (near, across, mate)]
        self.low_twin = made(far, spot.twin, 0, low)
        self.high_twin = made(far, spot.twin, low, size - low)

    def rows(self, block, first, count):
        return self.whole.at[pl.ds(pl.multiple_of(block * self.size, self.size) + first, count)]

    def first(self):
        self.x.start()
        self.y.start()
        self.near_twin.start()

    def second(self):
        self.x.get()
        self.low.start()
        self.x_twin.start()
        self.y.get()
        self.high.start()
        self.y_twin.start()

    def third(self):
        self.low.get()
        self.low_twin.start()
        self.high.get()
        self.high_twin.start()

    def finish_near(self):
        self.near_twin.get()
        self.x_twin.get()

    def finish(self):
        for part in (self.y_twin, self.low_twin, self.high_twin):
            part.get()


class GatherWeight:
    def __init__(self, links, spot, own, whole, sem):
        self.spot, self.whole = spot, whole
        self.shard, columns = own.shape[0], whole.shape[1]
        at, places = spot.at, spot.places
        half = lambda k: own.at[:, pl.ds(pl.multiple_of(k * columns, columns), columns)]
        place = whole.at[pl.ds(pl.multiple_of((2 * at + spot.half) * self.shard, self.shard), self.shard)]
        self.local = pltpu.make_async_copy(half(spot.half), place, sem)
        self.y = links.copy(half(1 - spot.half), place, spot.mate)
        made = lambda n, to, sends=None, gets=None: links.copy(
            self.pair(n), self.pair(n), spot.along(to), sends, gets
        )
        if places == 4:
            inner = (at == 1) | (at == 2)
            self.two = made(at, (at + 2) % 4)
            self.parts = [made(at, (at + 1) % 4, at < 3, at > 0), made(at, (at + 3) % 4, at > 0, at < 3)]
            self.three = made((at + 2) % 4, 3 * (at // 2), inner, ~inner)
        else:
            self.parts = [made(at, (at + j) % places) for j in range(1, places)]

    def pair(self, place):
        rows = 2 * self.shard
        return self.whole.at[pl.ds(pl.multiple_of(place * rows, rows), rows)]

    def first(self):
        self.local.start()
        self.y.start()

    def second(self):
        self.local.wait()
        self.y.get()
        if self.spot.places == 4:
            self.two.start()
        for part in self.parts:
            part.start()

    def third(self):
        if self.spot.places == 4:
            self.two.get()
            self.three.start()

    def finish(self):
        for part in self.parts:
            part.get()
        if self.spot.places == 4:
            self.three.get()


def qkv_body(h_ref, w_ref, b_ref, cos_ref, sin_ref, out_ref):
    acc = jnp.dot(h_ref[...], w_ref[...], preferred_element_type=F32) + b_ref[...]
    cosine, sine = cos_ref[...], sin_ref[...]
    for at in range(0, acc.shape[1], 3 * LANES):
        q = turn(acc[:, at : at + LANES], cosine, sine).astype(BF)
        out_ref[:, at : at + LANES] = (q.astype(F32) * HEAD**-0.5).astype(BF)
        k = turn(acc[:, at + LANES : at + 2 * LANES], cosine, sine)
        out_ref[:, at + LANES : at + 2 * LANES] = k.astype(BF)
        out_ref[:, at + 2 * LANES : at + 3 * LANES] = acc[:, at + 2 * LANES : at + 3 * LANES].astype(BF)


def gelu_body(h_ref, w_ref, b_ref, act_ref, slope_ref):
    z = jnp.dot(h_ref[...], w_ref[...], preferred_element_type=F32) + b_ref[...]
    c = math.sqrt(2.0 / math.pi)
    square = z * z
    gate = 0.5 + 0.5 * jnp.tanh(z * (c + (c * 0.044715) * square))
    value = z * gate
    act_ref[...] = value.astype(BF)
    slope_ref[...] = (gate + (value - value * gate) * (2.0 * c + (6.0 * 0.044715 * c) * square)).astype(BF)


def plain_body(h_ref, w_ref, out_ref):
    out_ref[...] = jnp.dot(h_ref[...], w_ref[...], preferred_element_type=F32).astype(BF)


def slope_body(h_ref, w_ref, slope_ref, out_ref):
    acc = jnp.dot(h_ref[...], w_ref[...], preferred_element_type=F32)
    out_ref[...] = (acc * slope_ref[...].astype(F32)).astype(BF)


def by_rows(body, ins, outs, block, first=0, count=None, events=None):
    total = outs[0].shape[0]
    count = count or total // block

    def spec(ref):
        width = ref.shape[1]
        if ref.shape[0] == total:
            return pl.BlockSpec((block, width), lambda i: (first + i, 0))
        return pl.BlockSpec(ref.shape, lambda i: (0, 0))

    def stepped(step, *refs):
        for k, event in (events or {}).items():
            pl.when(step.index[0] == k)(event)
        body(*refs)

    pltpu.emit_pipeline(
        stepped,
        grid=(count,),
        in_specs=[spec(r) for r in ins],
        out_specs=[spec(r) for r in outs],
        _explicit_indices=True,
    )(*ins, *outs)


def by_heads(body, wide_ins, ins, aug_ins, outs, rows, g):
    pairs = wide_ins[0].shape[1] // (3 * LANES)

    def spec(ref, kind):
        if kind == 2:
            return pl.BlockSpec((rows, LANES), lambda j: (g, 0))
        width = 3 * LANES if ref.shape[1] == pairs * 3 * LANES else LANES
        return pl.BlockSpec((rows, width), lambda j: (g, j))

    specs = [spec(r, 0) for r in wide_ins] + [spec(r, 2) for r in aug_ins] + [spec(r, 0) for r in ins]
    pltpu.emit_pipeline(
        body, grid=(pairs,), in_specs=specs, out_specs=[spec(r, 0) for r in outs]
    )(*wide_ins, *aug_ins, *ins, *outs)


def norm_inputs(spot, x_own, g_own, gain, shift, lens, h, gb, cut):
    own = x_own.shape[0]
    rows = own // cut

    def body(step, x_ref, g_ref, gain_ref, shift_ref, h_ref, gb_ref):
        x = x_ref[...].astype(F32)
        centred = x - jnp.mean(x, axis=1, keepdims=True)
        rstd = lax.rsqrt(jnp.mean(centred * centred, axis=1, keepdims=True) + EPS)
        h_ref[...] = (centred * rstd * gain_ref[...] + shift_ref[...]).astype(BF)
        used = jnp.sum(lens[0:1, :], axis=1, keepdims=True)
        row = lax.broadcasted_iota(jnp.int32, (rows, 1), 0) + (spot.t * own + step.index[0] * rows)
        gb_ref[...] = jnp.where(row.astype(F32) < used, g_ref[...].astype(F32), 0.0).astype(BF)

    wide = pl.BlockSpec((rows, x_own.shape[1]), lambda i: (i, 0))
    one = pl.BlockSpec(gain.shape, lambda i: (0, 0))
    there = pl.BlockSpec((rows, x_own.shape[1]), lambda i: (spot.block(0, 0, 0) * cut + i, 0))
    pltpu.emit_pipeline(
        body, grid=(cut,), in_specs=[wide, wide, one, one], out_specs=[there, there], _explicit_indices=True
    )(x_own, g_own, gain, shift, h, gb)


def make_tables(spot, lens, count, inverse, cosine, sine, aq, ak, block):
    total = cosine.shape[0]
    steps = total // 2 // block

    def body(step, inverse_ref, cos_ref, sin_ref, aq_ref, ak_ref):
        i = step.index[0]
        length = jnp.where(i // steps == spot.half, lens[0][0:1, :], lens[1][0:1, :])
        shape = (block, LANES)
        row = (lax.broadcasted_iota(jnp.int32, shape, 0) + (i % steps) * block).astype(F32)
        lane = lanes_of(shape) % HEAD
        segment, position, end = jnp.zeros(shape, F32), row, 0.0
        for j in range(count):
            end = end + length[:, j : j + 1]
            passed = row >= end
            segment = segment + jnp.where(passed, 1.0, 0.0)
            position = position - jnp.where(passed, length[:, j : j + 1], 0.0)
        angle = position * inverse_ref[...]
        sign = jnp.where(lane < ROT // 2, -1.0, 1.0)
        cos_ref[...] = jnp.cos(angle)
        sin_ref[...] = jnp.sin(angle) * sign
        same = segment == lane.astype(F32)
        aq_ref[...] = jnp.where(same & (lane <= count), NEG, 0.0).astype(BF)
        other = (lane <= count) & ~same
        ak_ref[...] = jnp.where(other | ((lane >= 8) & (lane < 11)), 1.0, 0.0).astype(BF)

    spec = pl.BlockSpec((block, LANES), lambda i: (i, 0))
    pltpu.emit_pipeline(
        body,
        grid=(2 * steps,),
        in_specs=[pl.BlockSpec((1, LANES), lambda i: (0, 0))],
        out_specs=[spec] * 4,
        _explicit_indices=True,
    )(inverse, cosine, sine, aq, ak)


def attend_kernel(rows, block, qkv_ref, aq_ref, ak_ref, *refs):
    o_ref, bf_ref, lse_ref = refs[-3:]
    lane = lanes_of((rows, LANES))
    lane_q = lanes_of((block, LANES))
    one = jnp.where(lane % HEAD < 3, 1.0, 0.0).astype(BF)
    first = lane < HEAD
    keys = [jnp.where(half, qkv_ref[:, LANES : 2 * LANES], ak_ref[...]) for half in (first, ~first)]
    values = [jnp.where(half, qkv_ref[:, 2 * LANES :], one) for half in (first, ~first)]
    causal = lanes_of((block, block)) <= lax.broadcasted_iota(jnp.int32, (block, block), 0)
    for b in range(rows // block):
        here = pl.ds(b * block, block)
        lo, hi = b * block, (b + 1) * block
        outs, sums = [], []
        for side in (0, 1):
            half = (lane_q < HEAD) if side == 0 else (lane_q >= HEAD)
            q = jnp.where(half, qkv_ref[here, :LANES], aq_ref[here])
            s_near = lax.dot_general(q, keys[side][lo:hi], NT, preferred_element_type=F32)
            s_near = jnp.where(causal, s_near, NEG)
            top = jnp.max(s_near, axis=1, keepdims=True)
            if b:
                s_far = lax.dot_general(q, keys[side][:lo], NT, preferred_element_type=F32)
                top = jnp.maximum(top, jnp.max(s_far, axis=1, keepdims=True))
            o = jnp.dot(jnp.exp(s_near - top).astype(BF), values[side][lo:hi], preferred_element_type=F32)
            if b:
                o = o + jnp.dot(
                    jnp.exp(s_far - top).astype(BF), values[side][:lo], preferred_element_type=F32
                )
            at = HEAD if side == 0 else 0
            total = o[:, at : at + 1]
            outs.append(o / total)
            sums.append(top + jnp.log(total))
        out = jnp.where(lane_q < HEAD, outs[0], outs[1])
        o_ref[here] = out
        bf_ref[here] = out.astype(BF)
        lse_ref[here] = jnp.where(lane_q < HEAD, sums[0], sums[1])


def split3(x):
    a = x.astype(BF).astype(F32)
    b = (x - a).astype(BF).astype(F32)
    return a, b, x - a - b


def attend_back_kernel(
    rows, block, qkv_ref, aq_ref, ak_ref, o_ref, lse_ref, go_ref, cos_ref, sin_ref, *refs
):
    out_ref, dk_s, dv_s, dqt_s = refs
    lane = lanes_of((rows, LANES))
    lane_k = lanes_of((block, LANES))
    one = jnp.where(lane % HEAD < 3, 1.0, 0.0).astype(BF)
    causal = lax.broadcasted_iota(jnp.int32, (block, block), 0) <= lanes_of((block, block))
    prod = o_ref[...] * go_ref[...].astype(F32)
    dq_first = None
    for side in (0, 1):
        half = (lane < HEAD) if side == 0 else (lane >= HEAD)
        delta = -jnp.sum(jnp.where(half, prod, 0.0), axis=1, keepdims=True)
        at = 0 if side == 0 else HEAD
        lse = -lse_ref[:, at : at + 1]
        q = jnp.where(half, qkv_ref[:, :LANES], aq_ref[...]).astype(F32)
        g = jnp.where(half, go_ref[...].astype(F32), 0.0)
        base = HEAD - at
        for i, (a, d) in enumerate(zip(split3(lse), split3(delta))):
            q = jnp.where(lane == base + 8 + i, a, q)
            g = jnp.where(lane == base + i, d, g)
        q, g = q.astype(BF), g.astype(BF)
        k = jnp.where(half, qkv_ref[:, LANES : 2 * LANES], ak_ref[...])
        v = jnp.where(half, qkv_ref[:, 2 * LANES :], one)
        kt = k.T
        for b in range(rows // block):
            lo, hi = b * block, (b + 1) * block
            here = pl.ds(lo, block)
            st = lax.dot_general(k[lo:hi], q[lo:], NT, preferred_element_type=F32)
            dpt = lax.dot_general(v[lo:hi], g[lo:], NT, preferred_element_type=F32)
            p = jnp.exp(st)
            near = jnp.where(causal, p[:, :block], 0.0)
            p = jnp.concatenate([near, p[:, block:]], axis=1) if hi < rows else near
            ds = (p * dpt).astype(BF)
            dv = jnp.dot(p.astype(BF), g[lo:], preferred_element_type=F32)
            dk = jnp.dot(ds, q[lo:], preferred_element_type=F32)
            dq = jnp.dot(kt[:, lo:hi], ds, preferred_element_type=F32)
            if side == 0:
                dk_s[here] = dk
                dv_s[here] = dv
            else:
                dk = jnp.where(lane_k < HEAD, dk_s[here], dk)
                dv = jnp.where(lane_k < HEAD, dv_s[here], dv)
                out_ref[here, LANES : 2 * LANES] = turn(dk, cos_ref[here], -sin_ref[here]).astype(BF)
                out_ref[here, 2 * LANES :] = dv.astype(BF)
            if b == 0:
                dqt_s[...] = dq
            else:
                dqt_s[:, lo:] += dq
        d = dqt_s[...].T * HEAD**-0.5
        if side == 0:
            dq_first = d
        else:
            d = jnp.where(lane < HEAD, dq_first, d)
            out_ref[:, :LANES] = turn(d, cos_ref[...], -sin_ref[...]).astype(BF)


def outer_products(left, rights, parts, acc, spot, block, sums=None):
    places = spot.places
    rows, size = left.shape[0], left.shape[1] // places
    steps = rows // block
    columns = parts.shape[2]

    def body(step, left_ref, *refs):
        right_refs, out = refs[:-1], refs[-1]
        r, j = step.index
        first = 0
        turned = left_ref[...].T
        for right_ref in right_refs:
            there = slice(first, first + right_ref.shape[1])
            first += right_ref.shape[1]
            term = jnp.dot(turned, right_ref[...], preferred_element_type=F32)

            @pl.when(r == 0)
            def _():
                acc[j, :, there] = term

            @pl.when((r > 0) & (r < steps - 1))
            def _():
                acc[j, :, there] += term

            @pl.when(r == steps - 1)
            def _():
                out[:, there] = (acc[j, :, there] + term).astype(BF)

            if sums is not None:
                @pl.when(j == 0)
                def _():
                    sums[...] += jnp.sum(right_ref[...].astype(F32), axis=0, keepdims=True)

    pltpu.emit_pipeline(
        body,
        grid=(steps, places),
        in_specs=[pl.BlockSpec((block, size), lambda r, j: (r, lax.rem(spot.at + j, places)))]
        + [pl.BlockSpec((block, x.shape[1]), lambda r, j: (r, 0)) for x in rights],
        out_specs=[pl.BlockSpec((None, size, columns), lambda r, j: (jnp.where(r == steps - 1, j, 0), 0, 0))],
        _explicit_indices=True,
    )(left, *rights, parts)


class ReduceWeight:
    def __init__(self, links, spot, parts, slots, end, joined, results, given, theirs):
        self.links, self.spot = links, spot
        self.parts, self.slots, self.end, self.joined = parts, slots, end, joined
        self.results, self.given, self.theirs = results, given, theirs
        self.shard = given.shape[0]

    def send(self, src, dst, to, sends=None, gets=None):
        return self.links.copy(src, dst, self.spot.along(to), sends, gets).start()

    def first(self):
        at = self.spot.at
        if self.spot.places == 4:
            self.edges = [
                self.send(self.parts.at[3], self.end, 1, at == 0, at == 1),
                self.send(self.parts.at[1], self.end, 2, at == 3, at == 2),
            ]

    def second(self):
        at, places, parts, slots = self.spot.at, self.spot.places, self.parts, self.slots
        if places == 4:
            inner = (at == 1) | (at == 2)
            self.got = [
                self.send(parts.at[1], slots.at[0], (at + 1) % 4, at < 3, at > 0),
                self.send(parts.at[3], slots.at[1], (at + 3) % 4, at > 0, at < 3),
                self.send(parts.at[2], slots.at[2], (at + 2) % 4, ~inner, inner),
            ]
        else:
            self.got = [self.send(parts.at[j], slots.at[j - 1], (at + j) % places) for j in range(1, places)]

    def third(self):
        if self.spot.places != 4:
            return
        at = self.spot.at
        inner = (at == 1) | (at == 2)
        for edge in self.edges:
            edge.get()
        size, columns = self.parts.shape[1:]

        def body(a, b, out):
            out[...] = (a[...].astype(F32) + b[...].astype(F32)).astype(BF)

        @pl.when(inner)
        def _():
            spec = pl.BlockSpec((self.shard, columns), lambda i: (i, 0))
            pltpu.emit_pipeline(
                body,
                grid=(size // self.shard,),
                in_specs=[pl.BlockSpec((None, self.shard, columns), lambda i: (2, i, 0)), spec],
                out_specs=[spec],
            )(self.parts, self.end, self.joined)

        self.got.append(self.send(self.joined, self.slots.at[2], (at + 2) % 4, inner, ~inner))

    def fourth(self):
        spot = self.spot
        at, places = spot.at, spot.places
        for sent in self.got:
            sent.get()
        columns = self.parts.shape[2]

        def body(given, own, *refs):
            total = own[...].astype(F32)
            for k, ref in enumerate(refs[: places - 1]):
                term = ref[...].astype(F32)
                if places == 4 and k < 2:
                    term = term * jnp.where(at > 0 if k == 0 else at < 3, 1.0, 0.0)
                total = total + term
            if given:
                refs[-1][...] = total.astype(BF)
            else:
                self.store(total, refs[places - 1 :])

        def slot(k, part):
            if places == 4 and k < 2:
                k = jnp.where(at > 0, 0, 2) if k == 0 else jnp.where(at < 3, 1, 2)
            return pl.BlockSpec((None, self.shard, columns), lambda i: (k, part, 0))

        for part in (1 - spot.half, spot.half):
            own = pl.BlockSpec((None, self.shard, columns), lambda i, part=part: (0, part, 0))
            given = part is not spot.half
            specs, outs = self.whole_given() if given else self.own_columns(spot.half)
            pltpu.emit_pipeline(
                functools.partial(body, given),
                grid=(1,),
                in_specs=[own] + [slot(k, part) for k in range(places - 1)],
                out_specs=specs,
            )(self.parts, *[self.slots] * (places - 1), *outs)
            if given:
                self.mate = self.links.copy(self.given, self.theirs, spot.mate).start()

    def whole_given(self):
        return [pl.BlockSpec(self.given.shape, lambda i: (0, 0))], [self.given]

    def own_columns(self, half):
        specs = []
        for ref, first, width, turned in self.results:
            if turned:
                specs.append(pl.BlockSpec((width, self.shard), lambda i: (half, 0)))
            else:
                specs.append(pl.BlockSpec((self.shard, width), lambda i: (0, half)))
        return specs, [result[0] for result in self.results]

    def store(self, total, outs):
        for out, (_, first, width, turned) in zip(outs, self.results):
            mine = total[:, first : first + width]
            out[...] = mine.T if turned else mine

    def finish(self):
        self.mate.get()

        def body(theirs, *outs):
            self.store(theirs[...].astype(F32), outs)

        specs, outs = self.own_columns(1 - self.spot.half)
        pltpu.emit_pipeline(body, grid=(1,), in_specs=self.whole_given()[0], out_specs=specs)(self.theirs, *outs)


class ReduceRows:
    def __init__(self, links, spot, factors, buffers, own):
        self.links, self.spot, self.factors, self.own = links, spot, factors, own
        self.given, self.got = buffers[:3], buffers[3:]
        self.columns = factors[0][1].shape[0] // 2
        self.sent = [[None, None] for _ in range(3)]

    def block(self, part, n, twins):
        spot = self.spot
        g_own = (1 - part) * (n // 2) + part * (n % 2)
        x_own = (1 - part) * (n % 2) + part * (n // 2)
        other, x1 = 1 - spot.half, 1 - spot.chip
        g = other + g_own * (spot.half - other)
        x = x1 + x_own * (spot.chip - x1)
        c = 1 - spot.core if twins else spot.core
        return g * spot.nt + 2 * x + c

    def added(self, stage):
        return [((), (0,), (2, 0), (3, 1, 0))[stage][k] for k in range(stage)]

    def run(self, stage, cut):
        first, last = ((0, 4), (0, 2), (2, 3))[stage]
        own, columns = self.own, self.columns
        rows = own // cut
        each = (last - first) * cut
        n_factors = len(self.factors)
        for part in (0, 1):
            for earlier in range(stage):
                self.wait(earlier, part, stage)

        def body(*refs):
            ins, out = refs[:-1], refs[-1]
            total = None
            for k in range(n_factors):
                term = lax.dot_general(ins[2 * k][...], ins[2 * k + 1][...], NT, preferred_element_type=F32)
                total = term if total is None else total + term
            for ref in ins[2 * n_factors :]:
                total = total + ref[...].astype(F32)
            out[...] = total.astype(BF)

        def row_block(i):
            part, k = i // each, i % each
            return self.block(part, first + k // cut, stage == 0) * cut + k % cut

        in_specs, args = [], []
        for a, b in self.factors:
            depth = a.shape[1]
            in_specs.append(pl.BlockSpec((rows, depth), lambda i: (row_block(i), 0)))
            in_specs.append(pl.BlockSpec((columns, depth), lambda i: (i // each, 0)))
            args += [a, b]
        for k, offset in enumerate(self.added(stage)):
            in_specs.append(
                pl.BlockSpec(
                    (None, rows, columns), lambda i, offset=offset: (i // each, offset * cut + i % each, 0)
                )
            )
            args.append(self.got[k])
        pltpu.emit_pipeline(
            body,
            grid=(2 * each,),
            in_specs=in_specs,
            out_specs=[pl.BlockSpec((None, rows, columns), lambda i: (i // each, i % each, 0))],
        )(*args, self.given[stage])
        pieces = ((0, 2), (2, 1), (3, 1)) if stage == 0 else ((0, 1), (1, 1)) if stage == 1 else ((0, 1),)
        self.sent[stage] = [[], []]
        for at, count in pieces:
            for part in (0, 1):
                axes = (self.spot.mate, self.spot.across) if part == 0 else (self.spot.across, self.spot.mate)
                device = self.spot.twin if stage == 0 else axes[stage - 1]
                there = pl.ds(at * own, count * own)
                copy = self.links.copy(self.given[stage].at[part, there], self.got[stage].at[part, there], device)
                self.sent[stage][part].append(copy.start())

    def wait(self, earlier, part, stage):
        self.sent[earlier][part][stage - earlier - 1].get()

    def last(self, epilogue, ins, outs, cut):
        own, columns = self.own, self.columns
        rows = own // cut
        n_factors = len(self.factors)
        for part in (0, 1):
            for earlier in range(3):
                self.wait(earlier, part, 3)

        def body(*refs):
            mine, rest = refs[: 2 * n_factors], refs[2 * n_factors :]
            total = None
            for k in range(n_factors):
                term = lax.dot_general(mine[2 * k][...], mine[2 * k + 1][...], NT, preferred_element_type=F32)
                total = term if total is None else total + term
            extra = []
            for part in (0, 1):
                terms = [ref[...].astype(F32) for ref in rest[3 * part : 3 * part + 3]]
                extra.append(terms[0] + terms[1] + terms[2])
            total = total + jnp.concatenate(extra, axis=1)
            epilogue(total, rest[6 : 6 + len(ins)], rest[6 + len(ins) :])

        in_specs, args = [], []
        for a, b in self.factors:
            depth = a.shape[1]
            in_specs.append(pl.BlockSpec((rows, depth), lambda i: (self.block(0, 3, False) * cut + i, 0)))
            in_specs.append(pl.BlockSpec((2 * columns, depth), lambda i: (0, 0)))
            args += [a, b]
        for part in (0, 1):
            for k, offset in enumerate(self.added(3)):
                in_specs.append(
                    pl.BlockSpec(
                        (None, rows, columns), lambda i, part=part, offset=offset: (part, offset * cut + i, 0)
                    )
                )
                args.append(self.got[k])

        def spec(ref):
            if ref.shape[0] == 1:
                return pl.BlockSpec(ref.shape, lambda i: (0, 0))
            return pl.BlockSpec((rows, ref.shape[1]), lambda i: (i, 0))

        pltpu.emit_pipeline(
            body, grid=(cut,), in_specs=in_specs + [spec(r) for r in ins], out_specs=[spec(r) for r in outs]
        )(*args, *ins, *outs)


def output_rows(total, ins, outs):
    x_ref, bias_ref = ins
    outs[0][...] = (x_ref[...].astype(F32) + total + bias_ref[...]).astype(BF)


def norm_rows(sums, total, ins, outs):
    x_ref, g_ref, gain_ref = ins
    x = x_ref[...].astype(F32)
    gy = g_ref[...].astype(F32)
    centred = x - jnp.mean(x, axis=1, keepdims=True)
    rstd = lax.rsqrt(jnp.mean(centred * centred, axis=1, keepdims=True) + EPS)
    x_hat = centred * rstd
    scaled = total * gain_ref[...]
    m1 = jnp.mean(scaled, axis=1, keepdims=True)
    m2 = jnp.mean(scaled * x_hat, axis=1, keepdims=True)
    outs[0][...] = rstd * (scaled - m1 - x_hat * m2) + gy
    sums[0:1, :] += jnp.sum(total * x_hat, axis=0, keepdims=True)
    sums[1:2, :] += jnp.sum(total, axis=0, keepdims=True)
    sums[2:3, :] += jnp.sum(gy, axis=0, keepdims=True)


SUMMED = 8


def layer_kernel(ndp, nt, count, *refs):
    refs = list(refs)
    take = lambda n: [refs.pop(0) for _ in range(n)]
    x_own, g_own, gain, shift, lens_own, inverse, wq_own, w1_own, wd_own, w2_own, bias_q, bias_1, bias_out = take(13)
    output, grad_x, small = take(3)
    g_w2, g_wd, g_wq, g_w1 = take(4)
    weights = [take(6) for _ in range(3)]
    row_buffers = [take(6) for _ in range(2)]
    h, gb, wq, w1, wd, w2, qkv, o_float, o, lse, act, slope, go, da, cosine, sine, aq, ak, gz = take(19)
    dk_s, dv_s, dqt_s, lens, acc, sums, biases, line_got, pair_got, local_sem, send, recv = take(12)
    spot = Spot(ndp, nt)
    links = Links(send, recv)
    group = h.shape[0] // 2
    own = x_own.shape[0]
    half, other = spot.half, 1 - spot.half
    greet(spot.partners())

    lens_given = links.copy(lens_own, lens, spot.mate)
    gather_q = GatherWeight(links, spot, wq_own, wq, local_sem.at[0])
    gather_1 = GatherWeight(links, spot, w1_own, w1, local_sem.at[1])
    gather_d = GatherWeight(links, spot, wd_own, wd, local_sem.at[2])
    gather_2 = GatherWeight(links, spot, w2_own, w2, local_sem.at[3])
    rows_h = GatherRows(links, spot, h, own)
    rows_gb = GatherRows(links, spot, gb, own)
    reduce_2, reduce_q, reduce_1 = [
        ReduceWeight(links, spot, parts, slots, end, joined, results, given, theirs)
        for results, (theirs, given, parts, slots, end, joined) in zip(
            (
                [(g_w2, 0, w2.shape[1], True), (g_wd, w2.shape[1], wd.shape[1], True)],
                [(g_wq, 0, wq.shape[1], False)],
                [(g_w1, 0, w1.shape[1], False)],
            ),
            weights,
        )
    ]
    branch = ReduceRows(links, spot, [(act, w2), (o, wd)], row_buffers[0], own)
    grad = ReduceRows(links, spot, [(gz, w1), (da, wq)], row_buffers[1], own)
    tables = [cosine, sine, aq, ak]
    blocks = group // own
    q_columns, f_columns = da.shape[1], act.shape[1]
    attend = functools.partial(attend_kernel, group, min(512, group))
    back = functools.partial(attend_back_kernel, group, min(256, group))

    def attend_back(qkv_ref, aq_ref, ak_ref, cos_ref, sin_ref, o_ref, lse_ref, go_ref, out_ref):
        back(qkv_ref, aq_ref, ak_ref, o_ref, lse_ref, go_ref, cos_ref, sin_ref, out_ref, dk_s, dv_s, dqt_s)

    def project(g):
        by_rows(qkv_body, [h, wq, bias_q, cosine, sine], [qkv], own, g * blocks, blocks)

    def attend_group(g):
        by_heads(attend, [qkv], [], [aq, ak], [o_float, o, lse], group, g)

    def output_grads(g):
        by_rows(plain_body, [gb, wd], [go], own, g * blocks, blocks)

    def attend_back_group(g):
        by_heads(attend_back, [qkv], [o_float, lse, go], [aq, ak, cosine, sine], [da], group, g)

    def outer(left, rights, target, columns, total=None):
        outer_products(left, rights, target.parts, acc.at[:, :, pl.ds(0, columns)], spot, left.shape[0] // 2, total)

    lens_given.start()
    gather_q.first()
    sums[...] = jnp.zeros(sums.shape, F32)
    biases[...] = jnp.zeros(biases.shape, F32)
    norm_inputs(spot, x_own, g_own, gain, shift, lens_own, h, gb, 2)
    rows_h.first()
    gather_q.second()
    gather_d.first()
    gather_1.first()
    lens_given.get()
    make_tables(spot, (lens_own, lens), count, inverse, cosine, sine, aq, ak, own)
    gather_q.third()
    rows_h.second()
    rows_gb.first()
    gather_q.finish()
    gather_d.second()
    gather_1.second()
    rows_h.finish_near()
    project(half)
    rows_h.third()
    gather_2.first()
    attend_group(half)
    gather_d.third()
    rows_h.finish()
    project(other)
    attend_group(other)
    rows_gb.second()
    gather_d.finish()
    rows_gb.finish_near()
    output_grads(half)
    gather_1.third()
    gather_2.second()
    attend_back_group(half)
    rows_gb.third()
    gather_1.finish()
    by_rows(gelu_body, [h, w1, bias_1], [act, slope], own)
    rows_gb.finish()
    output_grads(other)
    gather_2.third()
    outer(gb, [act, o], reduce_2, f_columns + o.shape[1])
    reduce_2.first()
    gather_2.finish()
    branch.run(0, 1)
    reduce_2.second()
    attend_back_group(other)
    reduce_2.third()
    branch.run(1, 1)
    outer(h, [da], reduce_q, q_columns, biases.at[1:2, pl.ds(0, q_columns)])
    reduce_q.first()
    by_rows(slope_body, [gb, w2, slope], [gz], own)
    reduce_q.second()
    grad.run(0, 1)
    reduce_q.third()
    branch.run(2, 1)
    grad.run(1, 1)
    outer(h, [gz], reduce_1, f_columns, biases.at[0:1, pl.ds(0, f_columns)])
    reduce_1.first()
    reduce_2.fourth()
    reduce_1.second()
    branch.last(output_rows, [x_own, bias_out], [output], 2)
    grad.run(2, 1)
    reduce_2.finish()
    reduce_q.fourth()
    reduce_1.third()
    norm = functools.partial(norm_rows, sums)
    grad.last(norm, [x_own, gb.at[pl.ds(pl.multiple_of(spot.block(0, 0, 0) * own, own), own)], gain], [grad_x], 2)

    sums[SUMMED // 2 : SUMMED // 2 + 2, :] = biases[...]
    places = spot.places
    line_got[0] = sums[...]
    got = [links.copy(sums, line_got.at[j], spot.along((spot.at + j) % places)).start() for j in range(1, places)]
    reduce_q.finish()
    reduce_1.fourth()
    for sent in got:
        sent.get()
    for sent in got:
        sent.drain()
    total = line_got[spot.at]
    for place in range(1, places):
        total = total + line_got[(spot.at + places - place) % places]
    sums[...] = total
    row = lax.broadcasted_iota(jnp.int32, sums.shape, 0)
    for k, device in enumerate((spot.mate, spot.across, spot.twin)):
        sent = links.copy(sums, pair_got.at[k], device).start()
        sent.get()
        sent.drain()
        theirs = pair_got[k]
        if k == 0:
            small[1] = theirs
        sums[...] = sums[...] + jnp.where(row < SUMMED // 2, theirs, 0.0)
    small[0] = sums[...]
    reduce_1.finish()
    links.finish()


def layer_call(ndp, nt, count, x_own, g_own, gain, shift, lens, inverse, weights, biases):
    own, width = x_own.shape
    group = nt * own
    rows = 2 * group
    places = ndp // 2
    size, shard = width // places, width // ndp
    q3, f, q = [weights[k].shape[1] // 2 for k in (0, 1, 2)]
    shape = lambda *s: jax.ShapeDtypeStruct(s, BF)
    full = lambda *s: jax.ShapeDtypeStruct(s, F32)
    out_shape = [shape(own, width), full(own, width), full(2, SUMMED, width)]
    out_shape += [full(2 * f, shard), full(2 * q, shard), full(shard, 2 * q3), full(shard, 2 * f)]
    for n in (f + q, q3, f):
        out_shape += [shape(shard, n), shape(shard, n)]
        out_shape += [shape(places, size, n), shape(places - 1, size, n), shape(size, n), shape(size, n)]
    for _ in range(2):
        out_shape += [shape(2, k * own, width // 2) for k in (4, 2, 1)] * 2
    out_shape += [shape(rows, width), shape(rows, width)]
    out_shape += [shape(width, n) for n in (q3, f, q, f)]
    out_shape += [shape(rows, q3), full(rows, q), shape(rows, q), full(rows, q)]
    out_shape += [shape(rows, f), shape(rows, f), shape(rows, q), shape(rows, q3)]
    out_shape += [full(rows, LANES), full(rows, LANES), shape(rows, LANES), shape(rows, LANES), shape(rows, f)]
    anywhere = pl.BlockSpec(memory_space=pl.ANY)
    in_specs = [anywhere] * 13
    in_specs[4] = pl.BlockSpec(memory_space=pltpu.VMEM)
    out_specs = [anywhere] * len(out_shape)
    out_specs[2] = pl.BlockSpec(memory_space=pltpu.VMEM)
    transfers = 1 + 2 * 9 + 4 * (1 + max(4, places)) + 3 * (1 + max(6, places)) + 2 * 2 * 6 + places + 3
    return pl.pallas_call(
        functools.partial(layer_kernel, ndp, nt, count),
        in_specs=in_specs,
        out_specs=out_specs,
        out_shape=out_shape,
        scratch_shapes=[
            pltpu.VMEM((group, LANES), F32),
            pltpu.VMEM((group, LANES), F32),
            pltpu.VMEM((LANES, group), F32),
            pltpu.VMEM(lens.shape, F32),
            pltpu.VMEM((places, size, f + q), F32),
            pltpu.VMEM((SUMMED, width), F32),
            pltpu.VMEM((2, width), F32),
            pltpu.VMEM((places, SUMMED, width), F32),
            pltpu.VMEM((3, SUMMED, width), F32),
            pltpu.SemaphoreType.DMA((4,)),
            pltpu.SemaphoreType.DMA((transfers,)),
            pltpu.SemaphoreType.DMA((transfers,)),
        ],
        compiler_params=pltpu.CompilerParams(collective_id=0, has_side_effects=True, vmem_limit_bytes=VMEM),
    )(x_own, g_own, gain, shift, lens, inverse, *weights, *biases)


def local(
    layer_input,
    seq_lens,
    ln_gain,
    ln_bias,
    w_qkv,
    b_qkv,
    w_dense,
    b_dense,
    w_fc1,
    b_fc1,
    w_fc2,
    b_fc2,
    cotangent,
):
    own, width = layer_input.shape
    ndp, nt = lax.axis_size("dp"), lax.axis_size("tensor")
    dp, t = lax.axis_index("dp"), lax.axis_index("tensor")
    half, at, places = dp % 2, dp // 2, ndp // 2
    chip, core = t // 2, t % 2
    group = own * nt
    shard = w_qkv.shape[0]
    q_width = w_qkv.shape[2] // 2
    f_width = w_fc1.shape[1] // 2
    pairs = q_width // LANES
    other = 1 - half

    wq = w_qkv.reshape(shard, 3, 2, pairs, LANES).transpose(0, 2, 3, 1, 4).reshape(shard, 6 * q_width)
    bias_q = pick(b_qkv.reshape(3, 2, pairs, LANES).transpose(1, 2, 0, 3), half).reshape(1, 3 * q_width)
    bias_1 = pick(b_fc1.reshape(2, f_width), half)[None]
    count = seq_lens.shape[1]
    lens = jnp.zeros((8, LANES), F32).at[0, :count].set(seq_lens[0].astype(F32))
    steps = jnp.arange(ROT // 2, dtype=F32)
    inverse = jnp.exp(-math.log(10000.0) * 2.0 * steps / ROT)
    inverse = jnp.concatenate([inverse, inverse, jnp.zeros((HEAD - ROT,), F32)] * 2)[None]

    made = layer_call(
        ndp, nt, count, layer_input, cotangent, ln_gain[None], ln_bias[None], lens, inverse,
        [wq, w_fc1, w_dense.T, w_fc2.T], [bias_q, bias_1, (b_dense + b_fc2)[None]],
    )
    output, grad_x, small = made[:3]

    def both(mine, theirs):
        return jnp.stack([jnp.where(half == 0, mine, theirs), jnp.where(half == 0, theirs, mine)])

    out_w2, out_wd, g_wq, g_w1 = made[3:7]
    late, early = small[0, :2], small[0, 2]
    g_biases = both(small[0, SUMMED // 2 : SUMMED // 2 + 2], small[1, SUMMED // 2 : SUMMED // 2 + 2])
    g_b1 = g_biases[:, 0, :f_width].reshape(-1)
    g_bq = g_biases[:, 1, : 3 * q_width].reshape(2, pairs, 3, LANES).transpose(2, 0, 1, 3).reshape(3, 2 * q_width)
    out_wq = g_wq.reshape(shard, 2, pairs, 3, LANES).transpose(0, 3, 1, 2, 4).reshape(shard, 3, 2 * q_width)
    return (
        output,
        grad_x,
        late[0],
        late[1],
        out_wq,
        g_bq,
        out_wd,
        early,
        g_w1,
        g_b1,
        out_w2,
        early,
    )


def solution(mesh):
    rows = P(("dp", "tensor"), None)
    in_specs = (
        rows,
        P("dp", None),
        P(),
        P(),
        P("dp", None, "tensor"),
        P(None, "tensor"),
        P("tensor", "dp"),
        P(),
        P("dp", "tensor"),
        P("tensor"),
        P("tensor", "dp"),
        P(),
        rows,
    )
    out_specs = (
        rows,
        rows,
        P(),
        P(),
        P("dp", None, "tensor"),
        P(None, "tensor"),
        P("tensor", "dp"),
        P(),
        P("dp", "tensor"),
        P("tensor"),
        P("tensor", "dp"),
        P(),
    )
    return jax.shard_map(local, mesh=mesh, in_specs=in_specs, out_specs=out_specs, check_vma=False)
```

```python
import functools
import math

import jax
import jax.numpy as jnp
from jax import lax
from jax.experimental import pallas as pl
from jax.experimental.pallas import tpu as pltpu
from jax.sharding import PartitionSpec as P

HEAD = 64
ROT = 32
EPS = 1e-05
NEG = -1e30
LANES = 128
BF = jnp.bfloat16
F32 = jnp.float32
NT = (((1,), (1,)), ((), ()))
TN = (((0,), (0,)), ((), ()))
VMEM = 56 * 2**20
COST = pl.CostEstimate(flops=0, bytes_accessed=0, transcendentals=0)


def pick(x, index):
    return lax.dynamic_index_in_dim(x, index, 0, keepdims=False)


def place(buffer, block, *index):
    return lax.dynamic_update_slice(
        buffer, block.reshape((1,) * len(index) + block.shape), tuple(index) + (0,) * block.ndim
    )


def lanes_of(shape):
    return lax.broadcasted_iota(jnp.int32, shape, 1)


def turn(x, cosine, sine):
    lane = lanes_of(x.shape) % HEAD
    other = jnp.where(lane < ROT // 2, pltpu.roll(x, LANES - ROT // 2, 1), pltpu.roll(x, ROT // 2, 1))
    return x * cosine + other * sine


def qkv_rows(acc, extras, outs):
    bias, cosine, sine = (ref[...] for ref in extras)
    acc = acc + bias
    out_ref = outs[0]
    for at in range(0, acc.shape[1], 3 * LANES):
        q = turn(acc[:, at : at + LANES], cosine, sine).astype(BF)
        out_ref[:, at : at + LANES] = (q.astype(F32) * HEAD**-0.5).astype(BF)
        k = turn(acc[:, at + LANES : at + 2 * LANES], cosine, sine)
        out_ref[:, at + LANES : at + 2 * LANES] = k.astype(BF)
        out_ref[:, at + 2 * LANES : at + 3 * LANES] = acc[:, at + 2 * LANES : at + 3 * LANES].astype(BF)


def plain_rows(acc, extras, outs):
    outs[0][...] = acc.astype(BF)


def gelu_rows(acc, extras, outs):
    z = acc + extras[0][...]
    c = math.sqrt(2.0 / math.pi)
    square = z * z
    gate = 0.5 + 0.5 * jnp.tanh(z * (c + (c * 0.044715) * square))
    value = z * gate
    outs[0][...] = value.astype(BF)
    outs[1][...] = (gate + (value - value * gate) * (2.0 * c + (6.0 * 0.044715 * c) * square)).astype(BF)


def slope_rows(acc, extras, outs):
    outs[0][...] = (acc * extras[0][...].astype(F32)).astype(BF)


class Links:
    def __init__(self, send, recv):
        self.send, self.recv, self.count, self.pending = send, recv, 0, []

    def copy(self, src, dst, device, sends=None, gets=None):
        n = self.count
        self.count += 1
        made = pltpu.make_async_remote_copy(
            src_ref=src,
            dst_ref=dst,
            send_sem=self.send.at[n],
            recv_sem=self.recv.at[n],
            device_id=device,
            device_id_type=pl.DeviceIdType.MESH,
        )
        return Sent(self, made, sends, gets)

    def finish(self):
        for sent in self.pending:
            sent.when(sent.sends, sent.made.wait_send)


class Sent:
    def __init__(self, links, made, sends, gets):
        self.links, self.made, self.sends, self.gets = links, made, sends, gets

    def when(self, condition, action):
        if condition is None:
            action()
        else:
            pl.when(condition)(action)

    def start(self):
        self.when(self.sends, self.made.start)
        self.links.pending.append(self)
        return self

    def get(self):
        self.when(self.gets, self.made.wait_recv)

    def drain(self):
        self.links.pending.remove(self)
        self.when(self.sends, self.made.wait_send)


def greet(devices):
    barrier = pltpu.get_barrier_semaphore()
    for device in devices:
        pl.semaphore_signal(barrier, inc=1, device_id=device, device_id_type=pl.DeviceIdType.MESH)
    pl.semaphore_wait(barrier, len(devices))


class Spot:
    def __init__(self, ndp, nt):
        self.dp, self.t = lax.axis_index("dp"), lax.axis_index("tensor")
        self.half, self.at = self.dp % 2, self.dp // 2
        self.chip, self.core = self.t // 2, self.t % 2
        self.places, self.nt = ndp // 2, nt
        self.mate = (self.dp + 1 - 2 * self.half, self.t)
        self.across = (self.dp, self.t + 2 - 4 * self.chip)
        self.twin = (self.dp, self.t + 1 - 2 * self.core)

    def along(self, place):
        return (2 * place + self.half, self.t)

    def partners(self):
        line = [self.along((self.at + j) % self.places) for j in range(1, self.places)]
        return [self.mate, self.across, self.twin] + line

    def block(self, mates, acrosses, twins):
        g = self.half if not mates else 1 - self.half
        x = self.chip if not acrosses else 1 - self.chip
        c = self.core if not twins else 1 - self.core
        return g * self.nt + 2 * x + c


class GatherRows:
    def __init__(self, links, spot, whole, size):
        self.whole, self.size = whole, size
        low = size // 4
        near, across, mate, far = [spot.block(g, x, 0) for g, x in ((0, 0), (0, 1), (1, 0), (1, 1))]
        made = lambda block, device, first=0, count=size: links.copy(
            self.rows(block, first, count), self.rows(block, first, count), device
        )
        self.x, self.y = made(near, spot.across), made(near, spot.mate)
        self.low = made(across, spot.mate, 0, low)
        self.high = made(mate, spot.across, low, size - low)
        self.near_twin, self.x_twin, self.y_twin = [made(n, spot.twin) for n in (near, across, mate)]
        self.low_twin = made(far, spot.twin, 0, low)
        self.high_twin = made(far, spot.twin, low, size - low)

    def rows(self, block, first, count):
        return self.whole.at[pl.ds(pl.multiple_of(block * self.size, self.size) + first, count)]

    def first(self):
        self.x.start()
        self.y.start()
        self.near_twin.start()

    def second(self):
        self.x.get()
        self.low.start()
        self.x_twin.start()
        self.y.get()
        self.high.start()
        self.y_twin.start()

    def third(self):
        self.low.get()
        self.low_twin.start()
        self.high.get()
        self.high_twin.start()

    def finish_near(self):
        self.near_twin.get()
        self.x_twin.get()

    def finish(self):
        for part in (self.y_twin, self.low_twin, self.high_twin):
            part.get()


class GatherWeight:
    def __init__(self, links, spot, own, whole, sem):
        self.spot, self.whole = spot, whole
        self.shard, columns = own.shape[0], whole.shape[1]
        at, places = spot.at, spot.places
        half = lambda k: own.at[:, pl.ds(pl.multiple_of(k * columns, columns), columns)]
        place = whole.at[pl.ds(pl.multiple_of((2 * at + spot.half) * self.shard, self.shard), self.shard)]
        self.local = pltpu.make_async_copy(half(spot.half), place, sem)
        self.y = links.copy(half(1 - spot.half), place, spot.mate)
        made = lambda n, to, sends=None, gets=None: links.copy(
            self.pair(n), self.pair(n), spot.along(to), sends, gets
        )
        if places == 4:
            inner = (at == 1) | (at == 2)
            self.two = made(at, (at + 2) % 4)
            self.parts = [made(at, (at + 1) % 4, at < 3, at > 0), made(at, (at + 3) % 4, at > 0, at < 3)]
            self.three = made((at + 2) % 4, 3 * (at // 2), inner, ~inner)
        else:
            self.parts = [made(at, (at + j) % places) for j in range(1, places)]

    def pair(self, place):
        rows = 2 * self.shard
        return self.whole.at[pl.ds(pl.multiple_of(place * rows, rows), rows)]

    def first(self):
        self.local.start()
        self.y.start()

    def second(self):
        self.local.wait()
        self.y.get()
        if self.spot.places == 4:
            self.two.start()
        for part in self.parts:
            part.start()

    def third(self):
        if self.spot.places == 4:
            self.two.get()
            self.three.start()

    def finish(self):
        for part in self.parts:
            part.get()
        if self.spot.places == 4:
            self.three.get()


def qkv_body(h_ref, w_ref, b_ref, cos_ref, sin_ref, out_ref):
    acc = jnp.dot(h_ref[...], w_ref[...], preferred_element_type=F32) + b_ref[...]
    cosine, sine = cos_ref[...], sin_ref[...]
    for at in range(0, acc.shape[1], 3 * LANES):
        q = turn(acc[:, at : at + LANES], cosine, sine).astype(BF)
        out_ref[:, at : at + LANES] = (q.astype(F32) * HEAD**-0.5).astype(BF)
        k = turn(acc[:, at + LANES : at + 2 * LANES], cosine, sine)
        out_ref[:, at + LANES : at + 2 * LANES] = k.astype(BF)
        out_ref[:, at + 2 * LANES : at + 3 * LANES] = acc[:, at + 2 * LANES : at + 3 * LANES].astype(BF)


def gelu_body(h_ref, w_ref, b_ref, act_ref, slope_ref):
    z = jnp.dot(h_ref[...], w_ref[...], preferred_element_type=F32) + b_ref[...]
    c = math.sqrt(2.0 / math.pi)
    square = z * z
    gate = 0.5 + 0.5 * jnp.tanh(z * (c + (c * 0.044715) * square))
    value = z * gate
    act_ref[...] = value.astype(BF)
    slope_ref[...] = (gate + (value - value * gate) * (2.0 * c + (6.0 * 0.044715 * c) * square)).astype(BF)


def plain_body(h_ref, w_ref, out_ref):
    out_ref[...] = jnp.dot(h_ref[...], w_ref[...], preferred_element_type=F32).astype(BF)


def slope_body(h_ref, w_ref, slope_ref, out_ref):
    acc = jnp.dot(h_ref[...], w_ref[...], preferred_element_type=F32)
    out_ref[...] = (acc * slope_ref[...].astype(F32)).astype(BF)


def by_rows(body, ins, outs, block, first=0, count=None, events=None):
    total = outs[0].shape[0]
    count = count or total // block

    def spec(ref):
        width = ref.shape[1]
        if ref.shape[0] == total:
            return pl.BlockSpec((block, width), lambda i: (first + i, 0))
        return pl.BlockSpec(ref.shape, lambda i: (0, 0))

    def stepped(step, *refs):
        for k, event in (events or {}).items():
            pl.when(step.index[0] == k)(event)
        body(*refs)

    pltpu.emit_pipeline(
        stepped,
        grid=(count,),
        in_specs=[spec(r) for r in ins],
        out_specs=[spec(r) for r in outs],
        _explicit_indices=True,
    )(*ins, *outs)


def by_heads(body, wide_ins, ins, aug_ins, outs, rows, g):
    pairs = wide_ins[0].shape[1] // (3 * LANES)

    def spec(ref, kind):
        if kind == 2:
            return pl.BlockSpec((rows, LANES), lambda j: (g, 0))
        width = 3 * LANES if ref.shape[1] == pairs * 3 * LANES else LANES
        return pl.BlockSpec((rows, width), lambda j: (g, j))

    specs = [spec(r, 0) for r in wide_ins] + [spec(r, 2) for r in aug_ins] + [spec(r, 0) for r in ins]
    pltpu.emit_pipeline(
        body, grid=(pairs,), in_specs=specs, out_specs=[spec(r, 0) for r in outs]
    )(*wide_ins, *aug_ins, *ins, *outs)


def norm_inputs(spot, x_own, g_own, gain, shift, lens, h, gb, cut):
    own = x_own.shape[0]
    rows = own // cut

    def body(step, x_ref, g_ref, gain_ref, shift_ref, h_ref, gb_ref):
        x = x_ref[...].astype(F32)
        centred = x - jnp.mean(x, axis=1, keepdims=True)
        rstd = lax.rsqrt(jnp.mean(centred * centred, axis=1, keepdims=True) + EPS)
        h_ref[...] = (centred * rstd * gain_ref[...] + shift_ref[...]).astype(BF)
        used = jnp.sum(lens[0:1, :], axis=1, keepdims=True)
        row = lax.broadcasted_iota(jnp.int32, (rows, 1), 0) + (spot.t * own + step.index[0] * rows)
        gb_ref[...] = jnp.where(row.astype(F32) < used, g_ref[...].astype(F32), 0.0).astype(BF)

    wide = pl.BlockSpec((rows, x_own.shape[1]), lambda i: (i, 0))
    one = pl.BlockSpec(gain.shape, lambda i: (0, 0))
    there = pl.BlockSpec((rows, x_own.shape[1]), lambda i: (spot.block(0, 0, 0) * cut + i, 0))
    pltpu.emit_pipeline(
        body, grid=(cut,), in_specs=[wide, wide, one, one], out_specs=[there, there], _explicit_indices=True
    )(x_own, g_own, gain, shift, h, gb)


def make_tables(spot, lens, count, inverse, cosine, sine, aq, ak, block):
    total = cosine.shape[0]
    steps = total // 2 // block

    def body(step, inverse_ref, cos_ref, sin_ref, aq_ref, ak_ref):
        i = step.index[0]
        length = jnp.where(i // steps == spot.half, lens[0][0:1, :], lens[1][0:1, :])
        shape = (block, LANES)
        row = (lax.broadcasted_iota(jnp.int32, shape, 0) + (i % steps) * block).astype(F32)
        lane = lanes_of(shape) % HEAD
        segment, position, end = jnp.zeros(shape, F32), row, 0.0
        for j in range(count):
            end = end + length[:, j : j + 1]
            passed = row >= end
            segment = segment + jnp.where(passed, 1.0, 0.0)
            position = position - jnp.where(passed, length[:, j : j + 1], 0.0)
        angle = position * inverse_ref[...]
        sign = jnp.where(lane < ROT // 2, -1.0, 1.0)
        cos_ref[...] = jnp.cos(angle)
        sin_ref[...] = jnp.sin(angle) * sign
        same = segment == lane.astype(F32)
        aq_ref[...] = jnp.where(same & (lane <= count), NEG, 0.0).astype(BF)
        other = (lane <= count) & ~same
        ak_ref[...] = jnp.where(other | ((lane >= 8) & (lane < 11)), 1.0, 0.0).astype(BF)

    spec = pl.BlockSpec((block, LANES), lambda i: (i, 0))
    pltpu.emit_pipeline(
        body,
        grid=(2 * steps,),
        in_specs=[pl.BlockSpec((1, LANES), lambda i: (0, 0))],
        out_specs=[spec] * 4,
        _explicit_indices=True,
    )(inverse, cosine, sine, aq, ak)


def attend_kernel(rows, block, qkv_ref, aq_ref, ak_ref, *refs):
    o_ref, bf_ref, lse_ref = refs[-3:]
    lane = lanes_of((rows, LANES))
    lane_q = lanes_of((block, LANES))
    one = jnp.where(lane % HEAD < 3, 1.0, 0.0).astype(BF)
    first = lane < HEAD
    keys = [jnp.where(half, qkv_ref[:, LANES : 2 * LANES], ak_ref[...]) for half in (first, ~first)]
    values = [jnp.where(half, qkv_ref[:, 2 * LANES :], one) for half in (first, ~first)]
    causal = lanes_of((block, block)) <= lax.broadcasted_iota(jnp.int32, (block, block), 0)
    for b in range(rows // block):
        here = pl.ds(b * block, block)
        lo, hi = b * block, (b + 1) * block
        outs, sums = [], []
        for side in (0, 1):
            half = (lane_q < HEAD) if side == 0 else (lane_q >= HEAD)
            q = jnp.where(half, qkv_ref[here, :LANES], aq_ref[here])
            s_near = lax.dot_general(q, keys[side][lo:hi], NT, preferred_element_type=F32)
            s_near = jnp.where(causal, s_near, NEG)
            top = jnp.max(s_near, axis=1, keepdims=True)
            if b:
                s_far = lax.dot_general(q, keys[side][:lo], NT, preferred_element_type=F32)
                top = jnp.maximum(top, jnp.max(s_far, axis=1, keepdims=True))
            o = jnp.dot(jnp.exp(s_near - top).astype(BF), values[side][lo:hi], preferred_element_type=F32)
            if b:
                o = o + jnp.dot(
                    jnp.exp(s_far - top).astype(BF), values[side][:lo], preferred_element_type=F32
                )
            at = HEAD if side == 0 else 0
            total = o[:, at : at + 1]
            outs.append(o / total)
            sums.append(top + jnp.log(total))
        out = jnp.where(lane_q < HEAD, outs[0], outs[1])
        o_ref[here] = out
        bf_ref[here] = out.astype(BF)
        lse_ref[here] = jnp.where(lane_q < HEAD, sums[0], sums[1])


def split3(x):
    a = x.astype(BF).astype(F32)
    b = (x - a).astype(BF).astype(F32)
    return a, b, x - a - b


def attend_back_kernel(
    rows, block, qkv_ref, aq_ref, ak_ref, o_ref, lse_ref, go_ref, cos_ref, sin_ref, *refs
):
    out_ref, dk_s, dv_s, dqt_s = refs
    lane = lanes_of((rows, LANES))
    lane_k = lanes_of((block, LANES))
    one = jnp.where(lane % HEAD < 3, 1.0, 0.0).astype(BF)
    causal = lax.broadcasted_iota(jnp.int32, (block, block), 0) <= lanes_of((block, block))
    prod = o_ref[...] * go_ref[...].astype(F32)
    dq_first = None
    for side in (0, 1):
        half = (lane < HEAD) if side == 0 else (lane >= HEAD)
        delta = -jnp.sum(jnp.where(half, prod, 0.0), axis=1, keepdims=True)
        at = 0 if side == 0 else HEAD
        lse = -lse_ref[:, at : at + 1]
        q = jnp.where(half, qkv_ref[:, :LANES], aq_ref[...]).astype(F32)
        g = jnp.where(half, go_ref[...].astype(F32), 0.0)
        base = HEAD - at
        for i, (a, d) in enumerate(zip(split3(lse), split3(delta))):
            q = jnp.where(lane == base + 8 + i, a, q)
            g = jnp.where(lane == base + i, d, g)
        q, g = q.astype(BF), g.astype(BF)
        k = jnp.where(half, qkv_ref[:, LANES : 2 * LANES], ak_ref[...])
        v = jnp.where(half, qkv_ref[:, 2 * LANES :], one)
        kt = k.T
        for b in range(rows // block):
            lo, hi = b * block, (b + 1) * block
            here = pl.ds(lo, block)
            st = lax.dot_general(k[lo:hi], q[lo:], NT, preferred_element_type=F32)
            dpt = lax.dot_general(v[lo:hi], g[lo:], NT, preferred_element_type=F32)
            p = jnp.exp(st)
            near = jnp.where(causal, p[:, :block], 0.0)
            p = jnp.concatenate([near, p[:, block:]], axis=1) if hi < rows else near
            ds = (p * dpt).astype(BF)
            dv = jnp.dot(p.astype(BF), g[lo:], preferred_element_type=F32)
            dk = jnp.dot(ds, q[lo:], preferred_element_type=F32)
            dq = jnp.dot(kt[:, lo:hi], ds, preferred_element_type=F32)
            if side == 0:
                dk_s[here] = dk
                dv_s[here] = dv
            else:
                dk = jnp.where(lane_k < HEAD, dk_s[here], dk)
                dv = jnp.where(lane_k < HEAD, dv_s[here], dv)
                out_ref[here, LANES : 2 * LANES] = turn(dk, cos_ref[here], -sin_ref[here]).astype(BF)
                out_ref[here, 2 * LANES :] = dv.astype(BF)
            if b == 0:
                dqt_s[...] = dq
            else:
                dqt_s[:, lo:] += dq
        d = dqt_s[...].T * HEAD**-0.5
        if side == 0:
            dq_first = d
        else:
            d = jnp.where(lane < HEAD, dq_first, d)
            out_ref[:, :LANES] = turn(d, cos_ref[...], -sin_ref[...]).astype(BF)


def outer_products(left, rights, parts, spot, sums=None):
    places = spot.places
    rows, size = left.shape[0], left.shape[1] // places
    columns = parts.shape[2]

    def body(step, left_ref, *refs):
        right_refs, out = refs[:-1], refs[-1]
        turned = left_ref[...].T
        first = 0
        for right_ref in right_refs:
            there = slice(first, first + right_ref.shape[1])
            first += right_ref.shape[1]
            out[:, there] = jnp.dot(turned, right_ref[...], preferred_element_type=F32).astype(BF)

            if sums is not None:
                @pl.when(step.index[0] == 0)
                def _():
                    sums[...] += jnp.sum(right_ref[...].astype(F32), axis=0, keepdims=True)

    pltpu.emit_pipeline(
        body,
        grid=(places,),
        in_specs=[pl.BlockSpec((rows, size), lambda j: (0, lax.rem(spot.at + j, places)))]
        + [pl.BlockSpec((rows, x.shape[1]), lambda j: (0, 0)) for x in rights],
        out_specs=[pl.BlockSpec((None, size, columns), lambda j: (j, 0, 0))],
        _explicit_indices=True,
    )(left, *rights, parts)


def turn_weight(source, turned, block):
    def body(a, out):
        out[...] = a[...].T

    pltpu.emit_pipeline(
        body,
        grid=(source.shape[0] // block,),
        in_specs=[pl.BlockSpec((block, source.shape[1]), lambda i: (i, 0))],
        out_specs=[pl.BlockSpec((source.shape[1], block), lambda i: (0, i))],
    )(source, turned)


class ReduceWeight:
    def __init__(self, links, spot, parts, slots, end, joined, results, given, theirs):
        self.links, self.spot = links, spot
        self.parts, self.slots, self.end, self.joined = parts, slots, end, joined
        self.results, self.given, self.theirs = results, given, theirs
        self.shard = given.shape[0]

    def send(self, src, dst, to, sends=None, gets=None):
        return self.links.copy(src, dst, self.spot.along(to), sends, gets).start()

    def first(self):
        at = self.spot.at
        if self.spot.places == 4:
            self.edges = [
                self.send(self.parts.at[3], self.end, 1, at == 0, at == 1),
                self.send(self.parts.at[1], self.end, 2, at == 3, at == 2),
            ]

    def second(self):
        at, places, parts, slots = self.spot.at, self.spot.places, self.parts, self.slots
        if places == 4:
            inner = (at == 1) | (at == 2)
            self.got = [
                self.send(parts.at[1], slots.at[0], (at + 1) % 4, at < 3, at > 0),
                self.send(parts.at[3], slots.at[1], (at + 3) % 4, at > 0, at < 3),
                self.send(parts.at[2], slots.at[2], (at + 2) % 4, ~inner, inner),
            ]
        else:
            self.got = [self.send(parts.at[j], slots.at[j - 1], (at + j) % places) for j in range(1, places)]

    def third(self):
        if self.spot.places != 4:
            return
        at = self.spot.at
        inner = (at == 1) | (at == 2)
        for edge in self.edges:
            edge.get()
        size, columns = self.parts.shape[1:]

        def body(a, b, out):
            out[...] = (a[...].astype(F32) + b[...].astype(F32)).astype(BF)

        @pl.when(inner)
        def _():
            spec = pl.BlockSpec((self.shard, columns), lambda i: (i, 0))
            pltpu.emit_pipeline(
                body,
                grid=(size // self.shard,),
                in_specs=[pl.BlockSpec((None, self.shard, columns), lambda i: (2, i, 0)), spec],
                out_specs=[spec],
            )(self.parts, self.end, self.joined)

        self.got.append(self.send(self.joined, self.slots.at[2], (at + 2) % 4, inner, ~inner))

    def fourth(self):
        spot = self.spot
        at, places = spot.at, spot.places
        for sent in self.got:
            sent.get()
        columns = self.parts.shape[2]

        def body(given, own, *refs):
            total = own[...].astype(F32)
            for k, ref in enumerate(refs[: places - 1]):
                term = ref[...].astype(F32)
                if places == 4 and k < 2:
                    term = term * jnp.where(at > 0 if k == 0 else at < 3, 1.0, 0.0)
                total = total + term
            if given:
                refs[-1][...] = total.astype(BF)
            else:
                self.store(total, refs[places - 1 :])

        def slot(k, part):
            if places == 4 and k < 2:
                k = jnp.where(at > 0, 0, 2) if k == 0 else jnp.where(at < 3, 1, 2)
            return pl.BlockSpec((None, self.shard, columns), lambda i: (k, part, 0))

        for part in (1 - spot.half, spot.half):
            own = pl.BlockSpec((None, self.shard, columns), lambda i, part=part: (0, part, 0))
            given = part is not spot.half
            specs, outs = self.whole_given() if given else self.own_columns(spot.half)
            pltpu.emit_pipeline(
                functools.partial(body, given),
                grid=(1,),
                in_specs=[own] + [slot(k, part) for k in range(places - 1)],
                out_specs=specs,
            )(self.parts, *[self.slots] * (places - 1), *outs)
            if given:
                self.mate = self.links.copy(self.given, self.theirs, spot.mate).start()

    def whole_given(self):
        return [pl.BlockSpec(self.given.shape, lambda i: (0, 0))], [self.given]

    def own_columns(self, half):
        specs = []
        for ref, first, width, turned in self.results:
            if turned:
                specs.append(pl.BlockSpec((width, self.shard), lambda i: (half, 0)))
            else:
                specs.append(pl.BlockSpec((self.shard, width), lambda i: (0, half)))
        return specs, [result[0] for result in self.results]

    def store(self, total, outs):
        for out, (_, first, width, turned) in zip(outs, self.results):
            mine = total[:, first : first + width]
            out[...] = mine.T if turned else mine

    def finish(self):
        self.mate.get()

        def body(theirs, *outs):
            self.store(theirs[...].astype(F32), outs)

        specs, outs = self.own_columns(1 - self.spot.half)
        pltpu.emit_pipeline(body, grid=(1,), in_specs=self.whole_given()[0], out_specs=specs)(self.theirs, *outs)


class ReduceRows:
    def __init__(self, links, spot, factors, buffers, own):
        self.links, self.spot, self.factors, self.own = links, spot, factors, own
        self.given, self.got = buffers[:3], buffers[3:]
        self.columns = factors[0][1].shape[0] // 2
        self.sent = [[None, None] for _ in range(3)]

    def block(self, part, n, twins):
        spot = self.spot
        g_own = (1 - part) * (n // 2) + part * (n % 2)
        x_own = (1 - part) * (n % 2) + part * (n // 2)
        other, x1 = 1 - spot.half, 1 - spot.chip
        g = other + g_own * (spot.half - other)
        x = x1 + x_own * (spot.chip - x1)
        c = 1 - spot.core if twins else spot.core
        return g * spot.nt + 2 * x + c

    def added(self, stage):
        return [((), (0,), (2, 0), (3, 1, 0))[stage][k] for k in range(stage)]

    def run(self, stage, cut):
        first, last = ((0, 4), (0, 2), (2, 3))[stage]
        own, columns = self.own, self.columns
        rows = own // cut
        each = (last - first) * cut
        n_factors = len(self.factors)
        for part in (0, 1):
            for earlier in range(stage):
                self.wait(earlier, part, stage)

        def body(*refs):
            ins, out = refs[:-1], refs[-1]
            total = None
            for k in range(n_factors):
                term = lax.dot_general(ins[2 * k][...], ins[2 * k + 1][...], NT, preferred_element_type=F32)
                total = term if total is None else total + term
            for ref in ins[2 * n_factors :]:
                total = total + ref[...].astype(F32)
            out[...] = total.astype(BF)

        def row_block(i):
            part, k = i // each, i % each
            return self.block(part, first + k // cut, stage == 0) * cut + k % cut

        in_specs, args = [], []
        for a, b in self.factors:
            depth = a.shape[1]
            in_specs.append(pl.BlockSpec((rows, depth), lambda i: (row_block(i), 0)))
            in_specs.append(pl.BlockSpec((columns, depth), lambda i: (i // each, 0)))
            args += [a, b]
        for k, offset in enumerate(self.added(stage)):
            in_specs.append(
                pl.BlockSpec(
                    (None, rows, columns), lambda i, offset=offset: (i // each, offset * cut + i % each, 0)
                )
            )
            args.append(self.got[k])
        pltpu.emit_pipeline(
            body,
            grid=(2 * each,),
            in_specs=in_specs,
            out_specs=[pl.BlockSpec((None, rows, columns), lambda i: (i // each, i % each, 0))],
        )(*args, self.given[stage])
        pieces = ((0, 2), (2, 1), (3, 1)) if stage == 0 else ((0, 1), (1, 1)) if stage == 1 else ((0, 1),)
        self.sent[stage] = [[], []]
        for at, count in pieces:
            for part in (0, 1):
                axes = (self.spot.mate, self.spot.across) if part == 0 else (self.spot.across, self.spot.mate)
                device = self.spot.twin if stage == 0 else axes[stage - 1]
                there = pl.ds(at * own, count * own)
                copy = self.links.copy(self.given[stage].at[part, there], self.got[stage].at[part, there], device)
                self.sent[stage][part].append(copy.start())

    def wait(self, earlier, part, stage):
        self.sent[earlier][part][stage - earlier - 1].get()

    def last(self, epilogue, ins, outs, cut):
        own, columns = self.own, self.columns
        rows = own // cut
        n_factors = len(self.factors)
        for part in (0, 1):
            for earlier in range(3):
                self.wait(earlier, part, 3)

        def body(*refs):
            mine, rest = refs[: 2 * n_factors], refs[2 * n_factors :]
            total = None
            for k in range(n_factors):
                term = lax.dot_general(mine[2 * k][...], mine[2 * k + 1][...], NT, preferred_element_type=F32)
                total = term if total is None else total + term
            extra = []
            for part in (0, 1):
                terms = [ref[...].astype(F32) for ref in rest[3 * part : 3 * part + 3]]
                extra.append(terms[0] + terms[1] + terms[2])
            total = total + jnp.concatenate(extra, axis=1)
            epilogue(total, rest[6 : 6 + len(ins)], rest[6 + len(ins) :])

        in_specs, args = [], []
        for a, b in self.factors:
            depth = a.shape[1]
            in_specs.append(pl.BlockSpec((rows, depth), lambda i: (self.block(0, 3, False) * cut + i, 0)))
            in_specs.append(pl.BlockSpec((2 * columns, depth), lambda i: (0, 0)))
            args += [a, b]
        for part in (0, 1):
            for k, offset in enumerate(self.added(3)):
                in_specs.append(
                    pl.BlockSpec(
                        (None, rows, columns), lambda i, part=part, offset=offset: (part, offset * cut + i, 0)
                    )
                )
                args.append(self.got[k])

        def spec(ref):
            if ref.shape[0] == 1:
                return pl.BlockSpec(ref.shape, lambda i: (0, 0))
            return pl.BlockSpec((rows, ref.shape[1]), lambda i: (i, 0))

        pltpu.emit_pipeline(
            body, grid=(cut,), in_specs=in_specs + [spec(r) for r in ins], out_specs=[spec(r) for r in outs]
        )(*args, *ins, *outs)


def output_rows(total, ins, outs):
    x_ref, dense_ref, fc2_ref = ins
    outs[0][...] = (x_ref[...].astype(F32) + total + dense_ref[...] + fc2_ref[...]).astype(BF)


def norm_rows(sums, total, ins, outs):
    x_ref, g_ref, gain_ref = ins
    x = x_ref[...].astype(F32)
    gy = g_ref[...].astype(F32)
    centred = x - jnp.mean(x, axis=1, keepdims=True)
    rstd = lax.rsqrt(jnp.mean(centred * centred, axis=1, keepdims=True) + EPS)
    x_hat = centred * rstd
    scaled = total * gain_ref[...]
    m1 = jnp.mean(scaled, axis=1, keepdims=True)
    m2 = jnp.mean(scaled * x_hat, axis=1, keepdims=True)
    outs[0][...] = rstd * (scaled - m1 - x_hat * m2) + gy
    sums[0:1, :] += jnp.sum(total * x_hat, axis=0, keepdims=True)
    sums[1:2, :] += jnp.sum(total, axis=0, keepdims=True)
    sums[2:3, :] += jnp.sum(gy, axis=0, keepdims=True)


SUMMED = 8


def layer_kernel(ndp, nt, count, *refs):
    refs = list(refs)
    take = lambda n: [refs.pop(0) for _ in range(n)]
    x_own, g_own, gain, shift, lens_own, inverse, wq_own, w1_own, wd_raw, w2_raw, bias_q, bias_1, b_dense, b_fc2 = take(14)
    output, grad_x, small = take(3)
    g_w2, g_wd, g_wq, g_w1 = take(4)
    weights = [take(6) for _ in range(3)]
    row_buffers = [take(6) for _ in range(2)]
    h, gb, wq, w1, wd, w2, qkv, o_float, o, lse, act, slope, go, da, cosine, sine, aq, ak, gz, wd_own, w2_own = take(21)
    dk_s, dv_s, dqt_s, lens, sums, biases, line_got, pair_got, local_sem, send, recv = take(11)
    spot = Spot(ndp, nt)
    links = Links(send, recv)
    group = h.shape[0] // 2
    own = x_own.shape[0]
    half, other = spot.half, 1 - spot.half
    greet(spot.partners())

    lens_given = links.copy(lens_own, lens, spot.mate)
    gather_q = GatherWeight(links, spot, wq_own, wq, local_sem.at[0])
    gather_1 = GatherWeight(links, spot, w1_own, w1, local_sem.at[1])
    gather_d = GatherWeight(links, spot, wd_own, wd, local_sem.at[2])
    gather_2 = GatherWeight(links, spot, w2_own, w2, local_sem.at[3])
    rows_h = GatherRows(links, spot, h, own)
    rows_gb = GatherRows(links, spot, gb, own)
    reduce_2, reduce_q, reduce_1 = [
        ReduceWeight(links, spot, parts, slots, end, joined, results, given, theirs)
        for results, (theirs, given, parts, slots, end, joined) in zip(
            (
                [(g_w2, 0, w2.shape[1], True), (g_wd, w2.shape[1], wd.shape[1], True)],
                [(g_wq, 0, wq.shape[1], False)],
                [(g_w1, 0, w1.shape[1], False)],
            ),
            weights,
        )
    ]
    branch = ReduceRows(links, spot, [(act, w2), (o, wd)], row_buffers[0], own)
    grad = ReduceRows(links, spot, [(gz, w1), (da, wq)], row_buffers[1], own)
    tables = [cosine, sine, aq, ak]
    blocks = group // own
    q_columns, f_columns = da.shape[1], act.shape[1]
    attend = functools.partial(attend_kernel, group, min(512, group))
    back = functools.partial(attend_back_kernel, group, min(256, group))

    def attend_back(qkv_ref, aq_ref, ak_ref, cos_ref, sin_ref, o_ref, lse_ref, go_ref, out_ref):
        back(qkv_ref, aq_ref, ak_ref, o_ref, lse_ref, go_ref, cos_ref, sin_ref, out_ref, dk_s, dv_s, dqt_s)

    def project(g):
        by_rows(qkv_body, [h, wq, bias_q, cosine, sine], [qkv], own, g * blocks, blocks)

    def attend_group(g):
        by_heads(attend, [qkv], [], [aq, ak], [o_float, o, lse], group, g)

    def output_grads(g):
        by_rows(plain_body, [gb, wd], [go], own, g * blocks, blocks)

    def attend_back_group(g):
        by_heads(attend_back, [qkv], [o_float, lse, go], [aq, ak, cosine, sine], [da], group, g)

    def outer(left, rights, target, total=None):
        outer_products(left, rights, target.parts, spot, total)

    lens_given.start()
    gather_q.first()
    sums[...] = jnp.zeros(sums.shape, F32)
    biases[...] = jnp.zeros(biases.shape, F32)
    norm_inputs(spot, x_own, g_own, gain, shift, lens_own, h, gb, 2)
    rows_h.first()
    gather_q.second()
    gather_1.first()
    turn_weight(wd_raw, wd_own, own)
    gather_d.first()
    turn_weight(w2_raw, w2_own, own)
    lens_given.get()
    make_tables(spot, (lens_own, lens), count, inverse, cosine, sine, aq, ak, own)
    gather_q.third()
    rows_h.second()
    rows_gb.first()
    gather_q.finish()
    gather_d.second()
    gather_1.second()
    rows_h.finish_near()
    project(half)
    rows_h.third()
    gather_2.first()
    attend_group(half)
    gather_d.third()
    rows_h.finish()
    project(other)
    attend_group(other)
    rows_gb.second()
    gather_d.finish()
    rows_gb.finish_near()
    output_grads(half)
    gather_1.third()
    gather_2.second()
    attend_back_group(half)
    rows_gb.third()
    gather_1.finish()
    by_rows(gelu_body, [h, w1, bias_1], [act, slope], own)
    rows_gb.finish()
    output_grads(other)
    gather_2.third()
    outer(gb, [act, o], reduce_2)
    reduce_2.first()
    gather_2.finish()
    branch.run(0, 1)
    reduce_2.second()
    attend_back_group(other)
    reduce_2.third()
    branch.run(1, 1)
    outer(h, [da], reduce_q, biases.at[1:2, pl.ds(0, q_columns)])
    reduce_q.first()
    by_rows(slope_body, [gb, w2, slope], [gz], own)
    reduce_q.second()
    grad.run(0, 1)
    reduce_q.third()
    branch.run(2, 1)
    grad.run(1, 1)
    outer(h, [gz], reduce_1, biases.at[0:1, pl.ds(0, f_columns)])
    reduce_1.first()
    reduce_2.fourth()
    reduce_1.second()
    branch.last(output_rows, [x_own, b_dense, b_fc2], [output], 2)
    grad.run(2, 1)
    reduce_2.finish()
    reduce_q.fourth()
    reduce_1.third()
    norm = functools.partial(norm_rows, sums)
    grad.last(norm, [x_own, gb.at[pl.ds(pl.multiple_of(spot.block(0, 0, 0) * own, own), own)], gain], [grad_x], 2)

    sums[SUMMED // 2 : SUMMED // 2 + 2, :] = biases[...]
    places = spot.places
    line_got[0] = sums[...]
    got = [links.copy(sums, line_got.at[j], spot.along((spot.at + j) % places)).start() for j in range(1, places)]
    reduce_q.finish()
    reduce_1.fourth()
    for sent in got:
        sent.get()
    for sent in got:
        sent.drain()
    total = line_got[spot.at]
    for place in range(1, places):
        total = total + line_got[(spot.at + places - place) % places]
    sums[...] = total
    row = lax.broadcasted_iota(jnp.int32, sums.shape, 0)
    for k, device in enumerate((spot.mate, spot.across, spot.twin)):
        sent = links.copy(sums, pair_got.at[k], device).start()
        sent.get()
        sent.drain()
        theirs = pair_got[k]
        if k == 0:
            small[1] = theirs
        sums[...] = sums[...] + jnp.where(row < SUMMED // 2, theirs, 0.0)
    small[0] = sums[...]
    reduce_1.finish()
    links.finish()


def layer_call(ndp, nt, count, x_own, g_own, gain, shift, lens, inverse, weights, biases):
    own, width = x_own.shape
    group = nt * own
    rows = 2 * group
    places = ndp // 2
    size, shard = width // places, width // ndp
    q3, f, q = weights[0].shape[1] // 2, weights[1].shape[1] // 2, weights[2].shape[0] // 2
    shape = lambda *s: jax.ShapeDtypeStruct(s, BF)
    full = lambda *s: jax.ShapeDtypeStruct(s, F32)
    out_shape = [shape(own, width), full(own, width), full(2, SUMMED, width)]
    out_shape += [full(2 * f, shard), full(2 * q, shard), full(shard, 2 * q3), full(shard, 2 * f)]
    for n in (f + q, q3, f):
        out_shape += [shape(shard, n), shape(shard, n)]
        out_shape += [shape(places, size, n), shape(places - 1, size, n), shape(size, n), shape(size, n)]
    for _ in range(2):
        out_shape += [shape(2, k * own, width // 2) for k in (4, 2, 1)] * 2
    out_shape += [shape(rows, width), shape(rows, width)]
    out_shape += [shape(width, n) for n in (q3, f, q, f)]
    out_shape += [shape(rows, q3), full(rows, q), shape(rows, q), full(rows, q)]
    out_shape += [shape(rows, f), shape(rows, f), shape(rows, q), shape(rows, q3)]
    out_shape += [full(rows, LANES), full(rows, LANES), shape(rows, LANES), shape(rows, LANES), shape(rows, f)]
    out_shape += [shape(shard, 2 * q), shape(shard, 2 * f)]
    anywhere = pl.BlockSpec(memory_space=pl.ANY)
    in_specs = [anywhere] * 14
    in_specs[4] = pl.BlockSpec(memory_space=pltpu.VMEM)
    out_specs = [anywhere] * len(out_shape)
    out_specs[2] = pl.BlockSpec(memory_space=pltpu.VMEM)
    transfers = 1 + 2 * 9 + 4 * (1 + max(4, places)) + 3 * (1 + max(6, places)) + 2 * 2 * 6 + places + 3
    return pl.pallas_call(
        functools.partial(layer_kernel, ndp, nt, count),
        in_specs=in_specs,
        out_specs=out_specs,
        out_shape=out_shape,
        scratch_shapes=[
            pltpu.VMEM((group, LANES), F32),
            pltpu.VMEM((group, LANES), F32),
            pltpu.VMEM((LANES, group), F32),
            pltpu.VMEM(lens.shape, F32),
            pltpu.VMEM((SUMMED, width), F32),
            pltpu.VMEM((2, width), F32),
            pltpu.VMEM((places, SUMMED, width), F32),
            pltpu.VMEM((3, SUMMED, width), F32),
            pltpu.SemaphoreType.DMA((4,)),
            pltpu.SemaphoreType.DMA((transfers,)),
            pltpu.SemaphoreType.DMA((transfers,)),
        ],
        compiler_params=pltpu.CompilerParams(collective_id=0, has_side_effects=True, vmem_limit_bytes=VMEM),
    )(x_own, g_own, gain, shift, lens, inverse, *weights, *biases)


def local(
    layer_input,
    seq_lens,
    ln_gain,
    ln_bias,
    w_qkv,
    b_qkv,
    w_dense,
    b_dense,
    w_fc1,
    b_fc1,
    w_fc2,
    b_fc2,
    cotangent,
):
    own, width = layer_input.shape
    ndp, nt = lax.axis_size("dp"), lax.axis_size("tensor")
    dp, t = lax.axis_index("dp"), lax.axis_index("tensor")
    half, at, places = dp % 2, dp // 2, ndp // 2
    chip, core = t // 2, t % 2
    group = own * nt
    shard = w_qkv.shape[0]
    q_width = w_qkv.shape[2] // 2
    f_width = w_fc1.shape[1] // 2
    pairs = q_width // LANES
    other = 1 - half

    wq = w_qkv.reshape(shard, 3, 2, pairs, LANES).transpose(0, 2, 3, 1, 4).reshape(shard, 6 * q_width)
    bias_q = pick(b_qkv.reshape(3, 2, pairs, LANES).transpose(1, 2, 0, 3), half).reshape(1, 3 * q_width)
    bias_1 = pick(b_fc1.reshape(2, f_width), half)[None]
    count = seq_lens.shape[1]
    lens = jnp.zeros((8, LANES), F32).at[0, :count].set(seq_lens[0].astype(F32))
    steps = jnp.arange(ROT // 2, dtype=F32)
    inverse = jnp.exp(-math.log(10000.0) * 2.0 * steps / ROT)
    inverse = jnp.concatenate([inverse, inverse, jnp.zeros((HEAD - ROT,), F32)] * 2)[None]

    made = layer_call(
        ndp, nt, count, layer_input, cotangent, ln_gain[None], ln_bias[None], lens, inverse,
        [wq, w_fc1, w_dense, w_fc2], [bias_q, bias_1, b_dense[None], b_fc2[None]],
    )
    output, grad_x, small = made[:3]

    def both(mine, theirs):
        return jnp.stack([jnp.where(half == 0, mine, theirs), jnp.where(half == 0, theirs, mine)])

    out_w2, out_wd, g_wq, g_w1 = made[3:7]
    late, early = small[0, :2], small[0, 2]
    g_biases = both(small[0, SUMMED // 2 : SUMMED // 2 + 2], small[1, SUMMED // 2 : SUMMED // 2 + 2])
    g_b1 = g_biases[:, 0, :f_width].reshape(-1)
    g_bq = g_biases[:, 1, : 3 * q_width].reshape(2, pairs, 3, LANES).transpose(2, 0, 1, 3).reshape(3, 2 * q_width)
    out_wq = g_wq.reshape(shard, 2, pairs, 3, LANES).transpose(0, 3, 1, 2, 4).reshape(shard, 3, 2 * q_width)
    return (
        output,
        grad_x,
        late[0],
        late[1],
        out_wq,
        g_bq,
        out_wd,
        early,
        g_w1,
        g_b1,
        out_w2,
        early,
    )


def solution(mesh):
    rows = P(("dp", "tensor"), None)
    in_specs = (
        rows,
        P("dp", None),
        P(),
        P(),
        P("dp", None, "tensor"),
        P(None, "tensor"),
        P("tensor", "dp"),
        P(),
        P("dp", "tensor"),
        P("tensor"),
        P("tensor", "dp"),
        P(),
        rows,
    )
    out_specs = (
        rows,
        rows,
        P(),
        P(),
        P("dp", None, "tensor"),
        P(None, "tensor"),
        P("tensor", "dp"),
        P(),
        P("dp", "tensor"),
        P("tensor"),
        P("tensor", "dp"),
        P(),
    )
    return jax.shard_map(local, mesh=mesh, in_specs=in_specs, out_specs=out_specs, check_vma=False)
```
